32 devices in a mesh: dom: 32 (over z, y, x, core).
Axes of the slice: x: 2, y: 2, z: 4, core: 2. Of those that a mesh axis runs over, the one named last changes fastest.
Arguments:
- connectivity: int32 [4096, 64], P('dom'), may hold values from 0 to 4991, as said below
- send_down: int32 [32, 768], P('dom'), may hold values from 0 to 3455, as said below
- send_up: int32 [32, 768], P('dom'), may hold values from 0 to 3455, as said below
- jacobian: float32 [4096], P('dom'), may hold values from 0.5 to 4
- pair_blocks: bfloat16 [8192, 4096], P('dom'), may hold values from -0.75 to 0.75
- pair_target: int32 [8192], P('dom'), may hold values from 0 to 127
- pair_source: int32 [8192], P('dom'), may hold values from 0 to 127
- source_values: bfloat16 [32, 262144], P(None, 'dom'), may hold values from -6 to 6
Outputs:
- solution: float32 [32, 110592], P(None, 'dom')
- residual: float32 [32, 110592], P(None, 'dom')
- new_basis: float32 [32, 110592], P(None, 'dom')
The draws below stay inside these ranges and needn't reach their ends.
Inputs may be any that keep to these rules, and one draw needn't show every extreme that they name: `connectivity`: slots below 3456 are the partition's own nodes, the next 768 the lower neighbour's send_up list in order, the last 768 the upper neighbour's send_down list in order; the first partition uses no lower slots, the last no upper ones. `send_down`: distinct own node indices in each row. `send_up`: distinct own node indices in each row.
All inputs are finite; a program needn't handle non-finite values.
Results may differ from the reference program's by a relative error of at most 0.0003.
Values sent between devices are 32-bit elements; how exact they have to be, the bound alone decides.
A program may use at most 64 MiB of HBM per device.

```python
import math
import jax
import jax.numpy as jnp
import numpy as np
from jax import lax

TR = 32
NP = 64
NODE_DEV = 3456
F = 768
E_DEV = 128
E_SRC = 128
P_DEV = 256
DOMAINS = 32
NODES = 110592
ELEMS = 4096
PAIRS = 8192
SRC_NODES = 262144


def draw_connectivity(key, part):
    raw = jax.random.randint(key, (ELEMS, NP), 0, NODE_DEV + 2 * F, dtype=jnp.int32)
    device = (jnp.arange(ELEMS, dtype=jnp.int32) // E_DEV)[:, None]
    last_device = ELEMS // E_DEV - 1
    lower = (raw >= NODE_DEV) & (raw < NODE_DEV + F)
    upper = raw >= NODE_DEV + F
    raw = jnp.where((device == 0) & lower, raw - NODE_DEV, raw)
    raw = jnp.where((device == last_device) & upper, raw - NODE_DEV - F, raw)
    return raw.astype(jnp.int32)


def face_lists(key):
    keys = jax.random.split(key, DOMAINS)
    return jax.vmap(lambda single: jax.random.permutation(single, NODE_DEV)[:F])(keys).astype(jnp.int32)


def draw_send_down(key, part):
    return face_lists(jax.random.fold_in(key, 11))


def draw_send_up(key, part):
    return face_lists(jax.random.fold_in(key, 23))


def plant(entries, key, smallest, largest):
    spot = [jax.random.randint(jax.random.fold_in(key, axis), (), 0, length) for axis, length in enumerate(entries.shape)]
    main_axis = entries.shape.index(max(entries.shape))
    beside = spot[:main_axis] + [(spot[main_axis] + 1) % entries.shape[main_axis]] + spot[main_axis + 1:]
    return entries.at[tuple(spot)].set(smallest).at[tuple(beside)].set(largest)


def block_scale(own_key, shape, cuts, low, high):
    def one(position, shards_of):
        steps = jax.random.uniform(jax.random.fold_in(jax.random.fold_in(own_key, 6), position), (shards_of,), jnp.float32, low / len(cuts), high / len(cuts))
        return jnp.repeat(jnp.exp(steps), shape[position] // shards_of).reshape((-1,) + (1,) * (len(shape) - position - 1))

    level = one(*cuts[0])
    for cut in cuts[1:]:
        level = level * one(*cut)
    return level


def gaussian(own_key, dims, spread, bound, pieces=(), kind=jnp.bfloat16):
    values = spread * jax.random.normal(own_key, dims, jnp.float32)
    if pieces:
        values = values * block_scale(own_key, dims, pieces, -0.22, 0.18)
    return jnp.clip(values, -bound, bound).astype(kind)


def setup_inputs(seed: int = 0) -> dict:
    seeds = jax.random.split(jax.random.key(seed), 9)
    return {
        "connectivity": draw_connectivity(jax.random.fold_in(seeds[8], 71), 0),
        "send_down": draw_send_down(jax.random.fold_in(seeds[8], 71), 0),
        "send_up": draw_send_up(jax.random.fold_in(seeds[8], 71), 0),
        "jacobian": jnp.clip(jnp.exp(math.log(4.0) - 2.0794415 * jax.random.uniform(seeds[3], (ELEMS,), jnp.float32) ** block_scale(seeds[3], (ELEMS,), ((0, 32),), -0.2, 0.2)), 0.5, 4.0),
        "pair_blocks": gaussian(seeds[4], (PAIRS, NP * NP), NP ** -0.5, 0.75, ((0, 32),)),
        "pair_target": plant(jax.random.randint(seeds[5], (PAIRS,), 0, E_DEV), jax.random.fold_in(seeds[5], 1), 0, E_DEV - 1).astype(jnp.int32),
        "pair_source": plant(jax.random.randint(seeds[6], (PAIRS,), 0, E_SRC), jax.random.fold_in(seeds[6], 1), 0, E_SRC - 1).astype(jnp.int32),
        "source_values": gaussian(seeds[7], (TR, SRC_NODES), 1.0, 6.0, ((1, 32),)),
    }


line_mass = np.array([[128.0, 99.0, -36.0, 19.0], [99.0, 648.0, -81.0, -36.0], [-36.0, -81.0, 648.0, 99.0], [19.0, -36.0, 99.0, 128.0]]) / 504.0
mass_table = np.kron(np.kron(line_mass, line_mass), line_mass)

def node_ids(connectivity, send_down, send_up):
    count = connectivity.shape[0]
    domains = send_down.shape[0]
    device = (jnp.arange(count, dtype=jnp.int32) // E_DEV)[:, None]
    below = jnp.clip(device - 1, 0, domains - 1)
    above = jnp.clip(device + 1, 0, domains - 1)
    low_slot = jnp.clip(connectivity - NODE_DEV, 0, F - 1)
    high_slot = jnp.clip(connectivity - NODE_DEV - F, 0, F - 1)
    own = device * NODE_DEV + connectivity
    lower = below * NODE_DEV + send_up[below, low_slot]
    upper = above * NODE_DEV + send_down[above, high_slot]
    picked = jnp.where(connectivity < NODE_DEV, own, jnp.where(connectivity < NODE_DEV + F, lower, upper))
    return picked.astype(jnp.int32)

def mass_apply(field, ids, jacobian):
    element_mass = jnp.asarray(mass_table, dtype=field.dtype)
    grouped = ids.reshape(DOMAINS, E_DEV * NP)
    scales = jacobian.reshape(DOMAINS, E_DEV)

    def one_domain(total, item):
        flat, scale = item
        values = field[:, flat].reshape(TR, E_DEV, NP)
        image = jnp.einsum('tep,pq->teq', values, element_mass, precision=lax.Precision.HIGHEST) * scale[None, :, None]
        return (total.at[:, flat].add(image.reshape(TR, E_DEV * NP)), None)
    total, unused = lax.scan(one_domain, jnp.zeros_like(field), (grouped, scales))
    return total

def reference(connectivity, send_down, send_up, jacobian, pair_blocks, pair_target, pair_source, source_values):
    ids = node_ids(connectivity, send_down, send_up)
    grouped_ids = ids.reshape(DOMAINS, E_DEV, NP)
    offsets = jnp.arange(NP, dtype=jnp.int32)

    def one_domain(total, item):
        blocks, target, source, elem_ids, domain = item
        columns = ((domain * E_SRC + source)[:, None] * NP + offsets[None, :]).reshape(-1).astype(jnp.int32)
        values = source_values[:, columns].astype(jnp.float32).reshape(TR, P_DEV, NP)
        mixed = blocks.astype(jnp.float32).reshape(P_DEV, NP, NP)
        contrib = jnp.einsum('pij,tpj->tpi', mixed, values, precision=lax.Precision.HIGHEST)
        targets = elem_ids[target].reshape(-1)
        return (total.at[:, targets].add(contrib.reshape(TR, P_DEV * NP)), None)
    start = jnp.zeros((TR, NODES), jnp.float32)
    items = (pair_blocks.reshape(DOMAINS, P_DEV, NP * NP), pair_target.reshape(DOMAINS, P_DEV), pair_source.reshape(DOMAINS, P_DEV), grouped_ids, jnp.arange(DOMAINS, dtype=jnp.int32))
    right_side, unused = lax.scan(one_domain, start, items)
    high = lax.Precision.HIGHEST
    gram_rhs = jnp.dot(right_side, right_side.T, precision=high)
    lower_rhs = jnp.linalg.cholesky(gram_rhs)
    basis = jax.scipy.linalg.solve_triangular(lower_rhs, right_side, lower=True)
    image = mass_apply(basis, ids, jacobian)
    step_gram = jnp.dot(basis, image.T, precision=high)
    lower_step = jnp.linalg.cholesky(step_gram)
    coeffs = jax.scipy.linalg.cho_solve((lower_step, True), lower_rhs.T).T
    solution = jnp.dot(coeffs, basis, precision=high)
    residual = right_side - jnp.dot(coeffs, image, precision=high)
    lower_new = jnp.linalg.cholesky(jnp.dot(residual, residual.T, precision=high))
    new_basis = jax.scipy.linalg.solve_triangular(lower_new, residual, lower=True)
    return (solution, residual, new_basis)
```

```python
import functools

import jax
import jax.numpy as jnp
import numpy as np
from jax import lax
from jax.experimental import pallas as pl
from jax.experimental.pallas import tpu as pltpu
from jax.sharding import PartitionSpec as P

TR = 32
NP = 64
NODE_DEV = 3456
F = 768
LO = 384
Q_OWN = NODE_DEV // LO
Q_FACE = F // LO
Q_ALL = Q_OWN + 2 * Q_FACE
OWN = Q_OWN * TR
FACE = Q_FACE * TR
CHUNK = 512
GROUP = 8
MESH = pl.DeviceIdType.MESH
HIGH = lax.Precision.HIGHEST
F32 = jnp.float32
BF16 = jnp.bfloat16
NT = (((1,), (1,)), ((), ()))

line_mass = (
    np.array(
        [
            [128.0, 99.0, -36.0, 19.0],
            [99.0, 648.0, -81.0, -36.0],
            [-36.0, -81.0, 648.0, 99.0],
            [19.0, -36.0, 99.0, 128.0],
        ]
    )
    / 504.0
)
mass_table = np.kron(np.kron(line_mass, line_mass), line_mass)
node_order = np.arange(NP).reshape(NP // 2, 2).T.reshape(-1)
mass_block = np.kron(np.eye(4), mass_table[np.ix_(node_order, node_order)]).astype(np.float32)


def lane_ids(shape):
    return lax.broadcasted_iota(jnp.int32, shape, len(shape) - 1)


def pieces(value):
    first = value.astype(BF16)
    return first, (value - first.astype(F32)).astype(BF16)


def one_hot(lo_row):
    width = lo_row.shape[1]
    rows = lax.broadcasted_iota(jnp.int32, (LO, width), 0)
    return jnp.where(rows == lo_row, 1.0, 0.0).astype(BF16)


def scatter(values, lo_row, q_row, blocks, hot=None):
    hot = one_hot(lo_row) if hot is None else hot
    first, second = pieces(values)
    both = jnp.concatenate([first, second], axis=1)
    q_both = jnp.concatenate([q_row, q_row], axis=1)
    left = jnp.concatenate(
        [both * jnp.where(q_both == q, 1.0, 0.0).astype(BF16) for q in blocks], axis=0
    )
    right = jnp.concatenate([hot, hot], axis=1)
    return lax.dot_general(left, right, NT, preferred_element_type=F32)


def gather(table, lo_row, q_row, blocks, hot=None):
    hot = one_hot(lo_row) if hot is None else hot
    found = jnp.dot(table, jnp.concatenate([hot, hot], axis=0), preferred_element_type=F32)
    total = None
    for at, q in enumerate(blocks):
        part = jnp.where(q_row == q, found[at * TR : (at + 1) * TR], 0.0)
        total = part if total is None else total + part
    return total


def pair_kernel(
    target_ref, source_ref, blocks_ref, values_ref, lo_ref, q_ref, out_ref, flat, table, total
):
    pairs = blocks_ref.shape[0]
    elements = total.shape[0]
    lanes = lane_ids((TR, 128))

    for w in range(elements // 2):
        window = values_ref[:, w * 128 : (w + 1) * 128].astype(F32)
        turned = pltpu.roll(window, 64, 1)
        table[2 * w] = jnp.where(lanes < 64, window, turned).astype(BF16)
        table[2 * w + 1] = jnp.where(lanes < 64, turned, window).astype(BF16)

    def lay_out(g, carry):
        rows = blocks_ref[pl.ds(pl.multiple_of(g * 16, 16), 16), :]
        for c in range(32):
            flat[pl.ds(g * 512 + c, 16, stride=32), :] = rows[:, c * 128 : (c + 1) * 128].astype(F32)
        return carry

    lax.fori_loop(0, pairs // 16, lay_out, 0)
    total[...] = jnp.zeros_like(total)

    def multiply(step, carry):
        left, right = [], []
        for g in range(4):
            p = step * 4 + g
            left.append(table[source_ref[p]])
            block = flat[pl.ds(pl.multiple_of(p * 32, 32), 32), :]
            right.append(jnp.where(lanes < 64, block, 0.0).astype(BF16))
            right.append(jnp.where(lanes < 64, 0.0, block).astype(BF16))
        product = lax.dot_general(
            jnp.concatenate(left, axis=0),
            jnp.concatenate(right, axis=0),
            NT,
            preferred_element_type=F32,
        )
        for g in range(4):
            part = product[g * TR : (g + 1) * TR, (g // 2) * 128 : (g // 2 + 1) * 128]
            keep = (lanes < 64) if g % 2 == 0 else (lanes >= 64)
            at = target_ref[step * 4 + g]
            total[at] = total[at] + jnp.where(keep, part, 0.0)
        return carry

    lax.fori_loop(0, pairs // 4, multiply, 0, unroll=4)
    out_ref[...] = jnp.zeros_like(out_ref)

    def add(step, carry):
        tiles = []
        for m in range(CHUNK // 128):
            even = total[step * (CHUNK // NP) + 2 * m]
            odd = total[step * (CHUNK // NP) + 2 * m + 1]
            tiles.append(
                jnp.where(lanes < 64, even + pltpu.roll(even, 64, 1), odd + pltpu.roll(odd, 64, 1))
            )
        out_ref[...] += scatter(
            jnp.concatenate(tiles, axis=1),
            lo_ref[pl.ds(step, 1), :],
            q_ref[pl.ds(step, 1), :],
            range(Q_ALL),
        )
        return carry

    lax.fori_loop(0, lo_ref.shape[0], add, 0)


def exchange_kernel(
    n,
    ext_ref,
    lo_ref,
    q_ref,
    face_lo_ref,
    face_q_ref,
    scale_ref,
    mass_ref,
    right_ref,
    image_ref,
    gram_ref,
    table,
    ext,
    outgoing,
    incoming,
    near,
    far,
    send_sem,
    recv_sem,
    near_send,
    near_recv,
    far_send,
    far_recv,
):
    me = lax.axis_index("dom")
    group = min(GROUP, n)
    layers = n // group
    spot, layer = lax.rem(me, group), me // group
    has_up, has_down = me < n - 1, me > 0
    near_ids = [layer * group + lax.rem(spot + o, group) for o in range(1, group)]
    far_ids = [lax.rem(layer + o, layers) * group + spot for o in range(1, layers)]
    cross_up = jnp.logical_and(spot == group - 1, has_up)
    cross_down = jnp.logical_and(spot == 0, has_down)

    barrier = pltpu.get_barrier_semaphore()
    for other in near_ids + far_ids:
        pl.semaphore_signal(barrier, inc=1, device_id=(other,), device_id_type=MESH)

    @pl.when(cross_up)
    def _():
        pl.semaphore_signal(barrier, inc=1, device_id=(me + 1,), device_id_type=MESH)

    @pl.when(cross_down)
    def _():
        pl.semaphore_signal(barrier, inc=1, device_id=(me - 1,), device_id_type=MESH)

    partners = group + layers - 2
    crossing = jnp.logical_or(cross_up, cross_down)

    @pl.when(crossing)
    def _():
        pl.semaphore_wait(barrier, partners + 1)

    @pl.when(jnp.logical_not(crossing))
    def _():
        pl.semaphore_wait(barrier, partners)

    def copy(source, phase, way):
        return pltpu.make_async_remote_copy(
            src_ref=source,
            dst_ref=incoming.at[phase, way],
            send_sem=send_sem.at[phase, way],
            recv_sem=recv_sem.at[phase, way],
            device_id=(me + (1 if way else -1),),
            device_id_type=MESH,
        )

    def start(source, phase, way):
        @pl.when(has_up if way else has_down)
        def _():
            copy(source, phase, way).start()

    def finish(source, phase, way):
        @pl.when(has_up if way else has_down)
        def _():
            copy(source, phase, way).wait_send()

    def arrive(source, phase, way):
        @pl.when(has_down if way else has_up)
        def _():
            copy(source, phase, way).wait_recv()

        @pl.when(jnp.logical_not(has_down if way else has_up))
        def _():
            incoming[phase, way] = jnp.zeros((FACE, LO), F32)

    down_rows = pl.ds(OWN, FACE)
    up_rows = pl.ds(OWN + FACE, FACE)
    own_blocks = range(Q_OWN)

    def face_row(ref, at):
        return ref[at : at + 1, :]

    def settle(own, phase):
        for way in range(2):
            for b in range(Q_FACE):
                at = way * Q_FACE + b
                own = own + scatter(
                    incoming[phase, way, b * TR : (b + 1) * TR, :],
                    face_row(face_lo_ref, at),
                    face_row(face_q_ref, at),
                    own_blocks,
                )
        return own

    start(ext_ref.at[down_rows], 0, 0)
    start(ext_ref.at[up_rows], 0, 1)
    arrive(ext_ref.at[down_rows], 0, 0)
    arrive(ext_ref.at[up_rows], 0, 1)
    right = settle(ext_ref[0:OWN, :], 0)
    right_ref[...] = right
    first, second = pieces(right)
    table[0:OWN, 0:LO] = first
    table[0:OWN, LO : 2 * LO] = second

    for way in (1, 0):
        for b in range(Q_FACE):
            at = (1 - way) * Q_FACE + b
            outgoing[way, b * TR : (b + 1) * TR, :] = gather(
                table[0:OWN, :], face_row(face_lo_ref, at), face_row(face_q_ref, at), own_blocks
            )
        start(outgoing.at[way], 1, way)
    for way in (1, 0):
        arrive(outgoing.at[way], 1, way)
        rows = OWN if way else OWN + FACE
        first, second = pieces(incoming[1, way])
        table[rows : rows + FACE, 0:LO] = first
        table[rows : rows + FACE, LO : 2 * LO] = second

    ext[...] = jnp.zeros_like(ext)

    def element_step(step, carry):
        lo_row = lo_ref[pl.ds(step, 1), :]
        q_row = q_ref[pl.ds(step, 1), :]
        hot = one_hot(lo_row)
        found = gather(table[...], lo_row, q_row, range(Q_ALL), hot)
        first, second = pieces(
            jnp.concatenate([found[:, h : h + 256] for h in range(0, CHUNK, 256)], axis=0)
        )
        applied = (
            jnp.dot(first, mass_ref[0], preferred_element_type=F32)
            + jnp.dot(second, mass_ref[0], preferred_element_type=F32)
            + jnp.dot(first, mass_ref[1], preferred_element_type=F32)
        )
        applied = jnp.concatenate(
            [applied[h * TR : (h + 1) * TR] for h in range(CHUNK // 256)], axis=1
        )
        applied = applied * scale_ref[pl.ds(step, 1), :]
        ext[...] += scatter(applied, lo_row, q_row, range(Q_ALL), hot)
        return carry

    lax.fori_loop(0, lo_ref.shape[0], element_step, 0)
    start(ext.at[down_rows], 2, 0)
    start(ext.at[up_rows], 2, 1)
    arrive(ext.at[down_rows], 2, 0)
    arrive(ext.at[up_rows], 2, 1)
    image = settle(ext[0:OWN, :], 2)
    image_ref[...] = image

    nothing = jnp.zeros((TR, LO), F32)
    gram = jnp.zeros((TR, 128), F32)
    for q in range(Q_OWN):
        r = right_ref[q * TR : (q + 1) * TR, :]
        y = image_ref[q * TR : (q + 1) * TR, :]
        gram += lax.dot_general(
            r,
            jnp.concatenate([r, y, nothing, nothing], axis=0),
            NT,
            precision=HIGH,
            preferred_element_type=F32,
        )
        gram += lax.dot_general(
            y,
            jnp.concatenate([nothing, nothing, y, nothing], axis=0),
            NT,
            precision=HIGH,
            preferred_element_type=F32,
        )

    def sum_over(value, buffer, others, sends, recvs):
        buffer[0] = value

        def part(o, other):
            return pltpu.make_async_remote_copy(
                src_ref=buffer.at[0],
                dst_ref=buffer.at[o],
                send_sem=sends.at[o],
                recv_sem=recvs.at[o],
                device_id=(other,),
                device_id_type=MESH,
            )

        for o, other in enumerate(others, 1):
            part(o, other).start()
        for o, other in enumerate(others, 1):
            part(o, other).wait_recv()
            value = value + buffer[o]
        for o, other in enumerate(others, 1):
            part(o, other).wait_send()
        return value

    gram = sum_over(gram, near, near_ids, near_send, near_recv)
    gram_ref[...] = sum_over(gram, far, far_ids, far_send, far_recv)

    finish(ext_ref.at[down_rows], 0, 0)
    finish(ext_ref.at[up_rows], 0, 1)
    for way in range(2):
        finish(outgoing.at[way], 1, way)
    finish(ext.at[down_rows], 2, 0)
    finish(ext.at[up_rows], 2, 1)


def output_kernel(gram_ref, right_ref, image_ref, solution_ref, residual_ref, basis_ref):
    def dot(a, b):
        return jnp.dot(a, b, precision=HIGH, preferred_element_type=F32)

    rows = lax.broadcasted_iota(jnp.int32, (TR, 128), 0)
    lanes = lane_ids((TR, 128))
    work = gram_ref[...]
    gram = work[:, 0:TR]
    for j in range(TR):
        pivot = work[j : j + 1, :] / work[j : j + 1, TR + j : TR + j + 1]
        work = jnp.where(rows == j, pivot, work - work[:, TR + j : TR + j + 1] * pivot)
    step_t = work[:, 0:TR]
    step = step_t.T
    image_part = work[:, 2 * TR : 3 * TR]
    new_gram = dot(gram, dot(image_part, step_t)) - gram
    work = jnp.concatenate([new_gram, jnp.zeros((TR, 128 - TR), F32)], axis=1)
    work = jnp.where(lanes == rows + TR, 1.0, work)
    scale = jnp.zeros((TR, 128), F32)
    for j in range(TR):
        pivot = work[j : j + 1, j : j + 1]
        scale = jnp.where(rows == j, lax.rsqrt(pivot), scale)
        factor = work[:, j : j + 1] / pivot
        work = jnp.where(rows > j, work - factor * work[j : j + 1, :], work)
    lower = (work * scale)[:, TR : 2 * TR]
    for q in range(Q_OWN):
        at = slice(q * LO, (q + 1) * LO)
        r = right_ref[q * TR : (q + 1) * TR, :]
        left = r - dot(step, image_ref[q * TR : (q + 1) * TR, :])
        solution_ref[:, at] = dot(step, r)
        residual_ref[:, at] = left
        basis_ref[:, at] = dot(lower, left)


def per_device(
    n, connectivity, send_down, send_up, jacobian, pair_blocks, pair_target, pair_source, source_values
):
    elements = connectivity.shape[0]
    pairs = pair_target.shape[0]
    chunks = elements * NP // CHUNK
    vmem = pl.BlockSpec(memory_space=pltpu.VMEM)
    smem = pl.BlockSpec(memory_space=pltpu.SMEM)

    slots = connectivity.reshape(elements, NP // 2, 2).transpose(0, 2, 1).reshape(chunks, CHUNK)
    q_ids = slots // LO
    lo_ids = slots - q_ids * LO
    faces = jnp.concatenate([send_up[0].reshape(Q_FACE, LO), send_down[0].reshape(Q_FACE, LO)])
    face_q = faces // LO
    face_lo = faces - face_q * LO
    scale = jnp.repeat(jacobian, NP).reshape(chunks, CHUNK)
    mass = jnp.asarray(mass_block)
    mass_first = mass.astype(BF16)
    mass_pair = jnp.stack([mass_first, (mass - mass_first.astype(F32)).astype(BF16)])

    ext = pl.pallas_call(
        pair_kernel,
        out_shape=jax.ShapeDtypeStruct((Q_ALL * TR, LO), F32),
        in_specs=[smem, smem, vmem, vmem, vmem, vmem],
        out_specs=vmem,
        scratch_shapes=[
            pltpu.VMEM((pairs * 32, 128), F32),
            pltpu.VMEM((elements, TR, 128), BF16),
            pltpu.VMEM((elements, TR, 128), F32),
        ],
        compiler_params=pltpu.CompilerParams(vmem_limit_bytes=48 * 2**20),
        name="pair_stage",
    )(pair_target, pair_source, pair_blocks, source_values, lo_ids, q_ids)

    group = min(GROUP, n)
    layers = n // group
    field = jax.ShapeDtypeStruct((OWN, LO), F32)
    right, image, gram = pl.pallas_call(
        functools.partial(exchange_kernel, n),
        out_shape=(field, field, jax.ShapeDtypeStruct((TR, 128), F32)),
        in_specs=[vmem] * 7,
        out_specs=(vmem, vmem, vmem),
        scratch_shapes=[
            pltpu.VMEM((Q_ALL * TR, 2 * LO), BF16),
            pltpu.VMEM((Q_ALL * TR, LO), F32),
            pltpu.VMEM((2, FACE, LO), F32),
            pltpu.VMEM((3, 2, FACE, LO), F32),
            pltpu.VMEM((group, TR, 128), F32),
            pltpu.VMEM((layers, TR, 128), F32),
            pltpu.SemaphoreType.DMA((3, 2)),
            pltpu.SemaphoreType.DMA((3, 2)),
            pltpu.SemaphoreType.DMA((group,)),
            pltpu.SemaphoreType.DMA((group,)),
            pltpu.SemaphoreType.DMA((layers,)),
            pltpu.SemaphoreType.DMA((layers,)),
        ],
        compiler_params=pltpu.CompilerParams(
            collective_id=0, has_side_effects=True, vmem_limit_bytes=48 * 2**20
        ),
        name="exchange_stage",
    )(ext, lo_ids, q_ids, face_lo, face_q, scale, mass_pair)

    out = jax.ShapeDtypeStruct((TR, NODE_DEV), F32)
    return pl.pallas_call(
        output_kernel,
        out_shape=(out, out, out),
        in_specs=[vmem] * 3,
        out_specs=(vmem, vmem, vmem),
        compiler_params=pltpu.CompilerParams(vmem_limit_bytes=32 * 2**20),
        name="output_stage",
    )(gram, right, image)


def solution(mesh):
    return jax.shard_map(
        functools.partial(per_device, mesh.shape["dom"]),
        mesh=mesh,
        in_specs=(
            P("dom", None),
            P("dom", None),
            P("dom", None),
            P("dom"),
            P("dom", None),
            P("dom"),
            P("dom"),
            P(None, "dom"),
        ),
        out_specs=(P(None, "dom"), P(None, "dom"), P(None, "dom")),
        check_vma=False,
    )
```

```python
import functools

import jax
import jax.numpy as jnp
import ml_dtypes
import numpy as np
from jax import lax
from jax.experimental import pallas as pl
from jax.experimental.pallas import tpu as pltpu
from jax.sharding import PartitionSpec as P

TR = 32
NP = 64
NODE_DEV = 3456
F = 768
LO = 384
Q_OWN = NODE_DEV // LO
Q_FACE = F // LO
Q_ALL = Q_OWN + 2 * Q_FACE
OWN = Q_OWN * TR
FACE = Q_FACE * TR
CHUNK = 512
GROUP = 8
MESH = pl.DeviceIdType.MESH
HIGH = lax.Precision.HIGHEST
F32 = jnp.float32
BF16 = jnp.bfloat16
NT = (((1,), (1,)), ((), ()))

line_mass = (
    np.array(
        [
            [128.0, 99.0, -36.0, 19.0],
            [99.0, 648.0, -81.0, -36.0],
            [-36.0, -81.0, 648.0, 99.0],
            [19.0, -36.0, 99.0, 128.0],
        ]
    )
    / 504.0
)
mass_table = np.kron(np.kron(line_mass, line_mass), line_mass)
node_order = np.arange(NP).reshape(NP // 2, 2).T.reshape(-1)
mass_block = np.kron(np.eye(4), mass_table[np.ix_(node_order, node_order)]).astype(np.float32)
mass_first = mass_block.astype(ml_dtypes.bfloat16)
mass_pair = np.stack(
    [mass_first, (mass_block - mass_first.astype(np.float32)).astype(ml_dtypes.bfloat16)]
)
order_table = np.tile(np.eye(NP, dtype=np.float32)[:, node_order], (1, 2))


def lane_ids(shape):
    return lax.broadcasted_iota(jnp.int32, shape, len(shape) - 1)


def pieces(value):
    first = value.astype(BF16)
    return first, (value - first.astype(F32)).astype(BF16)


def one_hot(lo_row):
    width = lo_row.shape[1]
    rows = lax.broadcasted_iota(jnp.int32, (LO, width), 0)
    return jnp.where(rows == lo_row, 1.0, 0.0).astype(BF16)


def spread(both, q_both, blocks):
    return jnp.concatenate(
        [both * jnp.where(q_both == q, 1.0, 0.0).astype(BF16) for q in blocks], axis=0
    )


def twice(value, axis):
    return jnp.concatenate([value, value], axis=axis)


def add_up(left, right):
    return lax.dot_general(left, right, NT, preferred_element_type=F32)


def gather(table, q_row, blocks, hot):
    found = jnp.dot(table, twice(hot, 0), preferred_element_type=F32)
    total = None
    for at, q in enumerate(blocks):
        part = jnp.where(q_row == q, found[at * TR : (at + 1) * TR], 0.0)
        total = part if total is None else total + part
    return total


def split_slots(slots):
    q = jnp.right_shift(jnp.right_shift(slots, 7) * 43, 7)
    return q, slots - q * LO


def pair_kernel(
    target_ref,
    source_ref,
    blocks_hbm,
    values_ref,
    slots_ref,
    jacobian_ref,
    order_ref,
    out_ref,
    lo_ref,
    q_ref,
    scale_ref,
    blocks_ref,
    flat,
    table,
    total,
    wide,
    blocks_sem,
):
    pairs = blocks_ref.shape[0]
    elements = total.shape[0]
    chunks = lo_ref.shape[0]
    per_chunk = CHUNK // NP
    lanes = lane_ids((TR, 128))

    fetch = pltpu.make_async_copy(blocks_hbm, blocks_ref, blocks_sem)
    fetch.start()

    def by_chunk():
        left_half = lane_ids((chunks, 128)) < 64
        return jnp.concatenate(
            [
                jnp.where(
                    left_half,
                    wide[pl.ds(2 * m, chunks, stride=per_chunk), :],
                    wide[pl.ds(2 * m + 1, chunks, stride=per_chunk), :],
                )
                for m in range(CHUNK // 128)
            ],
            axis=1,
        )

    wide[...] = jnp.dot(
        slots_ref[...].astype(F32), order_ref[...], precision=HIGH, preferred_element_type=F32
    )
    q_ids, lo_ids = split_slots((by_chunk() + 0.5).astype(jnp.int32))
    q_ref[...] = q_ids
    lo_ref[...] = lo_ids
    corner = lax.broadcasted_iota(jnp.int32, (elements, elements), 0) == lane_ids((elements, elements))
    wide[...] = jnp.dot(
        jnp.where(corner, jacobian_ref[...], 0.0),
        jnp.ones((elements, 128), F32),
        precision=HIGH,
        preferred_element_type=F32,
    )
    scale_ref[...] = by_chunk()

    for w in range(elements // 2):
        window = values_ref[:, w * 128 : (w + 1) * 128].astype(F32)
        turned = pltpu.roll(window, 64, 1)
        table[2 * w] = jnp.where(lanes < 64, window, turned).astype(BF16)
        table[2 * w + 1] = jnp.where(lanes < 64, turned, window).astype(BF16)
    total[...] = jnp.zeros_like(total)
    out_ref[...] = jnp.zeros_like(out_ref)
    fetch.wait()

    def lay_out(g, carry):
        rows = blocks_ref[pl.ds(pl.multiple_of(g * 16, 16), 16), :]
        for c in range(32):
            flat[pl.ds(g * 512 + c, 16, stride=32), :] = rows[:, c * 128 : (c + 1) * 128].astype(F32)
        return carry

    lax.fori_loop(0, pairs // 16, lay_out, 0)

    def multiply(step, carry):
        left, right = [], []
        for g in range(4):
            p = step * 4 + g
            left.append(table[source_ref[p]])
            block = flat[pl.ds(pl.multiple_of(p * 32, 32), 32), :]
            right.append(jnp.where(lanes < 64, block, 0.0).astype(BF16))
            right.append(jnp.where(lanes < 64, 0.0, block).astype(BF16))
        product = add_up(jnp.concatenate(left, axis=0), jnp.concatenate(right, axis=0))
        for g in range(4):
            part = product[g * TR : (g + 1) * TR, (g // 2) * 128 : (g // 2 + 1) * 128]
            keep = (lanes < 64) if g % 2 == 0 else (lanes >= 64)
            at = target_ref[step * 4 + g]
            total[at] = total[at] + jnp.where(keep, part, 0.0)
        return carry

    lax.fori_loop(0, pairs // 4, multiply, 0, unroll=8)

    def add(step, carry):
        tiles = []
        for m in range(CHUNK // 128):
            even = total[step * per_chunk + 2 * m]
            odd = total[step * per_chunk + 2 * m + 1]
            tiles.append(
                jnp.where(lanes < 64, even + pltpu.roll(even, 64, 1), odd + pltpu.roll(odd, 64, 1))
            )
        both = jnp.concatenate(pieces(jnp.concatenate(tiles, axis=1)), axis=1)
        q_both = twice(q_ref[pl.ds(step, 1), :], 1)
        hot = one_hot(lo_ref[pl.ds(step, 1), :])
        out_ref[...] += add_up(spread(both, q_both, range(Q_ALL)), twice(hot, 1))
        return carry

    lax.fori_loop(0, chunks, add, 0, unroll=2)


def exchange_kernel(
    n,
    ext_ref,
    lo_ref,
    q_ref,
    scale_ref,
    up_ref,
    down_ref,
    mass_ref,
    right_ref,
    image_ref,
    gram_ref,
    table,
    hot,
    face_hot,
    found,
    applied,
    ext,
    outgoing,
    incoming,
    near,
    far,
    send_sem,
    recv_sem,
    near_send,
    near_recv,
    far_send,
    far_recv,
):
    me = lax.axis_index("dom")
    group = min(GROUP, n)
    layers = n // group
    spot, layer = lax.rem(me, group), me // group
    has_up, has_down = me < n - 1, me > 0
    near_ids = [layer * group + lax.rem(spot + o, group) for o in range(1, group)]
    far_ids = [lax.rem(layer + o, layers) * group + spot for o in range(1, layers)]
    cross_up = jnp.logical_and(spot == group - 1, has_up)
    cross_down = jnp.logical_and(spot == 0, has_down)

    barrier = pltpu.get_barrier_semaphore()
    for other in near_ids + far_ids:
        pl.semaphore_signal(barrier, inc=1, device_id=(other,), device_id_type=MESH)

    @pl.when(cross_up)
    def _():
        pl.semaphore_signal(barrier, inc=1, device_id=(me + 1,), device_id_type=MESH)

    @pl.when(cross_down)
    def _():
        pl.semaphore_signal(barrier, inc=1, device_id=(me - 1,), device_id_type=MESH)

    partners = group + layers - 2
    crossing = jnp.logical_or(cross_up, cross_down)

    @pl.when(crossing)
    def _():
        pl.semaphore_wait(barrier, partners + 1)

    @pl.when(jnp.logical_not(crossing))
    def _():
        pl.semaphore_wait(barrier, partners)

    def copy(source, phase, way):
        return pltpu.make_async_remote_copy(
            src_ref=source,
            dst_ref=incoming.at[phase, way],
            send_sem=send_sem.at[phase, way],
            recv_sem=recv_sem.at[phase, way],
            device_id=(me + (1 if way else -1),),
            device_id_type=MESH,
        )

    def start(source, phase, way):
        @pl.when(has_up if way else has_down)
        def _():
            copy(source, phase, way).start()

    def finish(source, phase, way):
        @pl.when(has_up if way else has_down)
        def _():
            copy(source, phase, way).wait_send()

    def arrive(source, phase, way):
        @pl.when(has_down if way else has_up)
        def _():
            copy(source, phase, way).wait_recv()

        @pl.when(jnp.logical_not(has_down if way else has_up))
        def _():
            incoming[phase, way] = jnp.zeros((FACE, LO), F32)

    down_rows = pl.ds(OWN, FACE)
    up_rows = pl.ds(OWN + FACE, FACE)
    own_blocks, face_blocks = range(Q_OWN), range(Q_OWN, Q_ALL)
    chunks = lo_ref.shape[0]

    start(ext_ref.at[down_rows], 0, 0)
    start(ext_ref.at[up_rows], 0, 1)

    def mark(step, carry):
        hot[step] = one_hot(lo_ref[pl.ds(step, 1), :])
        return carry

    lax.fori_loop(0, chunks, mark, 0)
    faces = [split_slots(up_ref[...]), split_slots(down_ref[...])]
    for way in range(2):
        face_hot[way] = one_hot(faces[way][1])

    def settle(own, phase):
        left, right = [], []
        for way in range(2):
            for b in range(Q_FACE):
                part = slice(b * LO, (b + 1) * LO)
                both = jnp.concatenate(
                    pieces(incoming[phase, way, b * TR : (b + 1) * TR, :]), axis=1
                )
                left.append(spread(both, twice(faces[way][0][:, part], 1), own_blocks))
                right.append(twice(face_hot[way, :, part], 1))
        return own + add_up(jnp.concatenate(left, axis=1), jnp.concatenate(right, axis=1))

    arrive(ext_ref.at[down_rows], 0, 0)
    arrive(ext_ref.at[up_rows], 0, 1)
    right = settle(ext_ref[0:OWN, :], 0)
    first, second = pieces(right)
    table[0:OWN, 0:LO] = first
    table[0:OWN, LO : 2 * LO] = second

    for way in (1, 0):
        values = gather(table[0:OWN, :], faces[1 - way][0], own_blocks, face_hot[1 - way])
        for b in range(Q_FACE):
            outgoing[way, b * TR : (b + 1) * TR, :] = values[:, b * LO : (b + 1) * LO]
        start(outgoing.at[way], 1, way)

    def own_values(step, carry):
        q_row = q_ref[pl.ds(step, 1), :]
        found[step] = gather(table[0:OWN, :], q_row, own_blocks, hot[step])
        return carry

    lax.fori_loop(0, chunks, own_values, 0, unroll=2)
    for q in own_blocks:
        right_ref[:, q * LO : (q + 1) * LO] = right[q * TR : (q + 1) * TR]
    ext[...] = jnp.zeros_like(ext)
    for way in (1, 0):
        arrive(outgoing.at[way], 1, way)
        rows = OWN if way else OWN + FACE
        first, second = pieces(incoming[1, way])
        table[rows : rows + FACE, 0:LO] = first
        table[rows : rows + FACE, LO : 2 * LO] = second

    def elements(step, carry):
        q_row = q_ref[pl.ds(step, 1), :]
        values = found[step] + gather(table[OWN:, :], q_row, face_blocks, hot[step])
        first, second = pieces(
            jnp.concatenate([values[:, h : h + 256] for h in range(0, CHUNK, 256)], axis=0)
        )
        result = (
            jnp.dot(first, mass_ref[0], preferred_element_type=F32)
            + jnp.dot(second, mass_ref[0], preferred_element_type=F32)
            + jnp.dot(first, mass_ref[1], preferred_element_type=F32)
        )
        result = jnp.concatenate(
            [result[h * TR : (h + 1) * TR] for h in range(CHUNK // 256)], axis=1
        )
        both = jnp.concatenate(pieces(result * scale_ref[pl.ds(step, 1), :]), axis=1)
        applied[step] = both
        ext[OWN:, :] += add_up(spread(both, twice(q_row, 1), face_blocks), twice(hot[step], 1))
        return carry

    lax.fori_loop(0, chunks, elements, 0, unroll=2)
    start(ext.at[down_rows], 2, 0)
    start(ext.at[up_rows], 2, 1)

    def own_sums(step, carry):
        q_both = twice(q_ref[pl.ds(step, 1), :], 1)
        ext[0:OWN, :] += add_up(spread(applied[step], q_both, own_blocks), twice(hot[step], 1))
        return carry

    lax.fori_loop(0, chunks, own_sums, 0, unroll=2)
    arrive(ext.at[down_rows], 2, 0)
    arrive(ext.at[up_rows], 2, 1)
    image = settle(ext[0:OWN, :], 2)
    for q in own_blocks:
        image_ref[:, q * LO : (q + 1) * LO] = image[q * TR : (q + 1) * TR]

    def as_row(value):
        return jnp.concatenate([value[q * TR : (q + 1) * TR] for q in own_blocks], axis=1)

    first, second = pieces(image)
    stack = jnp.concatenate(
        [
            as_row(table[0:OWN, 0:LO]),
            as_row(table[0:OWN, LO : 2 * LO]),
            as_row(first),
            as_row(second),
        ],
        axis=0,
    )
    products = add_up(stack, stack)
    lanes = lane_ids((TR, 128))
    upper = products[0:TR] + products[TR : 2 * TR]
    lower = products[2 * TR : 3 * TR] + products[3 * TR :]
    upper = upper + pltpu.roll(upper, 96, 1)
    lower = pltpu.roll(lower + pltpu.roll(lower, 96, 1), 96, 1)
    gram = jnp.where(jnp.logical_and(lanes >= TR, lanes < 2 * TR), lower, upper)

    def sum_over(value, buffer, others, sends, recvs):
        buffer[0] = value

        def part(o, other):
            return pltpu.make_async_remote_copy(
                src_ref=buffer.at[0],
                dst_ref=buffer.at[o],
                send_sem=sends.at[o],
                recv_sem=recvs.at[o],
                device_id=(other,),
                device_id_type=MESH,
            )

        for o, other in enumerate(others, 1):
            part(o, other).start()
        for o, other in enumerate(others, 1):
            part(o, other).wait_recv()
            value = value + buffer[o]
        for o, other in enumerate(others, 1):
            part(o, other).wait_send()
        return value

    gram = sum_over(gram, near, near_ids, near_send, near_recv)
    gram_ref[...] = sum_over(gram, far, far_ids, far_send, far_recv)

    finish(ext_ref.at[down_rows], 0, 0)
    finish(ext_ref.at[up_rows], 0, 1)
    for way in range(2):
        finish(outgoing.at[way], 1, way)
    finish(ext.at[down_rows], 2, 0)
    finish(ext.at[up_rows], 2, 1)


def output_kernel(gram_ref, right_ref, image_ref, solution_ref, residual_ref, basis_ref):
    def dot(a, b):
        return jnp.dot(a, b, precision=HIGH, preferred_element_type=F32)

    rows = lax.broadcasted_iota(jnp.int32, (TR, 128), 0)
    lanes = lane_ids((TR, 128))
    work = gram_ref[...]
    gram = work[:, 0:TR]
    for j in range(0, TR, 2):
        c = 2 * TR + j
        a, b = work[j : j + 1, :], work[j + 1 : j + 2, :]
        inverse = 1.0 / a[:, c : c + 1]
        across = a[:, c + 1 : c + 2] * inverse
        b = b - (b[:, c : c + 1] * inverse) * a
        b = b * (1.0 / b[:, c + 1 : c + 2])
        a = a * inverse - across * b
        rest = work - work[:, c : c + 1] * a - work[:, c + 1 : c + 2] * b
        work = jnp.where(rows == j, a, jnp.where(rows == j + 1, b, rest))
    step_t = work[:, 0:TR]
    step = step_t.T
    image_part = work[:, TR : 2 * TR]
    new_gram = dot(gram, dot(image_part, step_t)) - gram

    def times(small):
        first, second = pieces(small)
        both = jnp.concatenate([first, second], axis=0)

        def apply(value):
            top, rest = pieces(value)
            found = jnp.dot(both, top, preferred_element_type=F32)
            return (
                found[0:TR] + found[TR : 2 * TR] + jnp.dot(first, rest, preferred_element_type=F32)
            )

        return apply

    parts = [slice(at, at + 3 * LO) for at in range(0, Q_OWN * LO, 3 * LO)]
    apply_step = times(step)
    for part in parts:
        right = right_ref[:, part]
        solution_ref[:, part] = apply_step(right)
        residual_ref[:, part] = right - apply_step(image_ref[:, part])

    work = jnp.concatenate([new_gram, jnp.zeros((TR, 128 - TR), F32)], axis=1)
    work = jnp.where(lanes == rows + TR, 1.0, work)
    scale = jnp.zeros((TR, 128), F32)
    for j in range(0, TR, 2):
        a, b = work[j : j + 1, :], work[j + 1 : j + 2, :]
        pivot, across = a[:, j : j + 1], a[:, j + 1 : j + 2]
        inverse = 1.0 / pivot
        b = b - (b[:, j : j + 1] * inverse) * a
        second_pivot = b[:, j + 1 : j + 2]
        factor = work[:, j : j + 1] * inverse
        second = (work[:, j + 1 : j + 2] - factor * across) * (1.0 / second_pivot)
        rest = work - factor * a - second * b
        work = jnp.where(rows > j + 1, rest, jnp.where(rows == j + 1, b, work))
        scale = jnp.where(rows == j, lax.rsqrt(pivot), scale)
        scale = jnp.where(rows == j + 1, lax.rsqrt(second_pivot), scale)
    apply_lower = times((work * scale)[:, TR : 2 * TR])
    for part in parts:
        basis_ref[:, part] = apply_lower(residual_ref[:, part])


def per_device(
    n, connectivity, send_down, send_up, jacobian, pair_blocks, pair_target, pair_source, source_values
):
    elements = connectivity.shape[0]
    pairs = pair_target.shape[0]
    chunks = elements * NP // CHUNK
    vmem = pl.BlockSpec(memory_space=pltpu.VMEM)
    smem = pl.BlockSpec(memory_space=pltpu.SMEM)

    ids = jax.ShapeDtypeStruct((chunks, CHUNK), jnp.int32)
    ext, lo_ids, q_ids, scale = pl.pallas_call(
        pair_kernel,
        out_shape=(
            jax.ShapeDtypeStruct((Q_ALL * TR, LO), F32),
            ids,
            ids,
            jax.ShapeDtypeStruct((chunks, CHUNK), F32),
        ),
        in_specs=[smem, smem, pl.BlockSpec(memory_space=pl.ANY), vmem, vmem, vmem, vmem],
        out_specs=(vmem,) * 4,
        scratch_shapes=[
            pltpu.VMEM(pair_blocks.shape, BF16),
            pltpu.VMEM((pairs * 32, 128), F32),
            pltpu.VMEM((elements, TR, 128), BF16),
            pltpu.VMEM((elements, TR, 128), F32),
            pltpu.VMEM((elements, 128), F32),
            pltpu.SemaphoreType.DMA,
        ],
        compiler_params=pltpu.CompilerParams(vmem_limit_bytes=48 * 2**20),
        name="pair_stage",
    )(
        pair_target,
        pair_source,
        pair_blocks,
        source_values,
        connectivity,
        jacobian.reshape(1, elements),
        jnp.asarray(order_table),
    )

    group = min(GROUP, n)
    layers = n // group
    field = jax.ShapeDtypeStruct((TR, NODE_DEV), F32)
    right, image, gram = pl.pallas_call(
        functools.partial(exchange_kernel, n),
        out_shape=(field, field, jax.ShapeDtypeStruct((TR, 128), F32)),
        in_specs=[vmem] * 7,
        out_specs=(vmem, vmem, vmem),
        scratch_shapes=[
            pltpu.VMEM((Q_ALL * TR, 2 * LO), BF16),
            pltpu.VMEM((chunks, LO, CHUNK), BF16),
            pltpu.VMEM((2, LO, F), BF16),
            pltpu.VMEM((chunks, TR, CHUNK), F32),
            pltpu.VMEM((chunks, TR, 2 * CHUNK), BF16),
            pltpu.VMEM((Q_ALL * TR, LO), F32),
            pltpu.VMEM((2, FACE, LO), F32),
            pltpu.VMEM((3, 2, FACE, LO), F32),
            pltpu.VMEM((group, TR, 128), F32),
            pltpu.VMEM((layers, TR, 128), F32),
            pltpu.SemaphoreType.DMA((3, 2)),
            pltpu.SemaphoreType.DMA((3, 2)),
            pltpu.SemaphoreType.DMA((group,)),
            pltpu.SemaphoreType.DMA((group,)),
            pltpu.SemaphoreType.DMA((layers,)),
            pltpu.SemaphoreType.DMA((layers,)),
        ],
        compiler_params=pltpu.CompilerParams(
            collective_id=0, has_side_effects=True, vmem_limit_bytes=48 * 2**20
        ),
        name="exchange_stage",
    )(ext, lo_ids, q_ids, scale, send_up, send_down, jnp.asarray(mass_pair))

    out = jax.ShapeDtypeStruct((TR, NODE_DEV), F32)
    return pl.pallas_call(
        output_kernel,
        out_shape=(out, out, out),
        in_specs=[vmem] * 3,
        out_specs=(vmem, vmem, vmem),
        compiler_params=pltpu.CompilerParams(vmem_limit_bytes=32 * 2**20),
        name="output_stage",
    )(gram, right, image)


def solution(mesh):
    return jax.shard_map(
        functools.partial(per_device, mesh.shape["dom"]),
        mesh=mesh,
        in_specs=(
            P("dom", None),
            P("dom", None),
            P("dom", None),
            P("dom"),
            P("dom", None),
            P("dom"),
            P("dom"),
            P(None, "dom"),
        ),
        out_specs=(P(None, "dom"), P(None, "dom"), P(None, "dom")),
        check_vma=False,
    )
```

```python
import functools

import jax
import jax.numpy as jnp
from jax import lax
from jax.experimental import pallas as pl
from jax.experimental.pallas import tpu as pltpu
from jax.sharding import PartitionSpec as P

TR = 32
NP = 64
NODE_DEV = 3456
F = 768
LO = 384
Q_OWN = NODE_DEV // LO
Q_FACE = F // LO
Q_ALL = Q_OWN + 2 * Q_FACE
OWN = Q_OWN * TR
FACE = Q_FACE * TR
CHUNK = 512
GROUP = 8
MESH = pl.DeviceIdType.MESH
HIGH = lax.Precision.HIGHEST
F32 = jnp.float32
BF16 = jnp.bfloat16
NT = (((1,), (1,)), ((), ()))


def line_entry(a, b):
    apart = jnp.abs(a - b)
    inner = jnp.logical_or(a == 1, a == 2)
    near = jnp.where(a + b == 3, -81.0, 99.0)
    far = jnp.where(apart == 2, -36.0, 19.0)
    return jnp.where(apart == 0, jnp.where(inner, 648.0, 128.0), jnp.where(apart == 1, near, far))


def node_of(position):
    return jnp.bitwise_and(position, 31) * 2 + jnp.bitwise_and(jnp.right_shift(position, 5), 1)


def mass_block():
    shape = (4 * NP, 4 * NP)
    rows, columns = lax.broadcasted_iota(jnp.int32, shape, 0), lane_ids(shape)
    first, second = node_of(rows), node_of(columns)
    value = jnp.where(jnp.right_shift(rows, 6) == jnp.right_shift(columns, 6), 504.0**-3, 0.0)
    for digit in (0, 2, 4):
        value = value * line_entry(
            jnp.bitwise_and(jnp.right_shift(first, digit), 3),
            jnp.bitwise_and(jnp.right_shift(second, digit), 3),
        )
    return value


def lane_ids(shape):
    return lax.broadcasted_iota(jnp.int32, shape, len(shape) - 1)


def pieces(value):
    first = value.astype(BF16)
    return first, (value - first.astype(F32)).astype(BF16)


def one_hot(lo_row):
    width = lo_row.shape[1]
    rows = lax.broadcasted_iota(jnp.int32, (LO, width), 0)
    return jnp.where(rows == lo_row, 1.0, 0.0).astype(BF16)


def stacked(value):
    return jnp.concatenate(pieces(value), axis=0)


def spread(stack, q_row, blocks):
    return jnp.concatenate(
        [stack * jnp.where(q_row == q, 1.0, 0.0).astype(BF16) for q in blocks], axis=0
    )


def add_up(left, right):
    return lax.dot_general(left, right, NT, preferred_element_type=F32)


def joined(value):
    return jnp.concatenate(
        [
            value[at : at + TR] + value[at + TR : at + 2 * TR]
            for at in range(0, value.shape[0], 2 * TR)
        ],
        axis=0,
    )


def scatter(stack, q_row, blocks, hot):
    return joined(add_up(spread(stack, q_row, blocks), hot))


def gather(table, q_row, blocks, hot):
    found = jnp.dot(table, hot, preferred_element_type=F32)
    total = None
    for at, q in enumerate(blocks):
        rows = found[2 * at * TR : (2 * at + 2) * TR]
        part = jnp.where(q_row == q, rows[0:TR] + rows[TR:], 0.0)
        total = part if total is None else total + part
    return total


def split_slots(slots):
    q = jnp.right_shift(jnp.right_shift(slots, 7) * 43, 7)
    return q, slots - q * LO


def pair_kernel(
    target_ref,
    source_ref,
    blocks_hbm,
    values_ref,
    slots_ref,
    jacobian_ref,
    up_ref,
    down_ref,
    out_ref,
    lo_ref,
    q_ref,
    scale_ref,
    face_lo_ref,
    face_q_ref,
    blocks_ref,
    flat,
    table,
    total,
    wide,
    blocks_sem,
):
    pairs = blocks_ref.shape[0]
    elements = total.shape[0]
    chunks = lo_ref.shape[0]
    per_chunk = CHUNK // NP
    lanes = lane_ids((TR, 128))

    fetch = pltpu.make_async_copy(blocks_hbm, blocks_ref, blocks_sem)
    fetch.start()

    def by_chunk():
        left_half = lane_ids((chunks, 128)) < 64
        return jnp.concatenate(
            [
                jnp.where(
                    left_half,
                    wide[pl.ds(2 * m, chunks, stride=per_chunk), :],
                    wide[pl.ds(2 * m + 1, chunks, stride=per_chunk), :],
                )
                for m in range(CHUNK // 128)
            ],
            axis=1,
        )

    shape = (NP, 2 * NP)
    order = lax.broadcasted_iota(jnp.int32, shape, 0) == node_of(lane_ids(shape))
    wide[...] = jnp.dot(
        slots_ref[...].astype(F32),
        jnp.where(order, 1.0, 0.0),
        precision=HIGH,
        preferred_element_type=F32,
    )
    q_ids, lo_ids = split_slots((by_chunk() + 0.5).astype(jnp.int32))
    q_ref[...] = q_ids
    lo_ref[...] = lo_ids
    corner = lax.broadcasted_iota(jnp.int32, (elements, elements), 0) == lane_ids((elements, elements))
    wide[...] = jnp.dot(
        jnp.where(corner, jacobian_ref[...], 0.0),
        jnp.ones((elements, 128), F32),
        precision=HIGH,
        preferred_element_type=F32,
    )
    scale_ref[...] = by_chunk()
    for way, face_ref in enumerate((up_ref, down_ref)):
        q_ids, lo_ids = split_slots(face_ref[...])
        face_q_ref[way : way + 1, :] = q_ids
        face_lo_ref[way : way + 1, :] = lo_ids

    for w in range(elements // 2):
        window = values_ref[:, w * 128 : (w + 1) * 128].astype(F32)
        turned = pltpu.roll(window, 64, 1)
        table[2 * w] = jnp.where(lanes < 64, window, turned).astype(BF16)
        table[2 * w + 1] = jnp.where(lanes < 64, turned, window).astype(BF16)
    total[...] = jnp.zeros_like(total)
    fetch.wait()

    def lay_out(g, carry):
        rows = blocks_ref[pl.ds(pl.multiple_of(g * 16, 16), 16), :]
        for c in range(32):
            flat[pl.ds(g * 512 + c, 16, stride=32), :] = rows[:, c * 128 : (c + 1) * 128].astype(F32)
        return carry

    lax.fori_loop(0, pairs // 16, lay_out, 0)

    def multiply(step, carry):
        left, right = [], []
        for g in range(4):
            p = step * 4 + g
            left.append(table[source_ref[p]])
            block = flat[pl.ds(pl.multiple_of(p * 32, 32), 32), :]
            right.append(jnp.where(lanes < 64, block, 0.0).astype(BF16))
            right.append(jnp.where(lanes < 64, 0.0, block).astype(BF16))
        product = add_up(jnp.concatenate(left, axis=0), jnp.concatenate(right, axis=0))
        for g in range(4):
            part = product[g * TR : (g + 1) * TR, (g // 2) * 128 : (g // 2 + 1) * 128]
            keep = (lanes < 64) if g % 2 == 0 else (lanes >= 64)
            at = target_ref[step * 4 + g]
            total[at] = total[at] + jnp.where(keep, part, 0.0)
        return carry

    lax.fori_loop(0, pairs // 4, multiply, 0, unroll=8)

    def add(step, carry):
        tiles = []
        for m in range(CHUNK // 128):
            even = total[step * per_chunk + 2 * m]
            odd = total[step * per_chunk + 2 * m + 1]
            tiles.append(
                jnp.where(lanes < 64, even + pltpu.roll(even, 64, 1), odd + pltpu.roll(odd, 64, 1))
            )
        out_ref[step] = stacked(jnp.concatenate(tiles, axis=1))
        return carry

    lax.fori_loop(0, chunks, add, 0, unroll=2)


def exchange_kernel(
    n,
    sums_ref,
    lo_ref,
    q_ref,
    scale_ref,
    face_lo_ref,
    face_q_ref,
    right_ref,
    image_ref,
    gram_ref,
    table,
    mass,
    hot,
    face_hot,
    found,
    applied,
    ext,
    outgoing,
    incoming,
    near,
    far,
    send_sem,
    recv_sem,
    near_send,
    near_recv,
    far_send,
    far_recv,
):
    me = lax.axis_index("dom")
    group = min(GROUP, n)
    layers = n // group
    spot, layer = lax.rem(me, group), me // group
    has_up, has_down = me < n - 1, me > 0
    near_ids = [layer * group + lax.rem(spot + o, group) for o in range(1, group)]
    far_ids = [lax.rem(layer + o, layers) * group + spot for o in range(1, layers)]
    cross_up = jnp.logical_and(spot == group - 1, has_up)
    cross_down = jnp.logical_and(spot == 0, has_down)

    barrier = pltpu.get_barrier_semaphore()
    for other in near_ids + far_ids:
        pl.semaphore_signal(barrier, inc=1, device_id=(other,), device_id_type=MESH)

    @pl.when(cross_up)
    def _():
        pl.semaphore_signal(barrier, inc=1, device_id=(me + 1,), device_id_type=MESH)

    @pl.when(cross_down)
    def _():
        pl.semaphore_signal(barrier, inc=1, device_id=(me - 1,), device_id_type=MESH)

    def copy(source, phase, way):
        return pltpu.make_async_remote_copy(
            src_ref=source,
            dst_ref=incoming.at[phase, way],
            send_sem=send_sem.at[phase, way],
            recv_sem=recv_sem.at[phase, way],
            device_id=(me + (1 if way else -1),),
            device_id_type=MESH,
        )

    def start(source, phase, way):
        @pl.when(has_up if way else has_down)
        def _():
            copy(source, phase, way).start()

    def finish(source, phase, way):
        @pl.when(has_up if way else has_down)
        def _():
            copy(source, phase, way).wait_send()

    def arrive(source, phase, way):
        @pl.when(has_down if way else has_up)
        def _():
            copy(source, phase, way).wait_recv()

        @pl.when(jnp.logical_not(has_down if way else has_up))
        def _():
            incoming[phase, way] = jnp.zeros((FACE, LO), F32)

    down_rows = pl.ds(OWN, FACE)
    up_rows = pl.ds(OWN + FACE, FACE)
    own_blocks, face_blocks = range(Q_OWN), range(Q_OWN, Q_ALL)
    chunks = lo_ref.shape[0]
    ext[...] = jnp.zeros_like(ext)

    def fill(rows, value):
        first, second = pieces(value)
        for b in range(value.shape[0] // TR):
            at = (rows + b) * 2 * TR
            table[at : at + TR] = first[b * TR : (b + 1) * TR]
            table[at + TR : at + 2 * TR] = second[b * TR : (b + 1) * TR]

    def face_sums(step, carry):
        marks = one_hot(lo_ref[pl.ds(step, 1), :])
        hot[step] = marks
        ext[0, OWN:, :] += scatter(sums_ref[step], q_ref[pl.ds(step, 1), :], face_blocks, marks)
        return carry

    lax.fori_loop(0, chunks, face_sums, 0, unroll=2)
    partners = group + layers - 2
    crossing = jnp.logical_or(cross_up, cross_down)

    @pl.when(crossing)
    def _():
        pl.semaphore_wait(barrier, partners + 1)

    @pl.when(jnp.logical_not(crossing))
    def _():
        pl.semaphore_wait(barrier, partners)

    start(ext.at[0, down_rows], 0, 0)
    start(ext.at[0, up_rows], 0, 1)

    def own_sums(values, phase):
        def step_sums(step, carry):
            ext[phase, 0:OWN, :] += scatter(
                values[step], q_ref[pl.ds(step, 1), :], own_blocks, hot[step]
            )
            return carry

        lax.fori_loop(0, chunks, step_sums, 0, unroll=2)

    own_sums(sums_ref, 0)
    for way in range(2):
        face_hot[:, way * F : (way + 1) * F] = one_hot(face_lo_ref[way : way + 1, :])
    first, second = pieces(mass_block())
    mass[0] = first
    mass[1] = second

    def settle(own, phase):
        left = []
        for way in range(2):
            for b in range(Q_FACE):
                part = slice(b * LO, (b + 1) * LO)
                stack = stacked(incoming[phase, way, b * TR : (b + 1) * TR, :])
                left.append(spread(stack, face_q_ref[way : way + 1, part], own_blocks))
        return own + joined(add_up(jnp.concatenate(left, axis=1), face_hot[...]))

    arrive(ext.at[0, down_rows], 0, 0)
    arrive(ext.at[0, up_rows], 0, 1)
    right = settle(ext[0, 0:OWN, :], 0)
    fill(0, right)

    own_table, face_table = pl.ds(0, 2 * OWN), pl.ds(2 * OWN, 4 * FACE)
    for way in (1, 0):
        mine = slice((1 - way) * F, (2 - way) * F)
        values = gather(
            table[own_table, :], face_q_ref[1 - way : 2 - way, :], own_blocks, face_hot[:, mine]
        )
        for b in range(Q_FACE):
            outgoing[way, b * TR : (b + 1) * TR, :] = values[:, b * LO : (b + 1) * LO]
        start(outgoing.at[way], 1, way)

    def own_values(step, carry):
        q_row = q_ref[pl.ds(step, 1), :]
        found[step] = gather(table[own_table, :], q_row, own_blocks, hot[step])
        return carry

    lax.fori_loop(0, chunks, own_values, 0, unroll=2)
    for q in own_blocks:
        right_ref[:, q * LO : (q + 1) * LO] = right[q * TR : (q + 1) * TR]
    for way in (1, 0):
        arrive(outgoing.at[way], 1, way)
        fill(Q_OWN if way else Q_OWN + Q_FACE, incoming[1, way])

    def elements(step, carry):
        q_row = q_ref[pl.ds(step, 1), :]
        values = found[step] + gather(table[face_table, :], q_row, face_blocks, hot[step])
        first, second = pieces(
            jnp.concatenate([values[:, h : h + 256] for h in range(0, CHUNK, 256)], axis=0)
        )
        result = (
            jnp.dot(first, mass[0], preferred_element_type=F32)
            + jnp.dot(second, mass[0], preferred_element_type=F32)
            + jnp.dot(first, mass[1], preferred_element_type=F32)
        )
        result = jnp.concatenate(
            [result[h * TR : (h + 1) * TR] for h in range(CHUNK // 256)], axis=1
        )
        stack = stacked(result * scale_ref[pl.ds(step, 1), :])
        applied[step] = stack
        ext[1, OWN:, :] += scatter(stack, q_row, face_blocks, hot[step])
        return carry

    lax.fori_loop(0, chunks, elements, 0, unroll=2)
    start(ext.at[1, down_rows], 2, 0)
    start(ext.at[1, up_rows], 2, 1)
    own_sums(applied, 1)
    arrive(ext.at[1, down_rows], 2, 0)
    arrive(ext.at[1, up_rows], 2, 1)
    image = settle(ext[1, 0:OWN, :], 2)
    for q in own_blocks:
        image_ref[:, q * LO : (q + 1) * LO] = image[q * TR : (q + 1) * TR]

    stack = jnp.concatenate(
        [
            jnp.concatenate([table[q * 2 * TR : (q + 1) * 2 * TR, :] for q in own_blocks], axis=1),
            jnp.concatenate(
                [stacked(image[q * TR : (q + 1) * TR]) for q in own_blocks], axis=1
            ),
        ],
        axis=0,
    )
    products = add_up(stack, stack)
    lanes = lane_ids((TR, 128))
    upper = products[0:TR] + products[TR : 2 * TR]
    lower = products[2 * TR : 3 * TR] + products[3 * TR :]
    upper = upper + pltpu.roll(upper, 96, 1)
    lower = pltpu.roll(lower + pltpu.roll(lower, 96, 1), 96, 1)
    gram = jnp.where(jnp.logical_and(lanes >= TR, lanes < 2 * TR), lower, upper)

    def sum_over(value, buffer, others, sends, recvs):
        buffer[0] = value

        def part(o, other):
            return pltpu.make_async_remote_copy(
                src_ref=buffer.at[0],
                dst_ref=buffer.at[o],
                send_sem=sends.at[o],
                recv_sem=recvs.at[o],
                device_id=(other,),
                device_id_type=MESH,
            )

        for o, other in enumerate(others, 1):
            part(o, other).start()
        for o, other in enumerate(others, 1):
            part(o, other).wait_recv()
            value = value + buffer[o]
        for o, other in enumerate(others, 1):
            part(o, other).wait_send()
        return value

    gram = sum_over(gram, near, near_ids, near_send, near_recv)
    gram_ref[...] = sum_over(gram, far, far_ids, far_send, far_recv)

    finish(ext.at[0, down_rows], 0, 0)
    finish(ext.at[0, up_rows], 0, 1)
    for way in range(2):
        finish(outgoing.at[way], 1, way)
    finish(ext.at[1, down_rows], 2, 0)
    finish(ext.at[1, up_rows], 2, 1)


def output_kernel(gram_ref, right_ref, image_ref, solution_ref, residual_ref, basis_ref):
    def dot(a, b):
        return jnp.dot(a, b, precision=HIGH, preferred_element_type=F32)

    rows = lax.broadcasted_iota(jnp.int32, (TR, 128), 0)
    lanes = lane_ids((TR, 128))
    work = gram_ref[...]
    gram = work[:, 0:TR]
    for j in range(0, TR, 2):
        c = 2 * TR + j
        a, b = work[j : j + 1, :], work[j + 1 : j + 2, :]
        inverse = 1.0 / a[:, c : c + 1]
        across = a[:, c + 1 : c + 2] * inverse
        b = b - (b[:, c : c + 1] * inverse) * a
        b = b * (1.0 / b[:, c + 1 : c + 2])
        a = a * inverse - across * b
        rest = work - work[:, c : c + 1] * a - work[:, c + 1 : c + 2] * b
        work = jnp.where(rows == j, a, jnp.where(rows == j + 1, b, rest))
    step_t = work[:, 0:TR]
    step = step_t.T
    image_part = work[:, TR : 2 * TR]
    new_gram = dot(gram, dot(image_part, step_t)) - gram

    def times(small):
        first, second = pieces(small)
        both = jnp.concatenate([first, second], axis=0)

        def apply(value):
            top, rest = pieces(value)
            found = jnp.dot(both, top, preferred_element_type=F32)
            return (
                found[0:TR] + found[TR : 2 * TR] + jnp.dot(first, rest, preferred_element_type=F32)
            )

        return apply

    parts = [slice(at, at + 3 * LO) for at in range(0, Q_OWN * LO, 3 * LO)]
    apply_step = times(step)
    for part in parts:
        right = right_ref[:, part]
        solution_ref[:, part] = apply_step(right)
        residual_ref[:, part] = right - apply_step(image_ref[:, part])

    work = jnp.concatenate([new_gram, jnp.zeros((TR, 128 - TR), F32)], axis=1)
    work = jnp.where(lanes == rows + TR, 1.0, work)
    scale = jnp.zeros((TR, 128), F32)
    for j in range(0, TR, 2):
        a, b = work[j : j + 1, :], work[j + 1 : j + 2, :]
        pivot, across = a[:, j : j + 1], a[:, j + 1 : j + 2]
        inverse = 1.0 / pivot
        b = b - (b[:, j : j + 1] * inverse) * a
        second_pivot = b[:, j + 1 : j + 2]
        factor = work[:, j : j + 1] * inverse
        second = (work[:, j + 1 : j + 2] - factor * across) * (1.0 / second_pivot)
        rest = work - factor * a - second * b
        work = jnp.where(rows > j + 1, rest, jnp.where(rows == j + 1, b, work))
        scale = jnp.where(rows == j, lax.rsqrt(pivot), scale)
        scale = jnp.where(rows == j + 1, lax.rsqrt(second_pivot), scale)
    apply_lower = times((work * scale)[:, TR : 2 * TR])
    for part in parts:
        basis_ref[:, part] = apply_lower(residual_ref[:, part])


def per_device(
    n, connectivity, send_down, send_up, jacobian, pair_blocks, pair_target, pair_source, source_values
):
    elements = connectivity.shape[0]
    pairs = pair_target.shape[0]
    chunks = elements * NP // CHUNK
    vmem = pl.BlockSpec(memory_space=pltpu.VMEM)
    smem = pl.BlockSpec(memory_space=pltpu.SMEM)

    ids = jax.ShapeDtypeStruct((chunks, CHUNK), jnp.int32)
    face_ids = jax.ShapeDtypeStruct((2, F), jnp.int32)
    prepared = pl.pallas_call(
        pair_kernel,
        out_shape=(
            jax.ShapeDtypeStruct((chunks, 2 * TR, CHUNK), BF16),
            ids,
            ids,
            jax.ShapeDtypeStruct((chunks, CHUNK), F32),
            face_ids,
            face_ids,
        ),
        in_specs=[smem, smem, pl.BlockSpec(memory_space=pl.ANY)] + [vmem] * 5,
        out_specs=(vmem,) * 6,
        scratch_shapes=[
            pltpu.VMEM(pair_blocks.shape, BF16),
            pltpu.VMEM((pairs * 32, 128), F32),
            pltpu.VMEM((elements, TR, 128), BF16),
            pltpu.VMEM((elements, TR, 128), F32),
            pltpu.VMEM((elements, 128), F32),
            pltpu.SemaphoreType.DMA,
        ],
        compiler_params=pltpu.CompilerParams(vmem_limit_bytes=61 * 2**20),
        name="pair_stage",
    )(
        pair_target,
        pair_source,
        pair_blocks,
        source_values,
        connectivity,
        jacobian.reshape(1, elements),
        send_up,
        send_down,
    )

    group = min(GROUP, n)
    layers = n // group
    field = jax.ShapeDtypeStruct((TR, NODE_DEV), F32)
    right, image, gram = pl.pallas_call(
        functools.partial(exchange_kernel, n),
        out_shape=(field, field, jax.ShapeDtypeStruct((TR, 128), F32)),
        in_specs=[vmem] * 6,
        out_specs=(vmem, vmem, vmem),
        scratch_shapes=[
            pltpu.VMEM((Q_ALL * 2 * TR, LO), BF16),
            pltpu.VMEM((2, 4 * NP, 4 * NP), BF16),
            pltpu.VMEM((chunks, LO, CHUNK), BF16),
            pltpu.VMEM((LO, 2 * F), BF16),
            pltpu.VMEM((chunks, TR, CHUNK), F32),
            pltpu.VMEM((chunks, 2 * TR, CHUNK), BF16),
            pltpu.VMEM((2, Q_ALL * TR, LO), F32),
            pltpu.VMEM((2, FACE, LO), F32),
            pltpu.VMEM((3, 2, FACE, LO), F32),
            pltpu.VMEM((group, TR, 128), F32),
            pltpu.VMEM((layers, TR, 128), F32),
            pltpu.SemaphoreType.DMA((3, 2)),
            pltpu.SemaphoreType.DMA((3, 2)),
            pltpu.SemaphoreType.DMA((group,)),
            pltpu.SemaphoreType.DMA((group,)),
            pltpu.SemaphoreType.DMA((layers,)),
            pltpu.SemaphoreType.DMA((layers,)),
        ],
        compiler_params=pltpu.CompilerParams(
            collective_id=0, has_side_effects=True, vmem_limit_bytes=48 * 2**20
        ),
        name="exchange_stage",
    )(*prepared)

    out = jax.ShapeDtypeStruct((TR, NODE_DEV), F32)
    return pl.pallas_call(
        output_kernel,
        out_shape=(out, out, out),
        in_specs=[vmem] * 3,
        out_specs=(vmem, vmem, vmem),
        compiler_params=pltpu.CompilerParams(vmem_limit_bytes=32 * 2**20),
        name="output_stage",
    )(gram, right, image)


def solution(mesh):
    return jax.shard_map(
        functools.partial(per_device, mesh.shape["dom"]),
        mesh=mesh,
        in_specs=(
            P("dom", None),
            P("dom", None),
            P("dom", None),
            P("dom"),
            P("dom", None),
            P("dom"),
            P("dom"),
            P(None, "dom"),
        ),
        out_specs=(P(None, "dom"), P(None, "dom"), P(None, "dom")),
        check_vma=False,
    )
```

```python
import functools

import jax
import jax.numpy as jnp
from jax import lax
from jax.experimental import pallas as pl
from jax.experimental.pallas import tpu as pltpu
from jax.sharding import PartitionSpec as P

TR = 32
NP = 64
NODE_DEV = 3456
F = 768
LO = 384
Q_OWN = NODE_DEV // LO
Q_FACE = F // LO
Q_ALL = Q_OWN + 2 * Q_FACE
OWN = Q_OWN * TR
FACE = Q_FACE * TR
CHUNK = 512
GROUP = 8
MESH = pl.DeviceIdType.MESH
HIGH = lax.Precision.HIGHEST
F32 = jnp.float32
BF16 = jnp.bfloat16
NT = (((1,), (1,)), ((), ()))


def line_entry(a, b):
    apart = jnp.abs(a - b)
    inner = jnp.logical_or(a == 1, a == 2)
    near = jnp.where(a + b == 3, -81.0, 99.0)
    far = jnp.where(apart == 2, -36.0, 19.0)
    return jnp.where(apart == 0, jnp.where(inner, 648.0, 128.0), jnp.where(apart == 1, near, far))


def node_of(position):
    return jnp.bitwise_and(position, 31) * 2 + jnp.bitwise_and(jnp.right_shift(position, 5), 1)


def mass_block():
    shape = (4 * NP, 4 * NP)
    rows, columns = lax.broadcasted_iota(jnp.int32, shape, 0), lane_ids(shape)
    first, second = node_of(rows), node_of(columns)
    value = jnp.where(jnp.right_shift(rows, 6) == jnp.right_shift(columns, 6), 504.0**-3, 0.0)
    for digit in (0, 2, 4):
        value = value * line_entry(
            jnp.bitwise_and(jnp.right_shift(first, digit), 3),
            jnp.bitwise_and(jnp.right_shift(second, digit), 3),
        )
    return value


def lane_ids(shape):
    return lax.broadcasted_iota(jnp.int32, shape, len(shape) - 1)


def pieces(value):
    first = value.astype(BF16)
    return first, (value - first.astype(F32)).astype(BF16)


def one_hot(lo_row):
    width = lo_row.shape[1]
    rows = lax.broadcasted_iota(jnp.int32, (LO, width), 0)
    return jnp.where(rows == lo_row, 1.0, 0.0).astype(BF16)


def stacked(value):
    return jnp.concatenate(pieces(value), axis=0)


def spread(stack, q_row, blocks):
    return jnp.concatenate(
        [stack * jnp.where(q_row == q, 1.0, 0.0).astype(BF16) for q in blocks], axis=0
    )


def add_up(left, right):
    return lax.dot_general(left, right, NT, preferred_element_type=F32)


def joined(value):
    return jnp.concatenate(
        [
            value[at : at + TR] + value[at + TR : at + 2 * TR]
            for at in range(0, value.shape[0], 2 * TR)
        ],
        axis=0,
    )


def scatter(stack, q_row, blocks, hot):
    return joined(add_up(spread(stack, q_row, blocks), hot))


def gather(table, first_tile, tiles, q_row, lo_row):
    tile_row = q_row * (LO // 128) + jnp.right_shift(lo_row, 7)
    lane_row = jnp.bitwise_and(lo_row, 127)
    columns = []
    for at in range(0, q_row.shape[1], 128):
        tile = jnp.broadcast_to(tile_row[:, at : at + 128], (TR, 128))
        lane = jnp.broadcast_to(lane_row[:, at : at + 128], (TR, 128))
        total = jnp.zeros((TR, 128), F32)
        for t in range(first_tile, first_tile + tiles):
            here = jnp.take_along_axis(table[t * TR : (t + 1) * TR, :], lane, axis=1)
            total = jnp.where(tile == t, here, total)
        columns.append(total)
    return jnp.concatenate(columns, axis=1)


def split_slots(slots):
    q = jnp.right_shift(jnp.right_shift(slots, 7) * 43, 7)
    return q, slots - q * LO


def pair_kernel(
    target_ref,
    source_ref,
    blocks_hbm,
    values_ref,
    slots_ref,
    jacobian_ref,
    up_ref,
    down_ref,
    out_ref,
    lo_ref,
    q_ref,
    scale_ref,
    face_lo_ref,
    face_q_ref,
    blocks_ref,
    flat,
    table,
    total,
    wide,
    blocks_sem,
):
    pairs = blocks_ref.shape[0]
    elements = total.shape[0]
    chunks = lo_ref.shape[0]
    per_chunk = CHUNK // NP
    lanes = lane_ids((TR, 128))

    fetch = pltpu.make_async_copy(blocks_hbm, blocks_ref, blocks_sem)
    fetch.start()

    def by_chunk():
        left_half = lane_ids((chunks, 128)) < 64
        return jnp.concatenate(
            [
                jnp.where(
                    left_half,
                    wide[pl.ds(2 * m, chunks, stride=per_chunk), :],
                    wide[pl.ds(2 * m + 1, chunks, stride=per_chunk), :],
                )
                for m in range(CHUNK // 128)
            ],
            axis=1,
        )

    shape = (NP, 2 * NP)
    order = lax.broadcasted_iota(jnp.int32, shape, 0) == node_of(lane_ids(shape))
    wide[...] = lax.dot_general(
        slots_ref[...].astype(F32),
        jnp.where(order, 1.0, 0.0),
        (((0,), (0,)), ((), ())),
        precision=HIGH,
        preferred_element_type=F32,
    )
    q_ids, lo_ids = split_slots((by_chunk() + 0.5).astype(jnp.int32))
    q_ref[...] = q_ids
    lo_ref[...] = lo_ids
    corner = lax.broadcasted_iota(jnp.int32, (elements, elements), 0) == lane_ids((elements, elements))
    wide[...] = jnp.dot(
        jnp.where(corner, jacobian_ref[...], 0.0),
        jnp.ones((elements, 128), F32),
        precision=HIGH,
        preferred_element_type=F32,
    )
    scale_ref[...] = by_chunk()
    for way, face_ref in enumerate((up_ref, down_ref)):
        q_ids, lo_ids = split_slots(face_ref[...])
        face_q_ref[way : way + 1, :] = q_ids
        face_lo_ref[way : way + 1, :] = lo_ids

    for w in range(elements // 2):
        window = values_ref[:, w * 128 : (w + 1) * 128].astype(F32)
        turned = pltpu.roll(window, 64, 1)
        table[2 * w] = jnp.where(lanes < 64, window, turned).astype(BF16)
        table[2 * w + 1] = jnp.where(lanes < 64, turned, window).astype(BF16)
    total[...] = jnp.zeros_like(total)
    fetch.wait()

    def lay_out(g, carry):
        rows = blocks_ref[pl.ds(pl.multiple_of(g * 16, 16), 16), :]
        for c in range(32):
            flat[pl.ds(g * 512 + c, 16, stride=32), :] = rows[:, c * 128 : (c + 1) * 128].astype(F32)
        return carry

    lax.fori_loop(0, pairs // 16, lay_out, 0)

    def multiply(step, carry):
        left, right = [], []
        for g in range(4):
            p = step * 4 + g
            left.append(table[source_ref[p]])
            block = flat[pl.ds(pl.multiple_of(p * 32, 32), 32), :]
            right.append(jnp.where(lanes < 64, block, 0.0).astype(BF16))
            right.append(jnp.where(lanes < 64, 0.0, block).astype(BF16))
        product = add_up(jnp.concatenate(left, axis=0), jnp.concatenate(right, axis=0))
        for g in range(4):
            part = product[g * TR : (g + 1) * TR, (g // 2) * 128 : (g // 2 + 1) * 128]
            keep = (lanes < 64) if g % 2 == 0 else (lanes >= 64)
            at = target_ref[step * 4 + g]
            total[at] = total[at] + jnp.where(keep, part, 0.0)
        return carry

    lax.fori_loop(0, pairs // 4, multiply, 0, unroll=8)

    def add(step, carry):
        tiles = []
        for m in range(CHUNK // 128):
            even = total[step * per_chunk + 2 * m]
            odd = total[step * per_chunk + 2 * m + 1]
            tiles.append(
                jnp.where(lanes < 64, even + pltpu.roll(even, 64, 1), odd + pltpu.roll(odd, 64, 1))
            )
        out_ref[step] = stacked(jnp.concatenate(tiles, axis=1))
        return carry

    lax.fori_loop(0, chunks, add, 0, unroll=2)


def exchange_kernel(
    n,
    sums_ref,
    lo_ref,
    q_ref,
    scale_ref,
    face_lo_ref,
    face_q_ref,
    right_ref,
    image_ref,
    gram_ref,
    table,
    mass,
    hot,
    face_hot,
    found,
    applied,
    ext,
    outgoing,
    incoming,
    near,
    far,
    send_sem,
    recv_sem,
    near_send,
    near_recv,
    far_send,
    far_recv,
):
    me = lax.axis_index("dom")
    group = min(GROUP, n)
    layers = n // group
    spot, layer = lax.rem(me, group), me // group
    has_up, has_down = me < n - 1, me > 0
    near_ids = [layer * group + lax.rem(spot + o, group) for o in range(1, group)]
    far_ids = [lax.rem(layer + o, layers) * group + spot for o in range(1, layers)]
    cross_up = jnp.logical_and(spot == group - 1, has_up)
    cross_down = jnp.logical_and(spot == 0, has_down)

    barrier = pltpu.get_barrier_semaphore()
    for other in near_ids + far_ids:
        pl.semaphore_signal(barrier, inc=1, device_id=(other,), device_id_type=MESH)

    @pl.when(cross_up)
    def _():
        pl.semaphore_signal(barrier, inc=1, device_id=(me + 1,), device_id_type=MESH)

    @pl.when(cross_down)
    def _():
        pl.semaphore_signal(barrier, inc=1, device_id=(me - 1,), device_id_type=MESH)

    def copy(source, phase, way):
        return pltpu.make_async_remote_copy(
            src_ref=source,
            dst_ref=incoming.at[phase, way],
            send_sem=send_sem.at[phase, way],
            recv_sem=recv_sem.at[phase, way],
            device_id=(me + (1 if way else -1),),
            device_id_type=MESH,
        )

    def start(source, phase, way):
        @pl.when(has_up if way else has_down)
        def _():
            copy(source, phase, way).start()

    def finish(source, phase, way):
        @pl.when(has_up if way else has_down)
        def _():
            copy(source, phase, way).wait_send()

    def arrive(source, phase, way):
        @pl.when(has_down if way else has_up)
        def _():
            copy(source, phase, way).wait_recv()

        @pl.when(jnp.logical_not(has_down if way else has_up))
        def _():
            incoming[phase, way] = jnp.zeros((FACE, LO), F32)

    down_rows = pl.ds(OWN, FACE)
    up_rows = pl.ds(OWN + FACE, FACE)
    own_blocks, face_blocks = range(Q_OWN), range(Q_OWN, Q_ALL)
    chunks = lo_ref.shape[0]
    ext[...] = jnp.zeros_like(ext)

    def fill(block, value):
        for b in range(value.shape[0] // TR):
            for part in range(LO // 128):
                at = ((block + b) * (LO // 128) + part) * TR
                table[at : at + TR, :] = value[
                    b * TR : (b + 1) * TR, part * 128 : (part + 1) * 128
                ]

    def face_sums(step, carry):
        marks = one_hot(lo_ref[pl.ds(step, 1), :])
        hot[step] = marks
        ext[0, OWN:, :] += scatter(sums_ref[step], q_ref[pl.ds(step, 1), :], face_blocks, marks)
        return carry

    lax.fori_loop(0, chunks, face_sums, 0, unroll=2)
    partners = group + layers - 2
    crossing = jnp.logical_or(cross_up, cross_down)

    @pl.when(crossing)
    def _():
        pl.semaphore_wait(barrier, partners + 1)

    @pl.when(jnp.logical_not(crossing))
    def _():
        pl.semaphore_wait(barrier, partners)

    start(ext.at[0, down_rows], 0, 0)
    start(ext.at[0, up_rows], 0, 1)

    def own_sums(values, phase):
        def step_sums(step, carry):
            ext[phase, 0:OWN, :] += scatter(
                values[step], q_ref[pl.ds(step, 1), :], own_blocks, hot[step]
            )
            return carry

        lax.fori_loop(0, chunks, step_sums, 0, unroll=2)

    own_sums(sums_ref, 0)
    for way in range(2):
        face_hot[:, way * F : (way + 1) * F] = one_hot(face_lo_ref[way : way + 1, :])
    first, second = pieces(mass_block())
    mass[0] = first
    mass[1] = second

    def settle(own, phase):
        left = []
        for way in range(2):
            for b in range(Q_FACE):
                part = slice(b * LO, (b + 1) * LO)
                stack = stacked(incoming[phase, way, b * TR : (b + 1) * TR, :])
                left.append(spread(stack, face_q_ref[way : way + 1, part], own_blocks))
        return own + joined(add_up(jnp.concatenate(left, axis=1), face_hot[...]))

    arrive(ext.at[0, down_rows], 0, 0)
    arrive(ext.at[0, up_rows], 0, 1)
    right = settle(ext[0, 0:OWN, :], 0)
    fill(0, right)

    own_tiles, face_tiles = Q_OWN * LO // 128, 2 * F // 128
    for way in (1, 0):
        mine = slice(1 - way, 2 - way)
        values = gather(table, 0, own_tiles, face_q_ref[mine, :], face_lo_ref[mine, :])
        for b in range(Q_FACE):
            outgoing[way, b * TR : (b + 1) * TR, :] = values[:, b * LO : (b + 1) * LO]
        start(outgoing.at[way], 1, way)

    def own_values(step, carry):
        q_row, lo_row = q_ref[pl.ds(step, 1), :], lo_ref[pl.ds(step, 1), :]
        found[step] = gather(table, 0, own_tiles, q_row, lo_row)
        return carry

    lax.fori_loop(0, chunks, own_values, 0)
    for q in own_blocks:
        right_ref[:, q * LO : (q + 1) * LO] = right[q * TR : (q + 1) * TR]
    for way in (1, 0):
        arrive(outgoing.at[way], 1, way)
        fill(Q_OWN if way else Q_OWN + Q_FACE, incoming[1, way])

    def elements(step, carry):
        q_row = q_ref[pl.ds(step, 1), :]
        lo_row = lo_ref[pl.ds(step, 1), :]
        values = found[step] + gather(table, own_tiles, face_tiles, q_row, lo_row)
        first, second = pieces(
            jnp.concatenate([values[:, h : h + 256] for h in range(0, CHUNK, 256)], axis=0)
        )
        result = (
            jnp.dot(first, mass[0], preferred_element_type=F32)
            + jnp.dot(second, mass[0], preferred_element_type=F32)
            + jnp.dot(first, mass[1], preferred_element_type=F32)
        )
        result = jnp.concatenate(
            [result[h * TR : (h + 1) * TR] for h in range(CHUNK // 256)], axis=1
        )
        stack = stacked(result * scale_ref[pl.ds(step, 1), :])
        applied[step] = stack
        ext[1, OWN:, :] += scatter(stack, q_row, face_blocks, hot[step])
        return carry

    lax.fori_loop(0, chunks, elements, 0, unroll=2)
    start(ext.at[1, down_rows], 2, 0)
    start(ext.at[1, up_rows], 2, 1)
    own_sums(applied, 1)
    arrive(ext.at[1, down_rows], 2, 0)
    arrive(ext.at[1, up_rows], 2, 1)
    image = settle(ext[1, 0:OWN, :], 2)
    for q in own_blocks:
        image_ref[:, q * LO : (q + 1) * LO] = image[q * TR : (q + 1) * TR]

    stack = jnp.concatenate(
        [
            jnp.concatenate(
                [stacked(field[q * TR : (q + 1) * TR]) for q in own_blocks], axis=1
            )
            for field in (right, image)
        ],
        axis=0,
    )
    products = add_up(stack, stack)
    lanes = lane_ids((TR, 128))
    upper = products[0:TR] + products[TR : 2 * TR]
    lower = products[2 * TR : 3 * TR] + products[3 * TR :]
    upper = upper + pltpu.roll(upper, 96, 1)
    lower = pltpu.roll(lower + pltpu.roll(lower, 96, 1), 96, 1)
    gram = jnp.where(jnp.logical_and(lanes >= TR, lanes < 2 * TR), lower, upper)

    def sum_over(value, buffer, others, sends, recvs):
        buffer[0] = value

        def part(o, other):
            return pltpu.make_async_remote_copy(
                src_ref=buffer.at[0],
                dst_ref=buffer.at[o],
                send_sem=sends.at[o],
                recv_sem=recvs.at[o],
                device_id=(other,),
                device_id_type=MESH,
            )

        for o, other in enumerate(others, 1):
            part(o, other).start()
        for o, other in enumerate(others, 1):
            part(o, other).wait_recv()
            value = value + buffer[o]
        for o, other in enumerate(others, 1):
            part(o, other).wait_send()
        return value

    gram = sum_over(gram, near, near_ids, near_send, near_recv)
    gram_ref[...] = sum_over(gram, far, far_ids, far_send, far_recv)

    finish(ext.at[0, down_rows], 0, 0)
    finish(ext.at[0, up_rows], 0, 1)
    for way in range(2):
        finish(outgoing.at[way], 1, way)
    finish(ext.at[1, down_rows], 2, 0)
    finish(ext.at[1, up_rows], 2, 1)


def output_kernel(gram_ref, right_ref, image_ref, solution_ref, residual_ref, basis_ref):
    def dot(a, b):
        return jnp.dot(a, b, precision=HIGH, preferred_element_type=F32)

    rows = lax.broadcasted_iota(jnp.int32, (TR, 128), 0)
    lanes = lane_ids((TR, 128))
    work = gram_ref[...]
    gram = work[:, 0:TR]
    for j in range(0, TR, 2):
        c = 2 * TR + j
        a, b = work[j : j + 1, :], work[j + 1 : j + 2, :]
        inverse = 1.0 / a[:, c : c + 1]
        across = a[:, c + 1 : c + 2] * inverse
        b = b - (b[:, c : c + 1] * inverse) * a
        b = b * (1.0 / b[:, c + 1 : c + 2])
        a = a * inverse - across * b
        rest = work - work[:, c : c + 1] * a - work[:, c + 1 : c + 2] * b
        work = jnp.where(rows == j, a, jnp.where(rows == j + 1, b, rest))
    step_t = work[:, 0:TR]
    step = step_t.T
    image_part = work[:, TR : 2 * TR]
    new_gram = dot(gram, dot(image_part, step_t)) - gram

    def times(small):
        first, second = pieces(small)
        both = jnp.concatenate([first, second], axis=0)

        def apply(value):
            top, rest = pieces(value)
            found = jnp.dot(both, top, preferred_element_type=F32)
            return (
                found[0:TR] + found[TR : 2 * TR] + jnp.dot(first, rest, preferred_element_type=F32)
            )

        return apply

    parts = [slice(at, at + 3 * LO) for at in range(0, Q_OWN * LO, 3 * LO)]
    apply_step = times(step)
    for part in parts:
        right = right_ref[:, part]
        solution_ref[:, part] = apply_step(right)
        residual_ref[:, part] = right - apply_step(image_ref[:, part])

    work = jnp.concatenate([new_gram, jnp.zeros((TR, 128 - TR), F32)], axis=1)
    work = jnp.where(lanes == rows + TR, 1.0, work)
    scale = jnp.zeros((TR, 128), F32)
    for j in range(0, TR, 2):
        a, b = work[j : j + 1, :], work[j + 1 : j + 2, :]
        pivot, across = a[:, j : j + 1], a[:, j + 1 : j + 2]
        inverse = 1.0 / pivot
        b = b - (b[:, j : j + 1] * inverse) * a
        second_pivot = b[:, j + 1 : j + 2]
        factor = work[:, j : j + 1] * inverse
        second = (work[:, j + 1 : j + 2] - factor * across) * (1.0 / second_pivot)
        rest = work - factor * a - second * b
        work = jnp.where(rows > j + 1, rest, jnp.where(rows == j + 1, b, work))
        scale = jnp.where(rows == j, lax.rsqrt(pivot), scale)
        scale = jnp.where(rows == j + 1, lax.rsqrt(second_pivot), scale)
    apply_lower = times((work * scale)[:, TR : 2 * TR])
    for part in parts:
        basis_ref[:, part] = apply_lower(residual_ref[:, part])


def per_device(
    n, connectivity, send_down, send_up, jacobian, pair_blocks, pair_target, pair_source, source_values
):
    elements = connectivity.shape[0]
    pairs = pair_target.shape[0]
    chunks = elements * NP // CHUNK
    vmem = pl.BlockSpec(memory_space=pltpu.VMEM)
    smem = pl.BlockSpec(memory_space=pltpu.SMEM)

    ids = jax.ShapeDtypeStruct((chunks, CHUNK), jnp.int32)
    face_ids = jax.ShapeDtypeStruct((2, F), jnp.int32)
    prepared = pl.pallas_call(
        pair_kernel,
        out_shape=(
            jax.ShapeDtypeStruct((chunks, 2 * TR, CHUNK), BF16),
            ids,
            ids,
            jax.ShapeDtypeStruct((chunks, CHUNK), F32),
            face_ids,
            face_ids,
        ),
        in_specs=[smem, smem, pl.BlockSpec(memory_space=pl.ANY)] + [vmem] * 5,
        out_specs=(vmem,) * 6,
        scratch_shapes=[
            pltpu.VMEM(pair_blocks.shape, BF16),
            pltpu.VMEM((pairs * 32, 128), F32),
            pltpu.VMEM((elements, TR, 128), BF16),
            pltpu.VMEM((elements, TR, 128), F32),
            pltpu.VMEM((elements, 128), F32),
            pltpu.SemaphoreType.DMA,
        ],
        compiler_params=pltpu.CompilerParams(vmem_limit_bytes=61 * 2**20),
        name="pair_stage",
    )(
        pair_target,
        pair_source,
        pair_blocks,
        source_values,
        connectivity.T,
        jacobian.reshape(1, elements),
        send_up,
        send_down,
    )

    group = min(GROUP, n)
    layers = n // group
    field = jax.ShapeDtypeStruct((TR, NODE_DEV), F32)
    right, image, gram = pl.pallas_call(
        functools.partial(exchange_kernel, n),
        out_shape=(field, field, jax.ShapeDtypeStruct((TR, 128), F32)),
        in_specs=[vmem] * 6,
        out_specs=(vmem, vmem, vmem),
        scratch_shapes=[
            pltpu.VMEM((Q_ALL * (LO // 128) * TR, 128), F32),
            pltpu.VMEM((2, 4 * NP, 4 * NP), BF16),
            pltpu.VMEM((chunks, LO, CHUNK), BF16),
            pltpu.VMEM((LO, 2 * F), BF16),
            pltpu.VMEM((chunks, TR, CHUNK), F32),
            pltpu.VMEM((chunks, 2 * TR, CHUNK), BF16),
            pltpu.VMEM((2, Q_ALL * TR, LO), F32),
            pltpu.VMEM((2, FACE, LO), F32),
            pltpu.VMEM((3, 2, FACE, LO), F32),
            pltpu.VMEM((group, TR, 128), F32),
            pltpu.VMEM((layers, TR, 128), F32),
            pltpu.SemaphoreType.DMA((3, 2)),
            pltpu.SemaphoreType.DMA((3, 2)),
            pltpu.SemaphoreType.DMA((group,)),
            pltpu.SemaphoreType.DMA((group,)),
            pltpu.SemaphoreType.DMA((layers,)),
            pltpu.SemaphoreType.DMA((layers,)),
        ],
        compiler_params=pltpu.CompilerParams(
            collective_id=0, has_side_effects=True, vmem_limit_bytes=61 * 2**20
        ),
        name="exchange_stage",
    )(*prepared)

    out = jax.ShapeDtypeStruct((TR, NODE_DEV), F32)
    return pl.pallas_call(
        output_kernel,
        out_shape=(out, out, out),
        in_specs=[vmem] * 3,
        out_specs=(vmem, vmem, vmem),
        compiler_params=pltpu.CompilerParams(vmem_limit_bytes=61 * 2**20),
        name="output_stage",
    )(gram, right, image)


def solution(mesh):
    return jax.shard_map(
        functools.partial(per_device, mesh.shape["dom"]),
        mesh=mesh,
        in_specs=(
            P("dom", None),
            P("dom", None),
            P("dom", None),
            P("dom"),
            P("dom", None),
            P("dom"),
            P("dom"),
            P(None, "dom"),
        ),
        out_specs=(P(None, "dom"), P(None, "dom"), P(None, "dom")),
        check_vma=False,
    )
```

```python
import functools

import jax
import jax.numpy as jnp
from jax import lax
from jax.experimental import pallas as pl
from jax.experimental.pallas import tpu as pltpu
from jax.sharding import PartitionSpec as P

TR = 32
NP = 64
NODE_DEV = 3456
F = 768
LO = 384
Q_OWN = NODE_DEV // LO
Q_FACE = F // LO
Q_ALL = Q_OWN + 2 * Q_FACE
OWN = Q_OWN * TR
FACE = Q_FACE * TR
CHUNK = 512
Q_PRODUCT = 5
GROUP = 8
MESH = pl.DeviceIdType.MESH
HIGH = lax.Precision.HIGHEST
F32 = jnp.float32
BF16 = jnp.bfloat16
NT = (((1,), (1,)), ((), ()))


def line_entry(a, b):
    apart = jnp.abs(a - b)
    inner = jnp.logical_or(a == 1, a == 2)
    near = jnp.where(a + b == 3, -81.0, 99.0)
    far = jnp.where(apart == 2, -36.0, 19.0)
    return jnp.where(apart == 0, jnp.where(inner, 648.0, 128.0), jnp.where(apart == 1, near, far))


def node_of(position):
    return jnp.bitwise_and(position, 31) * 2 + jnp.bitwise_and(jnp.right_shift(position, 5), 1)


def mass_block():
    shape = (4 * NP, 4 * NP)
    rows, columns = lax.broadcasted_iota(jnp.int32, shape, 0), lane_ids(shape)
    first, second = node_of(rows), node_of(columns)
    value = jnp.where(jnp.right_shift(rows, 6) == jnp.right_shift(columns, 6), 504.0**-3, 0.0)
    for digit in (0, 2, 4):
        value = value * line_entry(
            jnp.bitwise_and(jnp.right_shift(first, digit), 3),
            jnp.bitwise_and(jnp.right_shift(second, digit), 3),
        )
    return value


def lane_ids(shape):
    return lax.broadcasted_iota(jnp.int32, shape, len(shape) - 1)


def pieces(value):
    first = value.astype(BF16)
    return first, (value - first.astype(F32)).astype(BF16)


def one_hot(lo_row):
    width = lo_row.shape[1]
    rows = lax.broadcasted_iota(jnp.int32, (LO, width), 0)
    return jnp.where(rows == lo_row, 1.0, 0.0).astype(BF16)


def stacked(value):
    return jnp.concatenate(pieces(value), axis=0)


def spread(stack, q_row, blocks):
    return jnp.concatenate(
        [stack * jnp.where(q_row == q, 1.0, 0.0).astype(BF16) for q in blocks], axis=0
    )


def add_up(left, right):
    return lax.dot_general(left, right, NT, preferred_element_type=F32)


def joined(value):
    return jnp.concatenate(
        [
            value[at : at + TR] + value[at + TR : at + 2 * TR]
            for at in range(0, value.shape[0], 2 * TR)
        ],
        axis=0,
    )


def scatter(stack, q_row, blocks, hot):
    return joined(add_up(spread(stack, q_row, blocks), hot))


def gather(table, first_tile, tiles, q_row, lo_row):
    tile_row = q_row * (LO // 128) + jnp.right_shift(lo_row, 7)
    lane_row = jnp.bitwise_and(lo_row, 127)
    columns = []
    for at in range(0, q_row.shape[1], 128):
        tile = jnp.broadcast_to(tile_row[:, at : at + 128], (TR, 128))
        lane = jnp.broadcast_to(lane_row[:, at : at + 128], (TR, 128))
        total = jnp.zeros((TR, 128), F32)
        for t in range(first_tile, first_tile + tiles):
            here = jnp.take_along_axis(table[t * TR : (t + 1) * TR, :], lane, axis=1)
            total = jnp.where(tile == t, here, total)
        columns.append(total)
    return jnp.concatenate(columns, axis=1)


def gather_product(table, blocks, q_row, hot):
    found = jnp.dot(table, hot, preferred_element_type=F32)
    total = None
    for at, q in enumerate(blocks):
        rows = found[2 * at * TR : (2 * at + 2) * TR]
        part = jnp.where(q_row == q, rows[0:TR] + rows[TR:], 0.0)
        total = part if total is None else total + part
    return total


def split_slots(slots):
    q = jnp.right_shift(jnp.right_shift(slots, 7) * 43, 7)
    return q, slots - q * LO


def pair_kernel(
    target_ref,
    source_ref,
    blocks_hbm,
    values_ref,
    slots_ref,
    jacobian_ref,
    up_ref,
    down_ref,
    out_ref,
    lo_ref,
    q_ref,
    scale_ref,
    face_lo_ref,
    face_q_ref,
    blocks_ref,
    flat,
    table,
    total,
    wide,
    blocks_sem,
):
    pairs = blocks_ref.shape[0]
    elements = total.shape[0]
    chunks = lo_ref.shape[0]
    per_chunk = CHUNK // NP
    lanes = lane_ids((TR, 128))

    fetch = pltpu.make_async_copy(blocks_hbm, blocks_ref, blocks_sem)
    fetch.start()

    def by_chunk():
        left_half = lane_ids((chunks, 128)) < 64
        return jnp.concatenate(
            [
                jnp.where(
                    left_half,
                    wide[pl.ds(2 * m, chunks, stride=per_chunk), :],
                    wide[pl.ds(2 * m + 1, chunks, stride=per_chunk), :],
                )
                for m in range(CHUNK // 128)
            ],
            axis=1,
        )

    shape = (NP, 2 * NP)
    order = lax.broadcasted_iota(jnp.int32, shape, 0) == node_of(lane_ids(shape))
    wide[...] = lax.dot_general(
        slots_ref[...].astype(F32),
        jnp.where(order, 1.0, 0.0),
        (((0,), (0,)), ((), ())),
        precision=HIGH,
        preferred_element_type=F32,
    )
    q_ids, lo_ids = split_slots((by_chunk() + 0.5).astype(jnp.int32))
    q_ref[...] = q_ids
    lo_ref[...] = lo_ids
    corner = lax.broadcasted_iota(jnp.int32, (elements, elements), 0) == lane_ids((elements, elements))
    wide[...] = jnp.dot(
        jnp.where(corner, jacobian_ref[...], 0.0),
        jnp.ones((elements, 128), F32),
        precision=HIGH,
        preferred_element_type=F32,
    )
    scale_ref[...] = by_chunk()
    for way, face_ref in enumerate((up_ref, down_ref)):
        q_ids, lo_ids = split_slots(face_ref[...])
        face_q_ref[way : way + 1, :] = q_ids
        face_lo_ref[way : way + 1, :] = lo_ids

    for w in range(elements // 2):
        window = values_ref[:, w * 128 : (w + 1) * 128].astype(F32)
        turned = pltpu.roll(window, 64, 1)
        table[2 * w] = jnp.where(lanes < 64, window, turned).astype(BF16)
        table[2 * w + 1] = jnp.where(lanes < 64, turned, window).astype(BF16)
    total[...] = jnp.zeros_like(total)
    fetch.wait()

    def lay_out(g, carry):
        rows = blocks_ref[pl.ds(pl.multiple_of(g * 16, 16), 16), :]
        for c in range(32):
            flat[pl.ds(g * 512 + c, 16, stride=32), :] = rows[:, c * 128 : (c + 1) * 128].astype(F32)
        return carry

    lax.fori_loop(0, pairs // 16, lay_out, 0)

    def multiply(step, carry):
        left, right = [], []
        for g in range(4):
            p = step * 4 + g
            left.append(table[source_ref[p]])
            block = flat[pl.ds(pl.multiple_of(p * 32, 32), 32), :]
            right.append(jnp.where(lanes < 64, block, 0.0).astype(BF16))
            right.append(jnp.where(lanes < 64, 0.0, block).astype(BF16))
        product = add_up(jnp.concatenate(left, axis=0), jnp.concatenate(right, axis=0))
        for g in range(4):
            part = product[g * TR : (g + 1) * TR, (g // 2) * 128 : (g // 2 + 1) * 128]
            keep = (lanes < 64) if g % 2 == 0 else (lanes >= 64)
            at = target_ref[step * 4 + g]
            total[at] = total[at] + jnp.where(keep, part, 0.0)
        return carry

    lax.fori_loop(0, pairs // 4, multiply, 0, unroll=8)

    def add(step, carry):
        tiles = []
        for m in range(CHUNK // 128):
            even = total[step * per_chunk + 2 * m]
            odd = total[step * per_chunk + 2 * m + 1]
            tiles.append(
                jnp.where(lanes < 64, even + pltpu.roll(even, 64, 1), odd + pltpu.roll(odd, 64, 1))
            )
        out_ref[step] = stacked(jnp.concatenate(tiles, axis=1))
        return carry

    lax.fori_loop(0, chunks, add, 0, unroll=2)


def exchange_kernel(
    n,
    sums_ref,
    lo_ref,
    q_ref,
    scale_ref,
    face_lo_ref,
    face_q_ref,
    right_ref,
    image_ref,
    gram_ref,
    table,
    split_table,
    mass,
    hot,
    face_hot,
    found,
    applied,
    ext,
    outgoing,
    incoming,
    near,
    far,
    send_sem,
    recv_sem,
    near_send,
    near_recv,
    far_send,
    far_recv,
):
    me = lax.axis_index("dom")
    group = min(GROUP, n)
    layers = n // group
    spot, layer = lax.rem(me, group), me // group
    has_up, has_down = me < n - 1, me > 0
    near_ids = [layer * group + lax.rem(spot + o, group) for o in range(1, group)]
    far_ids = [lax.rem(layer + o, layers) * group + spot for o in range(1, layers)]
    cross_up = jnp.logical_and(spot == group - 1, has_up)
    cross_down = jnp.logical_and(spot == 0, has_down)

    barrier = pltpu.get_barrier_semaphore()
    for other in near_ids + far_ids:
        pl.semaphore_signal(barrier, inc=1, device_id=(other,), device_id_type=MESH)

    @pl.when(cross_up)
    def _():
        pl.semaphore_signal(barrier, inc=1, device_id=(me + 1,), device_id_type=MESH)

    @pl.when(cross_down)
    def _():
        pl.semaphore_signal(barrier, inc=1, device_id=(me - 1,), device_id_type=MESH)

    def copy(source, phase, way):
        return pltpu.make_async_remote_copy(
            src_ref=source,
            dst_ref=incoming.at[phase, way],
            send_sem=send_sem.at[phase, way],
            recv_sem=recv_sem.at[phase, way],
            device_id=(me + (1 if way else -1),),
            device_id_type=MESH,
        )

    def start(source, phase, way):
        @pl.when(has_up if way else has_down)
        def _():
            copy(source, phase, way).start()

    def finish(source, phase, way):
        @pl.when(has_up if way else has_down)
        def _():
            copy(source, phase, way).wait_send()

    def arrive(source, phase, way):
        @pl.when(has_down if way else has_up)
        def _():
            copy(source, phase, way).wait_recv()

        @pl.when(jnp.logical_not(has_down if way else has_up))
        def _():
            incoming[phase, way] = jnp.zeros((FACE, LO), F32)

    down_rows = pl.ds(OWN, FACE)
    up_rows = pl.ds(OWN + FACE, FACE)
    own_blocks, face_blocks = range(Q_OWN), range(Q_OWN, Q_ALL)
    chunks = lo_ref.shape[0]
    ext[...] = jnp.zeros_like(ext)

    def fill(block, value):
        for b in range(value.shape[0] // TR):
            for part in range(LO // 128):
                at = ((block + b) * (LO // 128) + part) * TR
                table[at : at + TR, :] = value[
                    b * TR : (b + 1) * TR, part * 128 : (part + 1) * 128
                ]
            if block + b < Q_PRODUCT:
                split_table[(block + b) * 2 * TR : (block + b + 1) * 2 * TR, :] = stacked(
                    value[b * TR : (b + 1) * TR]
                )

    def face_sums(step, carry):
        marks = one_hot(lo_ref[pl.ds(step, 1), :])
        hot[step] = marks
        ext[0, OWN:, :] += scatter(sums_ref[step], q_ref[pl.ds(step, 1), :], face_blocks, marks)
        return carry

    lax.fori_loop(0, chunks, face_sums, 0, unroll=2)
    partners = group + layers - 2
    crossing = jnp.logical_or(cross_up, cross_down)

    @pl.when(crossing)
    def _():
        pl.semaphore_wait(barrier, partners + 1)

    @pl.when(jnp.logical_not(crossing))
    def _():
        pl.semaphore_wait(barrier, partners)

    start(ext.at[0, down_rows], 0, 0)
    start(ext.at[0, up_rows], 0, 1)

    def own_sums(values, phase):
        def step_sums(step, carry):
            ext[phase, 0:OWN, :] += scatter(
                values[step], q_ref[pl.ds(step, 1), :], own_blocks, hot[step]
            )
            return carry

        lax.fori_loop(0, chunks, step_sums, 0, unroll=2)

    own_sums(sums_ref, 0)
    for way in range(2):
        face_hot[:, way * F : (way + 1) * F] = one_hot(face_lo_ref[way : way + 1, :])
    first, second = pieces(mass_block())
    mass[0] = first
    mass[1] = second

    def settle(own, phase):
        left = []
        for way in range(2):
            for b in range(Q_FACE):
                part = slice(b * LO, (b + 1) * LO)
                stack = stacked(incoming[phase, way, b * TR : (b + 1) * TR, :])
                left.append(spread(stack, face_q_ref[way : way + 1, part], own_blocks))
        return own + joined(add_up(jnp.concatenate(left, axis=1), face_hot[...]))

    arrive(ext.at[0, down_rows], 0, 0)
    arrive(ext.at[0, up_rows], 0, 1)
    right = settle(ext[0, 0:OWN, :], 0)
    fill(0, right)

    own_tiles, face_tiles = Q_OWN * LO // 128, 2 * F // 128
    first_tile = Q_PRODUCT * LO // 128

    def own_gather(q_row, lo_row, marks):
        return gather(table, first_tile, own_tiles - first_tile, q_row, lo_row) + gather_product(
            split_table[...], range(Q_PRODUCT), q_row, marks
        )

    for way in (1, 0):
        mine = slice(1 - way, 2 - way)
        values = own_gather(
            face_q_ref[mine, :], face_lo_ref[mine, :], face_hot[:, (1 - way) * F : (2 - way) * F]
        )
        for b in range(Q_FACE):
            outgoing[way, b * TR : (b + 1) * TR, :] = values[:, b * LO : (b + 1) * LO]
        start(outgoing.at[way], 1, way)

    def own_values(step, carry):
        q_row, lo_row = q_ref[pl.ds(step, 1), :], lo_ref[pl.ds(step, 1), :]
        found[step] = own_gather(q_row, lo_row, hot[step])
        return carry

    lax.fori_loop(0, chunks, own_values, 0, unroll=2)
    for q in own_blocks:
        right_ref[:, q * LO : (q + 1) * LO] = right[q * TR : (q + 1) * TR]
    for way in (1, 0):
        arrive(outgoing.at[way], 1, way)
        fill(Q_OWN if way else Q_OWN + Q_FACE, incoming[1, way])

    def face_values(step):
        q_row, lo_row = q_ref[pl.ds(step, 1), :], lo_ref[pl.ds(step, 1), :]
        return gather(table, own_tiles, face_tiles, q_row, lo_row)

    def elements(step, from_faces):
        q_row = q_ref[pl.ds(step, 1), :]
        values = found[step] + from_faces
        following = face_values(jnp.minimum(step + 1, chunks - 1))
        first, second = pieces(
            jnp.concatenate([values[:, h : h + 256] for h in range(0, CHUNK, 256)], axis=0)
        )
        result = (
            jnp.dot(first, mass[0], preferred_element_type=F32)
            + jnp.dot(second, mass[0], preferred_element_type=F32)
            + jnp.dot(first, mass[1], preferred_element_type=F32)
        )
        result = jnp.concatenate(
            [result[h * TR : (h + 1) * TR] for h in range(CHUNK // 256)], axis=1
        )
        stack = stacked(result * scale_ref[pl.ds(step, 1), :])
        applied[step] = stack
        ext[1, OWN:, :] += scatter(stack, q_row, face_blocks, hot[step])
        return following

    lax.fori_loop(0, chunks, elements, face_values(0), unroll=2)
    start(ext.at[1, down_rows], 2, 0)
    start(ext.at[1, up_rows], 2, 1)
    own_sums(applied, 1)
    arrive(ext.at[1, down_rows], 2, 0)
    arrive(ext.at[1, up_rows], 2, 1)
    image = settle(ext[1, 0:OWN, :], 2)
    for q in own_blocks:
        image_ref[:, q * LO : (q + 1) * LO] = image[q * TR : (q + 1) * TR]

    stack = jnp.concatenate(
        [
            jnp.concatenate(
                [stacked(field[q * TR : (q + 1) * TR]) for q in own_blocks], axis=1
            )
            for field in (right, image)
        ],
        axis=0,
    )
    products = add_up(stack, stack)
    lanes = lane_ids((TR, 128))
    upper = products[0:TR] + products[TR : 2 * TR]
    lower = products[2 * TR : 3 * TR] + products[3 * TR :]
    upper = upper + pltpu.roll(upper, 96, 1)
    lower = pltpu.roll(lower + pltpu.roll(lower, 96, 1), 96, 1)
    gram = jnp.where(jnp.logical_and(lanes >= TR, lanes < 2 * TR), lower, upper)

    def sum_over(value, buffer, others, sends, recvs):
        buffer[0] = value

        def part(o, other):
            return pltpu.make_async_remote_copy(
                src_ref=buffer.at[0],
                dst_ref=buffer.at[o],
                send_sem=sends.at[o],
                recv_sem=recvs.at[o],
                device_id=(other,),
                device_id_type=MESH,
            )

        for o, other in enumerate(others, 1):
            part(o, other).start()
        for o, other in enumerate(others, 1):
            part(o, other).wait_recv()
            value = value + buffer[o]
        for o, other in enumerate(others, 1):
            part(o, other).wait_send()
        return value

    gram = sum_over(gram, near, near_ids, near_send, near_recv)
    gram_ref[...] = sum_over(gram, far, far_ids, far_send, far_recv)

    finish(ext.at[0, down_rows], 0, 0)
    finish(ext.at[0, up_rows], 0, 1)
    for way in range(2):
        finish(outgoing.at[way], 1, way)
    finish(ext.at[1, down_rows], 2, 0)
    finish(ext.at[1, up_rows], 2, 1)


def output_kernel(
    gram_ref,
    right_ref,
    image_ref,
    solution_out,
    residual_out,
    basis_out,
    solution_ref,
    residual_ref,
    basis_ref,
    sems,
):
    def dot(a, b):
        return jnp.dot(a, b, precision=HIGH, preferred_element_type=F32)

    rows = lax.broadcasted_iota(jnp.int32, (TR, 128), 0)
    lanes = lane_ids((TR, 128))
    work = gram_ref[...]
    gram = work[:, 0:TR]
    for j in range(0, TR, 2):
        c = 2 * TR + j
        a, b = work[j : j + 1, :], work[j + 1 : j + 2, :]
        inverse = 1.0 / a[:, c : c + 1]
        across = a[:, c + 1 : c + 2] * inverse
        b = b - (b[:, c : c + 1] * inverse) * a
        b = b * (1.0 / b[:, c + 1 : c + 2])
        a = a * inverse - across * b
        rest = work - work[:, c : c + 1] * a - work[:, c + 1 : c + 2] * b
        work = jnp.where(rows == j, a, jnp.where(rows == j + 1, b, rest))
    step_t = work[:, 0:TR]
    step = step_t.T
    image_part = work[:, TR : 2 * TR]
    new_gram = dot(gram, dot(image_part, step_t)) - gram

    def times(small):
        first, second = pieces(small)
        both = jnp.concatenate([first, second], axis=0)

        def apply(value):
            top, rest = pieces(value)
            found = jnp.dot(both, top, preferred_element_type=F32)
            return (
                found[0:TR] + found[TR : 2 * TR] + jnp.dot(first, rest, preferred_element_type=F32)
            )

        return apply

    parts = [slice(at, at + 3 * LO) for at in range(0, Q_OWN * LO, 3 * LO)]
    apply_step = times(step)
    for part in parts:
        right = right_ref[:, part]
        solution_ref[:, part] = apply_step(right)
        residual_ref[:, part] = right - apply_step(image_ref[:, part])
    copies = [
        pltpu.make_async_copy(solution_ref, solution_out, sems.at[0]),
        pltpu.make_async_copy(residual_ref, residual_out, sems.at[1]),
        pltpu.make_async_copy(basis_ref, basis_out, sems.at[2]),
    ]
    copies[0].start()
    copies[1].start()

    work = jnp.concatenate([new_gram, jnp.zeros((TR, 128 - TR), F32)], axis=1)
    work = jnp.where(lanes == rows + TR, 1.0, work)
    scale = jnp.zeros((TR, 128), F32)
    for j in range(0, TR, 2):
        a, b = work[j : j + 1, :], work[j + 1 : j + 2, :]
        pivot, across = a[:, j : j + 1], a[:, j + 1 : j + 2]
        inverse = 1.0 / pivot
        b = b - (b[:, j : j + 1] * inverse) * a
        second_pivot = b[:, j + 1 : j + 2]
        factor = work[:, j : j + 1] * inverse
        second = (work[:, j + 1 : j + 2] - factor * across) * (1.0 / second_pivot)
        rest = work - factor * a - second * b
        work = jnp.where(rows > j + 1, rest, jnp.where(rows == j + 1, b, work))
        scale = jnp.where(rows == j, lax.rsqrt(pivot), scale)
        scale = jnp.where(rows == j + 1, lax.rsqrt(second_pivot), scale)
    apply_lower = times((work * scale)[:, TR : 2 * TR])
    for part in parts:
        basis_ref[:, part] = apply_lower(residual_ref[:, part])
    copies[2].start()
    for copy in copies:
        copy.wait()


def per_device(
    n, connectivity, send_down, send_up, jacobian, pair_blocks, pair_target, pair_source, source_values
):
    elements = connectivity.shape[0]
    pairs = pair_target.shape[0]
    chunks = elements * NP // CHUNK
    vmem = pl.BlockSpec(memory_space=pltpu.VMEM)
    smem = pl.BlockSpec(memory_space=pltpu.SMEM)

    ids = jax.ShapeDtypeStruct((chunks, CHUNK), jnp.int32)
    face_ids = jax.ShapeDtypeStruct((2, F), jnp.int32)
    prepared = pl.pallas_call(
        pair_kernel,
        out_shape=(
            jax.ShapeDtypeStruct((chunks, 2 * TR, CHUNK), BF16),
            ids,
            ids,
            jax.ShapeDtypeStruct((chunks, CHUNK), F32),
            face_ids,
            face_ids,
        ),
        in_specs=[smem, smem, pl.BlockSpec(memory_space=pl.ANY)] + [vmem] * 5,
        out_specs=(vmem,) * 6,
        scratch_shapes=[
            pltpu.VMEM(pair_blocks.shape, BF16),
            pltpu.VMEM((pairs * 32, 128), F32),
            pltpu.VMEM((elements, TR, 128), BF16),
            pltpu.VMEM((elements, TR, 128), F32),
            pltpu.VMEM((elements, 128), F32),
            pltpu.SemaphoreType.DMA,
        ],
        compiler_params=pltpu.CompilerParams(vmem_limit_bytes=61 * 2**20),
        name="pair_stage",
    )(
        pair_target,
        pair_source,
        pair_blocks,
        source_values,
        connectivity.T,
        jacobian.reshape(1, elements),
        send_up,
        send_down,
    )

    group = min(GROUP, n)
    layers = n // group
    field = jax.ShapeDtypeStruct((TR, NODE_DEV), F32)
    right, image, gram = pl.pallas_call(
        functools.partial(exchange_kernel, n),
        out_shape=(field, field, jax.ShapeDtypeStruct((TR, 128), F32)),
        in_specs=[vmem] * 6,
        out_specs=(vmem, vmem, vmem),
        scratch_shapes=[
            pltpu.VMEM((Q_ALL * (LO // 128) * TR, 128), F32),
            pltpu.VMEM((Q_PRODUCT * 2 * TR, LO), BF16),
            pltpu.VMEM((2, 4 * NP, 4 * NP), BF16),
            pltpu.VMEM((chunks, LO, CHUNK), BF16),
            pltpu.VMEM((LO, 2 * F), BF16),
            pltpu.VMEM((chunks, TR, CHUNK), F32),
            pltpu.VMEM((chunks, 2 * TR, CHUNK), BF16),
            pltpu.VMEM((2, Q_ALL * TR, LO), F32),
            pltpu.VMEM((2, FACE, LO), F32),
            pltpu.VMEM((3, 2, FACE, LO), F32),
            pltpu.VMEM((group, TR, 128), F32),
            pltpu.VMEM((layers, TR, 128), F32),
            pltpu.SemaphoreType.DMA((3, 2)),
            pltpu.SemaphoreType.DMA((3, 2)),
            pltpu.SemaphoreType.DMA((group,)),
            pltpu.SemaphoreType.DMA((group,)),
            pltpu.SemaphoreType.DMA((layers,)),
            pltpu.SemaphoreType.DMA((layers,)),
        ],
        compiler_params=pltpu.CompilerParams(
            collective_id=0, has_side_effects=True, vmem_limit_bytes=61 * 2**20
        ),
        name="exchange_stage",
    )(*prepared)

    out = jax.ShapeDtypeStruct((TR, NODE_DEV), F32)
    return pl.pallas_call(
        output_kernel,
        out_shape=(out, out, out),
        in_specs=[vmem] * 3,
        out_specs=(pl.BlockSpec(memory_space=pl.ANY),) * 3,
        scratch_shapes=[pltpu.VMEM((TR, NODE_DEV), F32)] * 3 + [pltpu.SemaphoreType.DMA((3,))],
        compiler_params=pltpu.CompilerParams(vmem_limit_bytes=61 * 2**20),
        name="output_stage",
    )(gram, right, image)


def solution(mesh):
    return jax.shard_map(
        functools.partial(per_device, mesh.shape["dom"]),
        mesh=mesh,
        in_specs=(
            P("dom", None),
            P("dom", None),
            P("dom", None),
            P("dom"),
            P("dom", None),
            P("dom"),
            P("dom"),
            P(None, "dom"),
        ),
        out_specs=(P(None, "dom"), P(None, "dom"), P(None, "dom")),
        check_vma=False,
    )
```

```python
import functools

import jax
import jax.numpy as jnp
from jax import lax
from jax.experimental import pallas as pl
from jax.experimental.pallas import tpu as pltpu
from jax.sharding import PartitionSpec as P

TR = 32
NP = 64
NODE_DEV = 3456
F = 768
LO = 256
Q_OWN = -(-NODE_DEV // LO)
Q_FACE = F // LO
Q_ALL = Q_OWN + 2 * Q_FACE
OWN = Q_OWN * TR
FACE = Q_FACE * TR
CHUNK = 512
Q_PRODUCT = 7
GROUP = 8
MESH = pl.DeviceIdType.MESH
HIGH = lax.Precision.HIGHEST
F32 = jnp.float32
BF16 = jnp.bfloat16
NT = (((1,), (1,)), ((), ()))


def line_entry(a, b):
    apart = jnp.abs(a - b)
    inner = jnp.logical_or(a == 1, a == 2)
    near = jnp.where(a + b == 3, -81.0, 99.0)
    far = jnp.where(apart == 2, -36.0, 19.0)
    return jnp.where(apart == 0, jnp.where(inner, 648.0, 128.0), jnp.where(apart == 1, near, far))


def node_of(position):
    return jnp.bitwise_and(position, 31) * 2 + jnp.bitwise_and(jnp.right_shift(position, 5), 1)


def mass_block():
    shape = (4 * NP, 4 * NP)
    rows, columns = lax.broadcasted_iota(jnp.int32, shape, 0), lane_ids(shape)
    first, second = node_of(rows), node_of(columns)
    value = jnp.where(jnp.right_shift(rows, 6) == jnp.right_shift(columns, 6), 504.0**-3, 0.0)
    for digit in (0, 2, 4):
        value = value * line_entry(
            jnp.bitwise_and(jnp.right_shift(first, digit), 3),
            jnp.bitwise_and(jnp.right_shift(second, digit), 3),
        )
    return value


def lane_ids(shape):
    return lax.broadcasted_iota(jnp.int32, shape, len(shape) - 1)


def pieces(value):
    first = value.astype(BF16)
    return first, (value - first.astype(F32)).astype(BF16)


def one_hot(lo_row):
    width = lo_row.shape[1]
    rows = lax.broadcasted_iota(jnp.int32, (LO, width), 0)
    return jnp.where(rows == lo_row, 1.0, 0.0).astype(BF16)


def stacked(value):
    return jnp.concatenate(pieces(value), axis=0)


def spread(stack, q_row, blocks):
    return jnp.concatenate(
        [stack * jnp.where(q_row == q, 1.0, 0.0).astype(BF16) for q in blocks], axis=0
    )


def add_up(left, right):
    return lax.dot_general(left, right, NT, preferred_element_type=F32)


def joined(value):
    return jnp.concatenate(
        [
            value[at : at + TR] + value[at + TR : at + 2 * TR]
            for at in range(0, value.shape[0], 2 * TR)
        ],
        axis=0,
    )


def scatter(stack, q_row, blocks, hot):
    return joined(add_up(spread(stack, q_row, blocks), hot))


def gather(table, first_tile, tiles, q_row, lo_row):
    tile_row = q_row * (LO // 128) + jnp.right_shift(lo_row, 7)
    lane_row = jnp.bitwise_and(lo_row, 127)
    columns = []
    for at in range(0, q_row.shape[1], 128):
        tile = jnp.broadcast_to(tile_row[:, at : at + 128], (TR, 128))
        lane = jnp.broadcast_to(lane_row[:, at : at + 128], (TR, 128))
        total = jnp.zeros((TR, 128), F32)
        for t in range(first_tile, first_tile + tiles):
            here = jnp.take_along_axis(table[t * TR : (t + 1) * TR, :], lane, axis=1)
            total = jnp.where(tile == t, here, total)
        columns.append(total)
    return jnp.concatenate(columns, axis=1)


def gather_product(table, blocks, q_row, hot):
    found = jnp.dot(table, hot, preferred_element_type=F32)
    total = None
    for at, q in enumerate(blocks):
        rows = found[2 * at * TR : (2 * at + 2) * TR]
        part = jnp.where(q_row == q, rows[0:TR] + rows[TR:], 0.0)
        total = part if total is None else total + part
    return total


def split_slots(slots):
    padded = jnp.where(slots < NODE_DEV, slots, slots + (Q_OWN * LO - NODE_DEV))
    return jnp.right_shift(padded, 8), jnp.bitwise_and(padded, LO - 1)


def pair_kernel(
    target_ref,
    source_ref,
    blocks_hbm,
    values_ref,
    slots_ref,
    jacobian_ref,
    up_ref,
    down_ref,
    out_ref,
    lo_ref,
    q_ref,
    scale_ref,
    face_lo_ref,
    face_q_ref,
    blocks_ref,
    flat,
    table,
    total,
    wide,
    blocks_sem,
):
    pairs = blocks_ref.shape[0]
    elements = total.shape[0]
    chunks = lo_ref.shape[0]
    per_chunk = CHUNK // NP
    lanes = lane_ids((TR, 128))

    fetch = pltpu.make_async_copy(blocks_hbm, blocks_ref, blocks_sem)
    fetch.start()

    def by_chunk():
        left_half = lane_ids((chunks, 128)) < 64
        return jnp.concatenate(
            [
                jnp.where(
                    left_half,
                    wide[pl.ds(2 * m, chunks, stride=per_chunk), :],
                    wide[pl.ds(2 * m + 1, chunks, stride=per_chunk), :],
                )
                for m in range(CHUNK // 128)
            ],
            axis=1,
        )

    shape = (NP, 2 * NP)
    order = lax.broadcasted_iota(jnp.int32, shape, 0) == node_of(lane_ids(shape))
    wide[...] = lax.dot_general(
        slots_ref[...].astype(F32),
        jnp.where(order, 1.0, 0.0),
        (((0,), (0,)), ((), ())),
        precision=HIGH,
        preferred_element_type=F32,
    )
    q_ids, lo_ids = split_slots((by_chunk() + 0.5).astype(jnp.int32))
    q_ref[...] = q_ids
    lo_ref[...] = lo_ids
    corner = lax.broadcasted_iota(jnp.int32, (elements, elements), 0) == lane_ids((elements, elements))
    wide[...] = jnp.dot(
        jnp.where(corner, jacobian_ref[...], 0.0),
        jnp.ones((elements, 128), F32),
        precision=HIGH,
        preferred_element_type=F32,
    )
    scale_ref[...] = by_chunk()
    for way, face_ref in enumerate((up_ref, down_ref)):
        q_ids, lo_ids = split_slots(face_ref[...])
        face_q_ref[way : way + 1, :] = q_ids
        face_lo_ref[way : way + 1, :] = lo_ids

    for w in range(elements // 2):
        window = values_ref[:, w * 128 : (w + 1) * 128].astype(F32)
        turned = pltpu.roll(window, 64, 1)
        table[2 * w] = jnp.where(lanes < 64, window, turned).astype(BF16)
        table[2 * w + 1] = jnp.where(lanes < 64, turned, window).astype(BF16)
    total[...] = jnp.zeros_like(total)
    fetch.wait()

    def lay_out(g, carry):
        rows = blocks_ref[pl.ds(pl.multiple_of(g * 16, 16), 16), :]
        for c in range(32):
            flat[pl.ds(g * 512 + c, 16, stride=32), :] = rows[:, c * 128 : (c + 1) * 128].astype(F32)
        return carry

    lax.fori_loop(0, pairs // 16, lay_out, 0)

    def multiply(step, carry):
        left, right = [], []
        for g in range(4):
            p = step * 4 + g
            left.append(table[source_ref[p]])
            block = flat[pl.ds(pl.multiple_of(p * 32, 32), 32), :]
            right.append(jnp.where(lanes < 64, block, 0.0).astype(BF16))
            right.append(jnp.where(lanes < 64, 0.0, block).astype(BF16))
        product = add_up(jnp.concatenate(left, axis=0), jnp.concatenate(right, axis=0))
        for g in range(4):
            part = product[g * TR : (g + 1) * TR, (g // 2) * 128 : (g // 2 + 1) * 128]
            keep = (lanes < 64) if g % 2 == 0 else (lanes >= 64)
            at = target_ref[step * 4 + g]
            total[at] = total[at] + jnp.where(keep, part, 0.0)
        return carry

    lax.fori_loop(0, pairs // 4, multiply, 0, unroll=8)

    def add(step, carry):
        tiles = []
        for m in range(CHUNK // 128):
            even = total[step * per_chunk + 2 * m]
            odd = total[step * per_chunk + 2 * m + 1]
            tiles.append(
                jnp.where(lanes < 64, even + pltpu.roll(even, 64, 1), odd + pltpu.roll(odd, 64, 1))
            )
        out_ref[step] = stacked(jnp.concatenate(tiles, axis=1))
        return carry

    lax.fori_loop(0, chunks, add, 0, unroll=2)


def exchange_kernel(
    n,
    sums_ref,
    lo_ref,
    q_ref,
    scale_ref,
    face_lo_ref,
    face_q_ref,
    right_ref,
    image_ref,
    gram_ref,
    table,
    split_table,
    mass,
    hot,
    face_hot,
    found,
    applied,
    ext,
    outgoing,
    incoming,
    near,
    far,
    send_sem,
    recv_sem,
    near_send,
    near_recv,
    far_send,
    far_recv,
):
    me = lax.axis_index("dom")
    group = min(GROUP, n)
    layers = n // group
    spot, layer = lax.rem(me, group), me // group
    has_up, has_down = me < n - 1, me > 0
    near_ids = [layer * group + lax.rem(spot + o, group) for o in range(1, group)]
    far_ids = [lax.rem(layer + o, layers) * group + spot for o in range(1, layers)]
    cross_up = jnp.logical_and(spot == group - 1, has_up)
    cross_down = jnp.logical_and(spot == 0, has_down)

    barrier = pltpu.get_barrier_semaphore()
    for other in near_ids + far_ids:
        pl.semaphore_signal(barrier, inc=1, device_id=(other,), device_id_type=MESH)

    @pl.when(cross_up)
    def _():
        pl.semaphore_signal(barrier, inc=1, device_id=(me + 1,), device_id_type=MESH)

    @pl.when(cross_down)
    def _():
        pl.semaphore_signal(barrier, inc=1, device_id=(me - 1,), device_id_type=MESH)

    def copy(source, phase, way):
        return pltpu.make_async_remote_copy(
            src_ref=source,
            dst_ref=incoming.at[phase, way],
            send_sem=send_sem.at[phase, way],
            recv_sem=recv_sem.at[phase, way],
            device_id=(me + (1 if way else -1),),
            device_id_type=MESH,
        )

    def start(source, phase, way):
        @pl.when(has_up if way else has_down)
        def _():
            copy(source, phase, way).start()

    def finish(source, phase, way):
        @pl.when(has_up if way else has_down)
        def _():
            copy(source, phase, way).wait_send()

    def arrive(source, phase, way):
        @pl.when(has_down if way else has_up)
        def _():
            copy(source, phase, way).wait_recv()

        @pl.when(jnp.logical_not(has_down if way else has_up))
        def _():
            incoming[phase, way] = jnp.zeros((FACE, LO), F32)

    down_rows = pl.ds(OWN, FACE)
    up_rows = pl.ds(OWN + FACE, FACE)
    own_blocks, face_blocks = range(Q_OWN), range(Q_OWN, Q_ALL)
    chunks = lo_ref.shape[0]
    ext[...] = jnp.zeros_like(ext)

    def fill(block, value):
        for b in range(value.shape[0] // TR):
            for part in range(LO // 128):
                at = ((block + b) * (LO // 128) + part) * TR
                table[at : at + TR, :] = value[
                    b * TR : (b + 1) * TR, part * 128 : (part + 1) * 128
                ]
            if block + b < Q_PRODUCT:
                split_table[(block + b) * 2 * TR : (block + b + 1) * 2 * TR, :] = stacked(
                    value[b * TR : (b + 1) * TR]
                )

    def face_sums(step, carry):
        marks = one_hot(lo_ref[pl.ds(step, 1), :])
        hot[step] = marks
        ext[0, OWN:, :] += scatter(sums_ref[step], q_ref[pl.ds(step, 1), :], face_blocks, marks)
        return carry

    lax.fori_loop(0, chunks, face_sums, 0, unroll=2)
    partners = group + layers - 2
    crossing = jnp.logical_or(cross_up, cross_down)

    @pl.when(crossing)
    def _():
        pl.semaphore_wait(barrier, partners + 1)

    @pl.when(jnp.logical_not(crossing))
    def _():
        pl.semaphore_wait(barrier, partners)

    start(ext.at[0, down_rows], 0, 0)
    start(ext.at[0, up_rows], 0, 1)

    def own_sums(values, phase):
        def step_sums(step, carry):
            ext[phase, 0:OWN, :] += scatter(
                values[step], q_ref[pl.ds(step, 1), :], own_blocks, hot[step]
            )
            return carry

        lax.fori_loop(0, chunks, step_sums, 0, unroll=2)

    def write_out(ref, value):
        for q in own_blocks:
            end = min((q + 1) * LO, NODE_DEV)
            ref[:, q * LO : end] = value[q * TR : (q + 1) * TR, 0 : end - q * LO]

    own_sums(sums_ref, 0)
    for way in range(2):
        face_hot[:, way * F : (way + 1) * F] = one_hot(face_lo_ref[way : way + 1, :])
    first, second = pieces(mass_block())
    mass[0] = first
    mass[1] = second

    def settle(own, phase):
        left = []
        for way in range(2):
            for b in range(Q_FACE):
                part = slice(b * LO, (b + 1) * LO)
                stack = stacked(incoming[phase, way, b * TR : (b + 1) * TR, :])
                left.append(spread(stack, face_q_ref[way : way + 1, part], own_blocks))
        return own + joined(add_up(jnp.concatenate(left, axis=1), face_hot[...]))

    arrive(ext.at[0, down_rows], 0, 0)
    arrive(ext.at[0, up_rows], 0, 1)
    right = settle(ext[0, 0:OWN, :], 0)
    fill(0, right)

    own_tiles, face_tiles = NODE_DEV // 128, 2 * F // 128
    first_tile, first_face = Q_PRODUCT * LO // 128, Q_OWN * LO // 128

    def own_gather(q_row, lo_row, marks):
        return gather(table, first_tile, own_tiles - first_tile, q_row, lo_row) + gather_product(
            split_table[...], range(Q_PRODUCT), q_row, marks
        )

    for way in (1, 0):
        mine = slice(1 - way, 2 - way)
        values = own_gather(
            face_q_ref[mine, :], face_lo_ref[mine, :], face_hot[:, (1 - way) * F : (2 - way) * F]
        )
        for b in range(Q_FACE):
            outgoing[way, b * TR : (b + 1) * TR, :] = values[:, b * LO : (b + 1) * LO]
        start(outgoing.at[way], 1, way)

    def own_values(step, carry):
        q_row, lo_row = q_ref[pl.ds(step, 1), :], lo_ref[pl.ds(step, 1), :]
        found[step] = own_gather(q_row, lo_row, hot[step])
        return carry

    lax.fori_loop(0, chunks, own_values, 0, unroll=2)
    write_out(right_ref, right)
    for way in (1, 0):
        arrive(outgoing.at[way], 1, way)
        fill(Q_OWN if way else Q_OWN + Q_FACE, incoming[1, way])

    def face_values(step):
        q_row, lo_row = q_ref[pl.ds(step, 1), :], lo_ref[pl.ds(step, 1), :]
        return gather(table, first_face, face_tiles, q_row, lo_row)

    def elements(step, from_faces):
        q_row = q_ref[pl.ds(step, 1), :]
        values = found[step] + from_faces
        following = face_values(jnp.minimum(step + 1, chunks - 1))
        first, second = pieces(
            jnp.concatenate([values[:, h : h + 256] for h in range(0, CHUNK, 256)], axis=0)
        )
        result = (
            jnp.dot(first, mass[0], preferred_element_type=F32)
            + jnp.dot(second, mass[0], preferred_element_type=F32)
            + jnp.dot(first, mass[1], preferred_element_type=F32)
        )
        result = jnp.concatenate(
            [result[h * TR : (h + 1) * TR] for h in range(CHUNK // 256)], axis=1
        )
        stack = stacked(result * scale_ref[pl.ds(step, 1), :])
        applied[step] = stack
        ext[1, OWN:, :] += scatter(stack, q_row, face_blocks, hot[step])
        return following

    lax.fori_loop(0, chunks, elements, face_values(0), unroll=2)
    start(ext.at[1, down_rows], 2, 0)
    start(ext.at[1, up_rows], 2, 1)
    own_sums(applied, 1)
    arrive(ext.at[1, down_rows], 2, 0)
    arrive(ext.at[1, up_rows], 2, 1)
    image = settle(ext[1, 0:OWN, :], 2)
    write_out(image_ref, image)

    stack = jnp.concatenate(
        [
            jnp.concatenate(
                [stacked(field[q * TR : (q + 1) * TR]) for q in own_blocks], axis=1
            )
            for field in (right, image)
        ],
        axis=0,
    )
    products = add_up(stack, stack)
    lanes = lane_ids((TR, 128))
    upper = products[0:TR] + products[TR : 2 * TR]
    lower = products[2 * TR : 3 * TR] + products[3 * TR :]
    upper = upper + pltpu.roll(upper, 96, 1)
    lower = pltpu.roll(lower + pltpu.roll(lower, 96, 1), 96, 1)
    gram = jnp.where(jnp.logical_and(lanes >= TR, lanes < 2 * TR), lower, upper)

    def sum_over(value, buffer, others, sends, recvs):
        buffer[0] = value

        def part(o, other):
            return pltpu.make_async_remote_copy(
                src_ref=buffer.at[0],
                dst_ref=buffer.at[o],
                send_sem=sends.at[o],
                recv_sem=recvs.at[o],
                device_id=(other,),
                device_id_type=MESH,
            )

        for o, other in enumerate(others, 1):
            part(o, other).start()
        for o, other in enumerate(others, 1):
            part(o, other).wait_recv()
            value = value + buffer[o]
        for o, other in enumerate(others, 1):
            part(o, other).wait_send()
        return value

    gram = sum_over(gram, near, near_ids, near_send, near_recv)
    gram_ref[...] = sum_over(gram, far, far_ids, far_send, far_recv)

    finish(ext.at[0, down_rows], 0, 0)
    finish(ext.at[0, up_rows], 0, 1)
    for way in range(2):
        finish(outgoing.at[way], 1, way)
    finish(ext.at[1, down_rows], 2, 0)
    finish(ext.at[1, up_rows], 2, 1)


def output_kernel(
    gram_ref,
    right_ref,
    image_ref,
    solution_out,
    residual_out,
    basis_out,
    solution_ref,
    residual_ref,
    basis_ref,
    sems,
):
    def dot(a, b):
        return jnp.dot(a, b, precision=HIGH, preferred_element_type=F32)

    rows = lax.broadcasted_iota(jnp.int32, (TR, 128), 0)
    lanes = lane_ids((TR, 128))
    work = gram_ref[...]
    gram = work[:, 0:TR]
    for j in range(0, TR, 2):
        c = 2 * TR + j
        a, b = work[j : j + 1, :], work[j + 1 : j + 2, :]
        inverse = 1.0 / a[:, c : c + 1]
        across = a[:, c + 1 : c + 2] * inverse
        b = b - (b[:, c : c + 1] * inverse) * a
        b = b * (1.0 / b[:, c + 1 : c + 2])
        a = a * inverse - across * b
        rest = work - work[:, c : c + 1] * a - work[:, c + 1 : c + 2] * b
        work = jnp.where(rows == j, a, jnp.where(rows == j + 1, b, rest))
    step_t = work[:, 0:TR]
    step = step_t.T
    image_part = work[:, TR : 2 * TR]
    new_gram = dot(gram, dot(image_part, step_t)) - gram

    def times(small):
        first, second = pieces(small)
        both = jnp.concatenate([first, second], axis=0)

        def apply(value):
            top, rest = pieces(value)
            found = jnp.dot(both, top, preferred_element_type=F32)
            return (
                found[0:TR] + found[TR : 2 * TR] + jnp.dot(first, rest, preferred_element_type=F32)
            )

        return apply

    parts = [slice(at, at + NODE_DEV // 3) for at in range(0, NODE_DEV, NODE_DEV // 3)]
    apply_step = times(step)
    for part in parts:
        right = right_ref[:, part]
        solution_ref[:, part] = apply_step(right)
        residual_ref[:, part] = right - apply_step(image_ref[:, part])
    copies = [
        pltpu.make_async_copy(solution_ref, solution_out, sems.at[0]),
        pltpu.make_async_copy(residual_ref, residual_out, sems.at[1]),
        pltpu.make_async_copy(basis_ref, basis_out, sems.at[2]),
    ]
    copies[0].start()
    copies[1].start()

    work = jnp.concatenate([new_gram, jnp.zeros((TR, 128 - TR), F32)], axis=1)
    work = jnp.where(lanes == rows + TR, 1.0, work)
    scale = jnp.zeros((TR, 128), F32)
    for j in range(0, TR, 2):
        a, b = work[j : j + 1, :], work[j + 1 : j + 2, :]
        pivot, across = a[:, j : j + 1], a[:, j + 1 : j + 2]
        inverse = 1.0 / pivot
        b = b - (b[:, j : j + 1] * inverse) * a
        second_pivot = b[:, j + 1 : j + 2]
        factor = work[:, j : j + 1] * inverse
        second = (work[:, j + 1 : j + 2] - factor * across) * (1.0 / second_pivot)
        rest = work - factor * a - second * b
        work = jnp.where(rows > j + 1, rest, jnp.where(rows == j + 1, b, work))
        scale = jnp.where(rows == j, lax.rsqrt(pivot), scale)
        scale = jnp.where(rows == j + 1, lax.rsqrt(second_pivot), scale)
    apply_lower = times((work * scale)[:, TR : 2 * TR])
    for part in parts:
        basis_ref[:, part] = apply_lower(residual_ref[:, part])
    copies[2].start()
    for copy in copies:
        copy.wait()


def per_device(
    n, connectivity, send_down, send_up, jacobian, pair_blocks, pair_target, pair_source, source_values
):
    elements = connectivity.shape[0]
    pairs = pair_target.shape[0]
    chunks = elements * NP // CHUNK
    vmem = pl.BlockSpec(memory_space=pltpu.VMEM)
    smem = pl.BlockSpec(memory_space=pltpu.SMEM)

    ids = jax.ShapeDtypeStruct((chunks, CHUNK), jnp.int32)
    face_ids = jax.ShapeDtypeStruct((2, F), jnp.int32)
    prepared = pl.pallas_call(
        pair_kernel,
        out_shape=(
            jax.ShapeDtypeStruct((chunks, 2 * TR, CHUNK), BF16),
            ids,
            ids,
            jax.ShapeDtypeStruct((chunks, CHUNK), F32),
            face_ids,
            face_ids,
        ),
        in_specs=[smem, smem, pl.BlockSpec(memory_space=pl.ANY)] + [vmem] * 5,
        out_specs=(vmem,) * 6,
        scratch_shapes=[
            pltpu.VMEM(pair_blocks.shape, BF16),
            pltpu.VMEM((pairs * 32, 128), F32),
            pltpu.VMEM((elements, TR, 128), BF16),
            pltpu.VMEM((elements, TR, 128), F32),
            pltpu.VMEM((elements, 128), F32),
            pltpu.SemaphoreType.DMA,
        ],
        compiler_params=pltpu.CompilerParams(vmem_limit_bytes=61 * 2**20),
        name="pair_stage",
    )(
        pair_target,
        pair_source,
        pair_blocks,
        source_values,
        connectivity.T,
        jacobian.reshape(1, elements),
        send_up,
        send_down,
    )

    group = min(GROUP, n)
    layers = n // group
    field = jax.ShapeDtypeStruct((TR, NODE_DEV), F32)
    right, image, gram = pl.pallas_call(
        functools.partial(exchange_kernel, n),
        out_shape=(field, field, jax.ShapeDtypeStruct((TR, 128), F32)),
        in_specs=[vmem] * 6,
        out_specs=(vmem, vmem, vmem),
        scratch_shapes=[
            pltpu.VMEM((Q_ALL * (LO // 128) * TR, 128), F32),
            pltpu.VMEM((Q_PRODUCT * 2 * TR, LO), BF16),
            pltpu.VMEM((2, 4 * NP, 4 * NP), BF16),
            pltpu.VMEM((chunks, LO, CHUNK), BF16),
            pltpu.VMEM((LO, 2 * F), BF16),
            pltpu.VMEM((chunks, TR, CHUNK), F32),
            pltpu.VMEM((chunks, 2 * TR, CHUNK), BF16),
            pltpu.VMEM((2, Q_ALL * TR, LO), F32),
            pltpu.VMEM((2, FACE, LO), F32),
            pltpu.VMEM((3, 2, FACE, LO), F32),
            pltpu.VMEM((group, TR, 128), F32),
            pltpu.VMEM((layers, TR, 128), F32),
            pltpu.SemaphoreType.DMA((3, 2)),
            pltpu.SemaphoreType.DMA((3, 2)),
            pltpu.SemaphoreType.DMA((group,)),
            pltpu.SemaphoreType.DMA((group,)),
            pltpu.SemaphoreType.DMA((layers,)),
            pltpu.SemaphoreType.DMA((layers,)),
        ],
        compiler_params=pltpu.CompilerParams(
            collective_id=0, has_side_effects=True, vmem_limit_bytes=61 * 2**20
        ),
        name="exchange_stage",
    )(*prepared)

    out = jax.ShapeDtypeStruct((TR, NODE_DEV), F32)
    return pl.pallas_call(
        output_kernel,
        out_shape=(out, out, out),
        in_specs=[vmem] * 3,
        out_specs=(pl.BlockSpec(memory_space=pl.ANY),) * 3,
        scratch_shapes=[pltpu.VMEM((TR, NODE_DEV), F32)] * 3 + [pltpu.SemaphoreType.DMA((3,))],
        compiler_params=pltpu.CompilerParams(vmem_limit_bytes=61 * 2**20),
        name="output_stage",
    )(gram, right, image)


def solution(mesh):
    return jax.shard_map(
        functools.partial(per_device, mesh.shape["dom"]),
        mesh=mesh,
        in_specs=(
            P("dom", None),
            P("dom", None),
            P("dom", None),
            P("dom"),
            P("dom", None),
            P("dom"),
            P("dom"),
            P(None, "dom"),
        ),
        out_specs=(P(None, "dom"), P(None, "dom"), P(None, "dom")),
        check_vma=False,
    )
```

```python
import functools

import jax
import jax.numpy as jnp
from jax import lax
from jax.experimental import pallas as pl
from jax.experimental.pallas import tpu as pltpu
from jax.sharding import PartitionSpec as P

TR = 32
NP = 64
NODE_DEV = 3456
F = 768
LO = 256
Q_OWN = -(-NODE_DEV // LO)
Q_FACE = F // LO
Q_ALL = Q_OWN + 2 * Q_FACE
OWN = Q_OWN * TR
FACE = Q_FACE * TR
CHUNK = 512
Q_PRODUCT = 7
GROUP = 8
MESH = pl.DeviceIdType.MESH
HIGH = lax.Precision.HIGHEST
F32 = jnp.float32
BF16 = jnp.bfloat16
NT = (((1,), (1,)), ((), ()))


def line_entry(a, b):
    apart = jnp.abs(a - b)
    inner = jnp.logical_or(a == 1, a == 2)
    near = jnp.where(a + b == 3, -81.0, 99.0)
    far = jnp.where(apart == 2, -36.0, 19.0)
    return jnp.where(apart == 0, jnp.where(inner, 648.0, 128.0), jnp.where(apart == 1, near, far))


def node_of(position):
    return jnp.bitwise_and(position, 31) * 2 + jnp.bitwise_and(jnp.right_shift(position, 5), 1)


def mass_block():
    shape = (4 * NP, 4 * NP)
    rows, columns = lax.broadcasted_iota(jnp.int32, shape, 0), lane_ids(shape)
    first, second = node_of(rows), node_of(columns)
    value = jnp.where(jnp.right_shift(rows, 6) == jnp.right_shift(columns, 6), 504.0**-3, 0.0)
    for digit in (0, 2, 4):
        value = value * line_entry(
            jnp.bitwise_and(jnp.right_shift(first, digit), 3),
            jnp.bitwise_and(jnp.right_shift(second, digit), 3),
        )
    return value


def lane_ids(shape):
    return lax.broadcasted_iota(jnp.int32, shape, len(shape) - 1)


def pieces(value):
    first = value.astype(BF16)
    return first, (value - first.astype(F32)).astype(BF16)


def one_hot(lo_row):
    width = lo_row.shape[1]
    rows = lax.broadcasted_iota(jnp.int32, (LO, width), 0)
    return jnp.where(rows == lo_row, 1.0, 0.0).astype(BF16)


def stacked(value):
    return jnp.concatenate(pieces(value), axis=0)


def spread(stack, q_row, blocks):
    return jnp.concatenate(
        [stack * jnp.where(q_row == q, 1.0, 0.0).astype(BF16) for q in blocks], axis=0
    )


def add_up(left, right):
    return lax.dot_general(left, right, NT, preferred_element_type=F32)


def joined(value):
    return jnp.concatenate(
        [
            value[at : at + TR] + value[at + TR : at + 2 * TR]
            for at in range(0, value.shape[0], 2 * TR)
        ],
        axis=0,
    )


def scatter(stack, q_row, blocks, hot):
    return joined(add_up(spread(stack, q_row, blocks), hot))


def scatter_two(values, q_ref, step, blocks, marks):
    left = [
        spread(values[2 * step + b], q_ref[pl.ds(2 * step + b, 1), :], blocks) for b in range(2)
    ]
    return joined(add_up(jnp.concatenate(left, axis=1), jnp.concatenate(marks, axis=1)))


def gather(table, first_tile, tiles, q_row, lo_row):
    tile_row = q_row * (LO // 128) + jnp.right_shift(lo_row, 7)
    lane_row = jnp.bitwise_and(lo_row, 127)
    columns = []
    for at in range(0, q_row.shape[1], 128):
        tile = jnp.broadcast_to(tile_row[:, at : at + 128], (TR, 128))
        lane = jnp.broadcast_to(lane_row[:, at : at + 128], (TR, 128))
        total = jnp.zeros((TR, 128), F32)
        for t in range(first_tile, first_tile + tiles):
            here = jnp.take_along_axis(table[t * TR : (t + 1) * TR, :], lane, axis=1)
            total = jnp.where(tile == t, here, total)
        columns.append(total)
    return jnp.concatenate(columns, axis=1)


def gather_product(table, blocks, q_row, hot):
    found = jnp.dot(table, hot, preferred_element_type=F32)
    total = None
    for at, q in enumerate(blocks):
        rows = found[2 * at * TR : (2 * at + 2) * TR]
        part = jnp.where(q_row == q, rows[0:TR] + rows[TR:], 0.0)
        total = part if total is None else total + part
    return total


def split_slots(slots):
    padded = jnp.where(slots < NODE_DEV, slots, slots + (Q_OWN * LO - NODE_DEV))
    return jnp.right_shift(padded, 8), jnp.bitwise_and(padded, LO - 1)


def pair_kernel(
    target_ref,
    source_ref,
    blocks_hbm,
    values_ref,
    slots_ref,
    jacobian_ref,
    up_ref,
    down_ref,
    out_ref,
    lo_ref,
    q_ref,
    scale_ref,
    face_lo_ref,
    face_q_ref,
    blocks_ref,
    flat,
    flat_two,
    table,
    total,
    wide,
    blocks_sem,
):
    pairs = blocks_ref.shape[0]
    elements = total.shape[0]
    chunks = lo_ref.shape[0]
    per_chunk = CHUNK // NP
    lanes = lane_ids((TR, 128))

    fetch = pltpu.make_async_copy(blocks_hbm, blocks_ref, blocks_sem)
    fetch.start()

    def by_chunk():
        left_half = lane_ids((chunks, 128)) < 64
        return jnp.concatenate(
            [
                jnp.where(
                    left_half,
                    wide[pl.ds(2 * m, chunks, stride=per_chunk), :],
                    wide[pl.ds(2 * m + 1, chunks, stride=per_chunk), :],
                )
                for m in range(CHUNK // 128)
            ],
            axis=1,
        )

    shape = (NP, 2 * NP)
    order = lax.broadcasted_iota(jnp.int32, shape, 0) == node_of(lane_ids(shape))
    wide[...] = lax.dot_general(
        slots_ref[...].astype(F32),
        jnp.where(order, 1.0, 0.0),
        (((0,), (0,)), ((), ())),
        precision=HIGH,
        preferred_element_type=F32,
    )
    q_ids, lo_ids = split_slots((by_chunk() + 0.5).astype(jnp.int32))
    q_ref[...] = q_ids
    lo_ref[...] = lo_ids
    corner = lax.broadcasted_iota(jnp.int32, (elements, elements), 0) == lane_ids((elements, elements))
    wide[...] = jnp.dot(
        jnp.where(corner, jacobian_ref[...], 0.0),
        jnp.ones((elements, 128), F32),
        precision=HIGH,
        preferred_element_type=F32,
    )
    scale_ref[...] = by_chunk()
    for way, face_ref in enumerate((up_ref, down_ref)):
        q_ids, lo_ids = split_slots(face_ref[...])
        face_q_ref[way : way + 1, :] = q_ids
        face_lo_ref[way : way + 1, :] = lo_ids

    for w in range(elements // 2):
        window = values_ref[:, w * 128 : (w + 1) * 128].astype(F32)
        turned = pltpu.roll(window, 64, 1)
        table[2 * w] = jnp.where(lanes < 64, window, turned).astype(BF16)
        table[2 * w + 1] = jnp.where(lanes < 64, turned, window).astype(BF16)
    total[...] = jnp.zeros_like(total)
    fetch.wait()

    rounds = pairs // 16

    def lay_out(g, buffer):
        rows = blocks_ref[pl.ds(pl.multiple_of(g * 16, 16), 16), :]
        for c in range(32):
            buffer[pl.ds(c, 16, stride=32), :] = rows[:, c * 128 : (c + 1) * 128].astype(F32)

    def multiply(first, at, buffer):
        left, right = [], []
        for g in range(4):
            left.append(table[source_ref[first + at + g]])
            block = buffer[(at + g) * 32 : (at + g + 1) * 32, :]
            right.append(jnp.where(lanes < 64, block, 0.0).astype(BF16))
            right.append(jnp.where(lanes < 64, 0.0, block).astype(BF16))
        product = add_up(jnp.concatenate(left, axis=0), jnp.concatenate(right, axis=0))
        for g in range(4):
            part = product[g * TR : (g + 1) * TR, (g // 2) * 128 : (g // 2 + 1) * 128]
            keep = (lanes < 64) if g % 2 == 0 else (lanes >= 64)
            to = target_ref[first + at + g]
            total[to] = total[to] + jnp.where(keep, part, 0.0)

    lay_out(0, flat)

    def two_rounds(step, carry):
        for now, here, later in ((2 * step, flat, flat_two), (2 * step + 1, flat_two, flat)):
            lay_out(jnp.minimum(now + 1, rounds - 1), later)
            for at in range(0, 16, 4):
                multiply(now * 16, at, here)
        return carry

    lax.fori_loop(0, rounds // 2, two_rounds, 0)

    def add(step, carry):
        tiles = []
        for m in range(CHUNK // 128):
            even = total[step * per_chunk + 2 * m]
            odd = total[step * per_chunk + 2 * m + 1]
            tiles.append(
                jnp.where(lanes < 64, even + pltpu.roll(even, 64, 1), odd + pltpu.roll(odd, 64, 1))
            )
        out_ref[step] = stacked(jnp.concatenate(tiles, axis=1))
        return carry

    lax.fori_loop(0, chunks, add, 0, unroll=2)


def exchange_kernel(
    n,
    sums_ref,
    lo_ref,
    q_ref,
    scale_ref,
    face_lo_ref,
    face_q_ref,
    right_ref,
    image_ref,
    gram_ref,
    table,
    split_table,
    mass,
    hot,
    face_hot,
    found,
    applied,
    ext,
    outgoing,
    incoming,
    near,
    far,
    send_sem,
    recv_sem,
    near_send,
    near_recv,
    far_send,
    far_recv,
):
    me = lax.axis_index("dom")
    group = min(GROUP, n)
    layers = n // group
    spot, layer = lax.rem(me, group), me // group
    has_up, has_down = me < n - 1, me > 0
    near_ids = [layer * group + lax.rem(spot + o, group) for o in range(1, group)]
    far_ids = [lax.rem(layer + o, layers) * group + spot for o in range(1, layers)]
    cross_up = jnp.logical_and(spot == group - 1, has_up)
    cross_down = jnp.logical_and(spot == 0, has_down)

    barrier = pltpu.get_barrier_semaphore()
    for other in near_ids + far_ids:
        pl.semaphore_signal(barrier, inc=1, device_id=(other,), device_id_type=MESH)

    @pl.when(cross_up)
    def _():
        pl.semaphore_signal(barrier, inc=1, device_id=(me + 1,), device_id_type=MESH)

    @pl.when(cross_down)
    def _():
        pl.semaphore_signal(barrier, inc=1, device_id=(me - 1,), device_id_type=MESH)

    def copy(source, phase, way):
        return pltpu.make_async_remote_copy(
            src_ref=source,
            dst_ref=incoming.at[phase, way],
            send_sem=send_sem.at[phase, way],
            recv_sem=recv_sem.at[phase, way],
            device_id=(me + (1 if way else -1),),
            device_id_type=MESH,
        )

    def start(source, phase, way):
        @pl.when(has_up if way else has_down)
        def _():
            copy(source, phase, way).start()

    def finish(source, phase, way):
        @pl.when(has_up if way else has_down)
        def _():
            copy(source, phase, way).wait_send()

    def arrive(source, phase, way):
        @pl.when(has_down if way else has_up)
        def _():
            copy(source, phase, way).wait_recv()

        @pl.when(jnp.logical_not(has_down if way else has_up))
        def _():
            incoming[phase, way] = jnp.zeros((FACE, LO), F32)

    down_rows = pl.ds(OWN, FACE)
    up_rows = pl.ds(OWN + FACE, FACE)
    own_blocks, face_blocks = range(Q_OWN), range(Q_OWN, Q_ALL)
    chunks = lo_ref.shape[0]
    ext[...] = jnp.zeros_like(ext)

    def fill(block, value):
        for b in range(value.shape[0] // TR):
            for part in range(LO // 128):
                at = ((block + b) * (LO // 128) + part) * TR
                table[at : at + TR, :] = value[
                    b * TR : (b + 1) * TR, part * 128 : (part + 1) * 128
                ]
            if block + b < Q_PRODUCT:
                split_table[(block + b) * 2 * TR : (block + b + 1) * 2 * TR, :] = stacked(
                    value[b * TR : (b + 1) * TR]
                )

    def face_sums(step, carry):
        marks = [one_hot(lo_ref[pl.ds(2 * step + b, 1), :]) for b in range(2)]
        for b in range(2):
            hot[2 * step + b] = marks[b]
        ext[0, OWN:, :] += scatter_two(sums_ref, q_ref, step, face_blocks, marks)
        return carry

    lax.fori_loop(0, chunks // 2, face_sums, 0, unroll=2)
    partners = group + layers - 2
    crossing = jnp.logical_or(cross_up, cross_down)

    @pl.when(crossing)
    def _():
        pl.semaphore_wait(barrier, partners + 1)

    @pl.when(jnp.logical_not(crossing))
    def _():
        pl.semaphore_wait(barrier, partners)

    start(ext.at[0, down_rows], 0, 0)
    start(ext.at[0, up_rows], 0, 1)

    def own_sums(values, phase):
        def step_sums(step, carry):
            marks = [hot[2 * step + b] for b in range(2)]
            ext[phase, 0:OWN, :] += scatter_two(values, q_ref, step, own_blocks, marks)
            return carry

        lax.fori_loop(0, chunks // 2, step_sums, 0, unroll=2)

    def write_out(ref, value):
        for q in own_blocks:
            end = min((q + 1) * LO, NODE_DEV)
            ref[:, q * LO : end] = value[q * TR : (q + 1) * TR, 0 : end - q * LO]

    own_sums(sums_ref, 0)
    for way in range(2):
        face_hot[:, way * F : (way + 1) * F] = one_hot(face_lo_ref[way : way + 1, :])
    first, second = pieces(mass_block())
    mass[0] = first
    mass[1] = second

    def settle(own, phase):
        left = []
        for way in range(2):
            for b in range(Q_FACE):
                part = slice(b * LO, (b + 1) * LO)
                stack = stacked(incoming[phase, way, b * TR : (b + 1) * TR, :])
                left.append(spread(stack, face_q_ref[way : way + 1, part], own_blocks))
        return own + joined(add_up(jnp.concatenate(left, axis=1), face_hot[...]))

    arrive(ext.at[0, down_rows], 0, 0)
    arrive(ext.at[0, up_rows], 0, 1)
    right = settle(ext[0, 0:OWN, :], 0)
    fill(0, right)

    own_tiles, face_tiles = NODE_DEV // 128, 2 * F // 128
    first_tile, first_face = Q_PRODUCT * LO // 128, Q_OWN * LO // 128

    def own_gather(q_row, lo_row, marks):
        return gather(table, first_tile, own_tiles - first_tile, q_row, lo_row) + gather_product(
            split_table[...], range(Q_PRODUCT), q_row, marks
        )

    for way in (1, 0):
        mine = slice(1 - way, 2 - way)
        values = own_gather(
            face_q_ref[mine, :], face_lo_ref[mine, :], face_hot[:, (1 - way) * F : (2 - way) * F]
        )
        for b in range(Q_FACE):
            outgoing[way, b * TR : (b + 1) * TR, :] = values[:, b * LO : (b + 1) * LO]
        start(outgoing.at[way], 1, way)

    def own_values(step, carry):
        q_row, lo_row = q_ref[pl.ds(step, 1), :], lo_ref[pl.ds(step, 1), :]
        found[step] = own_gather(q_row, lo_row, hot[step])
        return carry

    lax.fori_loop(0, chunks, own_values, 0, unroll=2)
    write_out(right_ref, right)
    for way in (1, 0):
        arrive(outgoing.at[way], 1, way)
        fill(Q_OWN if way else Q_OWN + Q_FACE, incoming[1, way])

    def face_values(step):
        q_row, lo_row = q_ref[pl.ds(step, 1), :], lo_ref[pl.ds(step, 1), :]
        return gather(table, first_face, face_tiles, q_row, lo_row)

    def elements(step, from_faces):
        q_row = q_ref[pl.ds(step, 1), :]
        values = found[step] + from_faces
        following = face_values(jnp.minimum(step + 1, chunks - 1))
        first, second = pieces(
            jnp.concatenate([values[:, h : h + 256] for h in range(0, CHUNK, 256)], axis=0)
        )
        result = (
            jnp.dot(first, mass[0], preferred_element_type=F32)
            + jnp.dot(second, mass[0], preferred_element_type=F32)
            + jnp.dot(first, mass[1], preferred_element_type=F32)
        )
        result = jnp.concatenate(
            [result[h * TR : (h + 1) * TR] for h in range(CHUNK // 256)], axis=1
        )
        stack = stacked(result * scale_ref[pl.ds(step, 1), :])
        applied[step] = stack
        ext[1, OWN:, :] += scatter(stack, q_row, face_blocks, hot[step])
        return following

    lax.fori_loop(0, chunks, elements, face_values(0), unroll=2)
    start(ext.at[1, down_rows], 2, 0)
    start(ext.at[1, up_rows], 2, 1)
    own_sums(applied, 1)
    arrive(ext.at[1, down_rows], 2, 0)
    arrive(ext.at[1, up_rows], 2, 1)
    image = settle(ext[1, 0:OWN, :], 2)
    write_out(image_ref, image)

    stack = jnp.concatenate(
        [
            jnp.concatenate(
                [stacked(field[q * TR : (q + 1) * TR]) for q in own_blocks], axis=1
            )
            for field in (right, image)
        ],
        axis=0,
    )
    products = add_up(stack, stack)
    lanes = lane_ids((TR, 128))
    upper = products[0:TR] + products[TR : 2 * TR]
    lower = products[2 * TR : 3 * TR] + products[3 * TR :]
    upper = upper + pltpu.roll(upper, 96, 1)
    lower = pltpu.roll(lower + pltpu.roll(lower, 96, 1), 96, 1)
    gram = jnp.where(jnp.logical_and(lanes >= TR, lanes < 2 * TR), lower, upper)

    def sum_over(value, buffer, others, sends, recvs):
        buffer[0] = value

        def part(o, other):
            return pltpu.make_async_remote_copy(
                src_ref=buffer.at[0],
                dst_ref=buffer.at[o],
                send_sem=sends.at[o],
                recv_sem=recvs.at[o],
                device_id=(other,),
                device_id_type=MESH,
            )

        for o, other in enumerate(others, 1):
            part(o, other).start()
        for o, other in enumerate(others, 1):
            part(o, other).wait_recv()
            value = value + buffer[o]
        for o, other in enumerate(others, 1):
            part(o, other).wait_send()
        return value

    gram = sum_over(gram, near, near_ids, near_send, near_recv)
    gram_ref[...] = sum_over(gram, far, far_ids, far_send, far_recv)

    finish(ext.at[0, down_rows], 0, 0)
    finish(ext.at[0, up_rows], 0, 1)
    for way in range(2):
        finish(outgoing.at[way], 1, way)
    finish(ext.at[1, down_rows], 2, 0)
    finish(ext.at[1, up_rows], 2, 1)


def output_kernel(
    gram_ref,
    right_ref,
    image_ref,
    solution_out,
    residual_out,
    basis_out,
    solution_ref,
    residual_ref,
    basis_ref,
    sems,
):
    def dot(a, b):
        return jnp.dot(a, b, precision=HIGH, preferred_element_type=F32)

    rows = lax.broadcasted_iota(jnp.int32, (TR, 128), 0)
    lanes = lane_ids((TR, 128))
    work = gram_ref[...]
    gram = work[:, 0:TR]
    for j in range(0, TR, 2):
        c = 2 * TR + j
        a, b = work[j : j + 1, :], work[j + 1 : j + 2, :]
        inverse = 1.0 / a[:, c : c + 1]
        across = a[:, c + 1 : c + 2] * inverse
        b = b - (b[:, c : c + 1] * inverse) * a
        b = b * (1.0 / b[:, c + 1 : c + 2])
        a = a * inverse - across * b
        rest = work - work[:, c : c + 1] * a - work[:, c + 1 : c + 2] * b
        work = jnp.where(rows == j, a, jnp.where(rows == j + 1, b, rest))
    step_t = work[:, 0:TR]
    step = step_t.T
    image_part = work[:, TR : 2 * TR]
    new_gram = dot(gram, dot(image_part, step_t)) - gram

    def times(small):
        first, second = pieces(small)
        both = jnp.concatenate([first, second], axis=0)

        def apply(value):
            top, rest = pieces(value)
            found = jnp.dot(both, top, preferred_element_type=F32)
            return (
                found[0:TR] + found[TR : 2 * TR] + jnp.dot(first, rest, preferred_element_type=F32)
            )

        return apply

    parts = [slice(at, at + NODE_DEV // 3) for at in range(0, NODE_DEV, NODE_DEV // 3)]
    apply_step = times(step)
    for part in parts:
        right = right_ref[:, part]
        solution_ref[:, part] = apply_step(right)
        residual_ref[:, part] = right - apply_step(image_ref[:, part])
    copies = [
        pltpu.make_async_copy(solution_ref, solution_out, sems.at[0]),
        pltpu.make_async_copy(residual_ref, residual_out, sems.at[1]),
        pltpu.make_async_copy(basis_ref, basis_out, sems.at[2]),
    ]
    copies[0].start()
    copies[1].start()

    work = jnp.concatenate([new_gram, jnp.zeros((TR, 128 - TR), F32)], axis=1)
    work = jnp.where(lanes == rows + TR, 1.0, work)
    scale = jnp.zeros((TR, 128), F32)
    for j in range(0, TR, 2):
        a, b = work[j : j + 1, :], work[j + 1 : j + 2, :]
        pivot, across = a[:, j : j + 1], a[:, j + 1 : j + 2]
        inverse = 1.0 / pivot
        b = b - (b[:, j : j + 1] * inverse) * a
        second_pivot = b[:, j + 1 : j + 2]
        factor = work[:, j : j + 1] * inverse
        second = (work[:, j + 1 : j + 2] - factor * across) * (1.0 / second_pivot)
        rest = work - factor * a - second * b
        work = jnp.where(rows > j + 1, rest, jnp.where(rows == j + 1, b, work))
        scale = jnp.where(rows == j, lax.rsqrt(pivot), scale)
        scale = jnp.where(rows == j + 1, lax.rsqrt(second_pivot), scale)
    apply_lower = times((work * scale)[:, TR : 2 * TR])
    for part in parts:
        basis_ref[:, part] = apply_lower(residual_ref[:, part])
    copies[2].start()
    for copy in copies:
        copy.wait()


def per_device(
    n, connectivity, send_down, send_up, jacobian, pair_blocks, pair_target, pair_source, source_values
):
    elements = connectivity.shape[0]
    pairs = pair_target.shape[0]
    chunks = elements * NP // CHUNK
    vmem = pl.BlockSpec(memory_space=pltpu.VMEM)
    smem = pl.BlockSpec(memory_space=pltpu.SMEM)

    ids = jax.ShapeDtypeStruct((chunks, CHUNK), jnp.int32)
    face_ids = jax.ShapeDtypeStruct((2, F), jnp.int32)
    prepared = pl.pallas_call(
        pair_kernel,
        out_shape=(
            jax.ShapeDtypeStruct((chunks, 2 * TR, CHUNK), BF16),
            ids,
            ids,
            jax.ShapeDtypeStruct((chunks, CHUNK), F32),
            face_ids,
            face_ids,
        ),
        in_specs=[smem, smem, pl.BlockSpec(memory_space=pl.ANY)] + [vmem] * 5,
        out_specs=(vmem,) * 6,
        scratch_shapes=[
            pltpu.VMEM(pair_blocks.shape, BF16),
            pltpu.VMEM((16 * 32, 128), F32),
            pltpu.VMEM((16 * 32, 128), F32),
            pltpu.VMEM((elements, TR, 128), BF16),
            pltpu.VMEM((elements, TR, 128), F32),
            pltpu.VMEM((elements, 128), F32),
            pltpu.SemaphoreType.DMA,
        ],
        compiler_params=pltpu.CompilerParams(vmem_limit_bytes=61 * 2**20),
        name="pair_stage",
    )(
        pair_target,
        pair_source,
        pair_blocks,
        source_values,
        connectivity.T,
        jacobian.reshape(1, elements),
        send_up,
        send_down,
    )

    group = min(GROUP, n)
    layers = n // group
    field = jax.ShapeDtypeStruct((TR, NODE_DEV), F32)
    right, image, gram = pl.pallas_call(
        functools.partial(exchange_kernel, n),
        out_shape=(field, field, jax.ShapeDtypeStruct((TR, 128), F32)),
        in_specs=[vmem] * 6,
        out_specs=(vmem, vmem, vmem),
        scratch_shapes=[
            pltpu.VMEM((Q_ALL * (LO // 128) * TR, 128), F32),
            pltpu.VMEM((Q_PRODUCT * 2 * TR, LO), BF16),
            pltpu.VMEM((2, 4 * NP, 4 * NP), BF16),
            pltpu.VMEM((chunks, LO, CHUNK), BF16),
            pltpu.VMEM((LO, 2 * F), BF16),
            pltpu.VMEM((chunks, TR, CHUNK), F32),
            pltpu.VMEM((chunks, 2 * TR, CHUNK), BF16),
            pltpu.VMEM((2, Q_ALL * TR, LO), F32),
            pltpu.VMEM((2, FACE, LO), F32),
            pltpu.VMEM((3, 2, FACE, LO), F32),
            pltpu.VMEM((group, TR, 128), F32),
            pltpu.VMEM((layers, TR, 128), F32),
            pltpu.SemaphoreType.DMA((3, 2)),
            pltpu.SemaphoreType.DMA((3, 2)),
            pltpu.SemaphoreType.DMA((group,)),
            pltpu.SemaphoreType.DMA((group,)),
            pltpu.SemaphoreType.DMA((layers,)),
            pltpu.SemaphoreType.DMA((layers,)),
        ],
        compiler_params=pltpu.CompilerParams(
            collective_id=0, has_side_effects=True, vmem_limit_bytes=61 * 2**20
        ),
        name="exchange_stage",
    )(*prepared)

    out = jax.ShapeDtypeStruct((TR, NODE_DEV), F32)
    return pl.pallas_call(
        output_kernel,
        out_shape=(out, out, out),
        in_specs=[vmem] * 3,
        out_specs=(pl.BlockSpec(memory_space=pl.ANY),) * 3,
        scratch_shapes=[pltpu.VMEM((TR, NODE_DEV), F32)] * 3 + [pltpu.SemaphoreType.DMA((3,))],
        compiler_params=pltpu.CompilerParams(vmem_limit_bytes=61 * 2**20),
        name="output_stage",
    )(gram, right, image)


def solution(mesh):
    return jax.shard_map(
        functools.partial(per_device, mesh.shape["dom"]),
        mesh=mesh,
        in_specs=(
            P("dom", None),
            P("dom", None),
            P("dom", None),
            P("dom"),
            P("dom", None),
            P("dom"),
            P("dom"),
            P(None, "dom"),
        ),
        out_specs=(P(None, "dom"), P(None, "dom"), P(None, "dom")),
        check_vma=False,
    )
```

```python
import functools

import jax
import jax.numpy as jnp
from jax import lax
from jax.experimental import pallas as pl
from jax.experimental.pallas import tpu as pltpu
from jax.sharding import PartitionSpec as P

TR = 32
NP = 64
NODE_DEV = 3456
F = 768
LO = 256
Q_OWN = -(-NODE_DEV // LO)
Q_FACE = F // LO
Q_ALL = Q_OWN + 2 * Q_FACE
OWN = Q_OWN * TR
FACE = Q_FACE * TR
CHUNK = 512
Q_PRODUCT = 7
GROUP = 8
MESH = pl.DeviceIdType.MESH
HIGH = lax.Precision.HIGHEST
F32 = jnp.float32
BF16 = jnp.bfloat16
NT = (((1,), (1,)), ((), ()))


def line_entry(a, b):
    apart = jnp.abs(a - b)
    inner = jnp.logical_or(a == 1, a == 2)
    near = jnp.where(a + b == 3, -81.0, 99.0)
    far = jnp.where(apart == 2, -36.0, 19.0)
    return jnp.where(apart == 0, jnp.where(inner, 648.0, 128.0), jnp.where(apart == 1, near, far))


def node_of(position):
    return jnp.bitwise_and(position, 31) * 2 + jnp.bitwise_and(jnp.right_shift(position, 5), 1)


def mass_block():
    shape = (4 * NP, 4 * NP)
    rows, columns = lax.broadcasted_iota(jnp.int32, shape, 0), lane_ids(shape)
    first, second = node_of(rows), node_of(columns)
    value = jnp.where(jnp.right_shift(rows, 6) == jnp.right_shift(columns, 6), 504.0**-3, 0.0)
    for digit in (0, 2, 4):
        value = value * line_entry(
            jnp.bitwise_and(jnp.right_shift(first, digit), 3),
            jnp.bitwise_and(jnp.right_shift(second, digit), 3),
        )
    return value


def lane_ids(shape):
    return lax.broadcasted_iota(jnp.int32, shape, len(shape) - 1)


def pieces(value):
    first = value.astype(BF16)
    return first, (value - first.astype(F32)).astype(BF16)


def one_hot(lo_row):
    width = lo_row.shape[1]
    rows = lax.broadcasted_iota(jnp.int32, (LO, width), 0)
    return jnp.where(rows == lo_row, 1.0, 0.0).astype(BF16)


def stacked(value):
    return jnp.concatenate(pieces(value), axis=0)


def spread(stack, q_row, blocks):
    return jnp.concatenate(
        [stack * jnp.where(q_row == q, 1.0, 0.0).astype(BF16) for q in blocks], axis=0
    )


def add_up(left, right):
    return lax.dot_general(left, right, NT, preferred_element_type=F32)


def joined(value):
    return jnp.concatenate(
        [
            value[at : at + TR] + value[at + TR : at + 2 * TR]
            for at in range(0, value.shape[0], 2 * TR)
        ],
        axis=0,
    )


def scatter(stack, q_row, blocks, hot):
    return joined(add_up(spread(stack, q_row, blocks), hot))


def scatter_four(values, q_ref, step, blocks, marks):
    left = [
        spread(values[4 * step + b], q_ref[pl.ds(4 * step + b, 1), :], blocks) for b in range(4)
    ]
    return joined(add_up(jnp.concatenate(left, axis=1), jnp.concatenate(marks, axis=1)))


def gather(table, first_tile, tiles, q_row, lo_row):
    tile_row = q_row * (LO // 128) + jnp.right_shift(lo_row, 7)
    lane_row = jnp.bitwise_and(lo_row, 127)
    columns = []
    for at in range(0, q_row.shape[1], 128):
        tile = jnp.broadcast_to(tile_row[:, at : at + 128], (TR, 128))
        lane = jnp.broadcast_to(lane_row[:, at : at + 128], (TR, 128))
        total = jnp.zeros((TR, 128), F32)
        for t in range(first_tile, first_tile + tiles):
            here = jnp.take_along_axis(table[t * TR : (t + 1) * TR, :], lane, axis=1)
            total = jnp.where(tile == t, here, total)
        columns.append(total)
    return jnp.concatenate(columns, axis=1)


def gather_product(table, blocks, q_row, hot):
    found = jnp.dot(table, hot, preferred_element_type=F32)
    total = None
    for at, q in enumerate(blocks):
        rows = found[2 * at * TR : (2 * at + 2) * TR]
        part = jnp.where(q_row == q, rows[0:TR] + rows[TR:], 0.0)
        total = part if total is None else total + part
    return total


def split_slots(slots):
    padded = jnp.where(slots < NODE_DEV, slots, slots + (Q_OWN * LO - NODE_DEV))
    return jnp.right_shift(padded, 8), jnp.bitwise_and(padded, LO - 1)


def pair_kernel(
    target_ref,
    source_ref,
    blocks_hbm,
    values_ref,
    slots_ref,
    jacobian_ref,
    up_ref,
    down_ref,
    out_ref,
    lo_ref,
    q_ref,
    scale_ref,
    face_lo_ref,
    face_q_ref,
    blocks_ref,
    flat,
    flat_two,
    table,
    total,
    wide,
    blocks_sem,
):
    pairs = blocks_ref.shape[0]
    elements = total.shape[0]
    chunks = lo_ref.shape[0]
    per_chunk = CHUNK // NP
    lanes = lane_ids((TR, 128))

    fetch = pltpu.make_async_copy(blocks_hbm, blocks_ref, blocks_sem)
    fetch.start()

    def by_chunk():
        left_half = lane_ids((chunks, 128)) < 64
        return jnp.concatenate(
            [
                jnp.where(
                    left_half,
                    wide[pl.ds(2 * m, chunks, stride=per_chunk), :],
                    wide[pl.ds(2 * m + 1, chunks, stride=per_chunk), :],
                )
                for m in range(CHUNK // 128)
            ],
            axis=1,
        )

    shape = (NP, 2 * NP)
    order = lax.broadcasted_iota(jnp.int32, shape, 0) == node_of(lane_ids(shape))
    wide[...] = lax.dot_general(
        slots_ref[...].astype(F32),
        jnp.where(order, 1.0, 0.0),
        (((0,), (0,)), ((), ())),
        precision=HIGH,
        preferred_element_type=F32,
    )
    q_ids, lo_ids = split_slots((by_chunk() + 0.5).astype(jnp.int32))
    q_ref[...] = q_ids
    lo_ref[...] = lo_ids
    corner = lax.broadcasted_iota(jnp.int32, (elements, elements), 0) == lane_ids((elements, elements))
    wide[...] = jnp.dot(
        jnp.where(corner, jacobian_ref[...], 0.0),
        jnp.ones((elements, 128), F32),
        precision=HIGH,
        preferred_element_type=F32,
    )
    scale_ref[...] = by_chunk()
    for way, face_ref in enumerate((up_ref, down_ref)):
        q_ids, lo_ids = split_slots(face_ref[...])
        face_q_ref[way : way + 1, :] = q_ids
        face_lo_ref[way : way + 1, :] = lo_ids

    for w in range(elements // 2):
        window = values_ref[:, w * 128 : (w + 1) * 128].astype(F32)
        turned = pltpu.roll(window, 64, 1)
        table[2 * w] = jnp.where(lanes < 64, window, turned).astype(BF16)
        table[2 * w + 1] = jnp.where(lanes < 64, turned, window).astype(BF16)
    total[...] = jnp.zeros_like(total)
    fetch.wait()

    rounds = pairs // 16

    def lay_out(g, buffer):
        rows = blocks_ref[pl.ds(pl.multiple_of(g * 16, 16), 16), :]
        for c in range(32):
            buffer[pl.ds(c, 16, stride=32), :] = rows[:, c * 128 : (c + 1) * 128].astype(F32)

    def multiply(first, at, buffer):
        left, right = [], []
        for g in range(4):
            left.append(table[source_ref[first + at + g]])
            block = buffer[(at + g) * 32 : (at + g + 1) * 32, :]
            right.append(jnp.where(lanes < 64, block, 0.0).astype(BF16))
            right.append(jnp.where(lanes < 64, 0.0, block).astype(BF16))
        product = add_up(jnp.concatenate(left, axis=0), jnp.concatenate(right, axis=0))
        for g in range(4):
            part = product[g * TR : (g + 1) * TR, (g // 2) * 128 : (g // 2 + 1) * 128]
            keep = (lanes < 64) if g % 2 == 0 else (lanes >= 64)
            to = target_ref[first + at + g]
            total[to] = total[to] + jnp.where(keep, part, 0.0)

    lay_out(0, flat)

    def two_rounds(step, carry):
        for now, here, later in ((2 * step, flat, flat_two), (2 * step + 1, flat_two, flat)):
            lay_out(jnp.minimum(now + 1, rounds - 1), later)
            for at in range(0, 16, 4):
                multiply(now * 16, at, here)
        return carry

    lax.fori_loop(0, rounds // 2, two_rounds, 0)

    def add(step, carry):
        tiles = []
        for m in range(CHUNK // 128):
            even = total[step * per_chunk + 2 * m]
            odd = total[step * per_chunk + 2 * m + 1]
            tiles.append(
                jnp.where(lanes < 64, even + pltpu.roll(even, 64, 1), odd + pltpu.roll(odd, 64, 1))
            )
        out_ref[step] = stacked(jnp.concatenate(tiles, axis=1))
        return carry

    lax.fori_loop(0, chunks, add, 0, unroll=2)


def exchange_kernel(
    n,
    sums_ref,
    lo_ref,
    q_ref,
    scale_ref,
    face_lo_ref,
    face_q_ref,
    right_ref,
    image_ref,
    gram_ref,
    table,
    split_table,
    mass,
    hot,
    face_hot,
    found,
    applied,
    ext,
    outgoing,
    incoming,
    near,
    far,
    send_sem,
    recv_sem,
    near_send,
    near_recv,
    far_send,
    far_recv,
):
    me = lax.axis_index("dom")
    group = min(GROUP, n)
    layers = n // group
    spot, layer = lax.rem(me, group), me // group
    has_up, has_down = me < n - 1, me > 0
    near_ids = [layer * group + lax.rem(spot + o, group) for o in range(1, group)]
    far_ids = [lax.rem(layer + o, layers) * group + spot for o in range(1, layers)]
    cross_up = jnp.logical_and(spot == group - 1, has_up)
    cross_down = jnp.logical_and(spot == 0, has_down)

    barrier = pltpu.get_barrier_semaphore()
    for other in near_ids + far_ids:
        pl.semaphore_signal(barrier, inc=1, device_id=(other,), device_id_type=MESH)

    @pl.when(cross_up)
    def _():
        pl.semaphore_signal(barrier, inc=1, device_id=(me + 1,), device_id_type=MESH)

    @pl.when(cross_down)
    def _():
        pl.semaphore_signal(barrier, inc=1, device_id=(me - 1,), device_id_type=MESH)

    def copy(source, phase, way):
        return pltpu.make_async_remote_copy(
            src_ref=source,
            dst_ref=incoming.at[phase, way],
            send_sem=send_sem.at[phase, way],
            recv_sem=recv_sem.at[phase, way],
            device_id=(me + (1 if way else -1),),
            device_id_type=MESH,
        )

    def start(source, phase, way):
        @pl.when(has_up if way else has_down)
        def _():
            copy(source, phase, way).start()

    def finish(source, phase, way):
        @pl.when(has_up if way else has_down)
        def _():
            copy(source, phase, way).wait_send()

    def arrive(source, phase, way):
        @pl.when(has_down if way else has_up)
        def _():
            copy(source, phase, way).wait_recv()

        @pl.when(jnp.logical_not(has_down if way else has_up))
        def _():
            incoming[phase, way] = jnp.zeros((FACE, LO), F32)

    down_rows = pl.ds(OWN, FACE)
    up_rows = pl.ds(OWN + FACE, FACE)
    own_blocks, face_blocks = range(Q_OWN), range(Q_OWN, Q_ALL)
    chunks = lo_ref.shape[0]
    ext[...] = jnp.zeros_like(ext)

    def fill(block, value):
        for b in range(value.shape[0] // TR):
            for part in range(LO // 128):
                at = ((block + b) * (LO // 128) + part) * TR
                table[at : at + TR, :] = value[
                    b * TR : (b + 1) * TR, part * 128 : (part + 1) * 128
                ]
            if block + b < Q_PRODUCT:
                split_table[(block + b) * 2 * TR : (block + b + 1) * 2 * TR, :] = stacked(
                    value[b * TR : (b + 1) * TR]
                )

    def face_sums(step, carry):
        marks = [one_hot(lo_ref[pl.ds(4 * step + b, 1), :]) for b in range(4)]
        for b in range(4):
            hot[4 * step + b] = marks[b]
        ext[0, OWN:, :] += scatter_four(sums_ref, q_ref, step, face_blocks, marks)
        return carry

    lax.fori_loop(0, chunks // 4, face_sums, 0)
    partners = group + layers - 2
    crossing = jnp.logical_or(cross_up, cross_down)

    @pl.when(crossing)
    def _():
        pl.semaphore_wait(barrier, partners + 1)

    @pl.when(jnp.logical_not(crossing))
    def _():
        pl.semaphore_wait(barrier, partners)

    start(ext.at[0, down_rows], 0, 0)
    start(ext.at[0, up_rows], 0, 1)

    def own_sums(values, phase):
        def step_sums(step, carry):
            marks = [hot[4 * step + b] for b in range(4)]
            ext[phase, 0:OWN, :] += scatter_four(values, q_ref, step, own_blocks, marks)
            return carry

        lax.fori_loop(0, chunks // 4, step_sums, 0)

    def write_out(ref, value):
        for q in own_blocks:
            end = min((q + 1) * LO, NODE_DEV)
            ref[:, q * LO : end] = value[q * TR : (q + 1) * TR, 0 : end - q * LO]

    own_sums(sums_ref, 0)
    for way in range(2):
        face_hot[:, way * F : (way + 1) * F] = one_hot(face_lo_ref[way : way + 1, :])
    first, second = pieces(mass_block())
    mass[0] = first
    mass[1] = second

    def settle(own, phase):
        left = []
        for way in range(2):
            for b in range(Q_FACE):
                part = slice(b * LO, (b + 1) * LO)
                stack = stacked(incoming[phase, way, b * TR : (b + 1) * TR, :])
                left.append(spread(stack, face_q_ref[way : way + 1, part], own_blocks))
        return own + joined(add_up(jnp.concatenate(left, axis=1), face_hot[...]))

    arrive(ext.at[0, down_rows], 0, 0)
    arrive(ext.at[0, up_rows], 0, 1)
    right = settle(ext[0, 0:OWN, :], 0)
    fill(0, right)

    own_tiles, face_tiles = NODE_DEV // 128, 2 * F // 128
    first_tile, first_face = Q_PRODUCT * LO // 128, Q_OWN * LO // 128

    def own_gather(q_row, lo_row, marks):
        return gather(table, first_tile, own_tiles - first_tile, q_row, lo_row) + gather_product(
            split_table[...], range(Q_PRODUCT), q_row, marks
        )

    for way in (1, 0):
        mine = slice(1 - way, 2 - way)
        values = own_gather(
            face_q_ref[mine, :], face_lo_ref[mine, :], face_hot[:, (1 - way) * F : (2 - way) * F]
        )
        for b in range(Q_FACE):
            outgoing[way, b * TR : (b + 1) * TR, :] = values[:, b * LO : (b + 1) * LO]
        start(outgoing.at[way], 1, way)

    def own_values(step, carry):
        q_row, lo_row = q_ref[pl.ds(step, 1), :], lo_ref[pl.ds(step, 1), :]
        found[step] = own_gather(q_row, lo_row, hot[step])
        return carry

    lax.fori_loop(0, chunks, own_values, 0, unroll=2)
    write_out(right_ref, right)
    for way in (1, 0):
        arrive(outgoing.at[way], 1, way)
        fill(Q_OWN if way else Q_OWN + Q_FACE, incoming[1, way])

    def face_values(step):
        q_row, lo_row = q_ref[pl.ds(step, 1), :], lo_ref[pl.ds(step, 1), :]
        return gather(table, first_face, face_tiles, q_row, lo_row)

    def elements(step, from_faces):
        q_row = q_ref[pl.ds(step, 1), :]
        values = found[step] + from_faces
        following = face_values(jnp.minimum(step + 1, chunks - 1))
        first, second = pieces(
            jnp.concatenate([values[:, h : h + 256] for h in range(0, CHUNK, 256)], axis=0)
        )
        result = (
            jnp.dot(first, mass[0], preferred_element_type=F32)
            + jnp.dot(second, mass[0], preferred_element_type=F32)
            + jnp.dot(first, mass[1], preferred_element_type=F32)
        )
        result = jnp.concatenate(
            [result[h * TR : (h + 1) * TR] for h in range(CHUNK // 256)], axis=1
        )
        stack = stacked(result * scale_ref[pl.ds(step, 1), :])
        applied[step] = stack
        ext[1, OWN:, :] += scatter(stack, q_row, face_blocks, hot[step])
        return following

    lax.fori_loop(0, chunks, elements, face_values(0), unroll=2)
    start(ext.at[1, down_rows], 2, 0)
    start(ext.at[1, up_rows], 2, 1)
    own_sums(applied, 1)
    arrive(ext.at[1, down_rows], 2, 0)
    arrive(ext.at[1, up_rows], 2, 1)
    image = settle(ext[1, 0:OWN, :], 2)
    write_out(image_ref, image)

    stack = jnp.concatenate(
        [
            jnp.concatenate(
                [stacked(field[q * TR : (q + 1) * TR]) for q in own_blocks], axis=1
            )
            for field in (right, image)
        ],
        axis=0,
    )
    products = add_up(stack, stack)
    lanes = lane_ids((TR, 128))
    upper = products[0:TR] + products[TR : 2 * TR]
    lower = products[2 * TR : 3 * TR] + products[3 * TR :]
    upper = upper + pltpu.roll(upper, 96, 1)
    lower = pltpu.roll(lower + pltpu.roll(lower, 96, 1), 96, 1)
    gram = jnp.where(jnp.logical_and(lanes >= TR, lanes < 2 * TR), lower, upper)

    def sum_over(value, buffer, others, sends, recvs):
        buffer[0] = value

        def part(o, other):
            return pltpu.make_async_remote_copy(
                src_ref=buffer.at[0],
                dst_ref=buffer.at[o],
                send_sem=sends.at[o],
                recv_sem=recvs.at[o],
                device_id=(other,),
                device_id_type=MESH,
            )

        for o, other in enumerate(others, 1):
            part(o, other).start()
        for o, other in enumerate(others, 1):
            part(o, other).wait_recv()
            value = value + buffer[o]
        for o, other in enumerate(others, 1):
            part(o, other).wait_send()
        return value

    gram = sum_over(gram, near, near_ids, near_send, near_recv)
    gram_ref[...] = sum_over(gram, far, far_ids, far_send, far_recv)

    finish(ext.at[0, down_rows], 0, 0)
    finish(ext.at[0, up_rows], 0, 1)
    for way in range(2):
        finish(outgoing.at[way], 1, way)
    finish(ext.at[1, down_rows], 2, 0)
    finish(ext.at[1, up_rows], 2, 1)


def output_kernel(
    gram_ref,
    right_ref,
    image_ref,
    solution_out,
    residual_out,
    basis_out,
    solution_ref,
    residual_ref,
    basis_ref,
    sems,
):
    def dot(a, b):
        return jnp.dot(a, b, precision=HIGH, preferred_element_type=F32)

    rows = lax.broadcasted_iota(jnp.int32, (TR, 128), 0)
    lanes = lane_ids((TR, 128))
    work = gram_ref[...]
    gram = work[:, 0:TR]
    for j in range(0, TR, 2):
        c = 2 * TR + j
        a, b = work[j : j + 1, :], work[j + 1 : j + 2, :]
        inverse = 1.0 / a[:, c : c + 1]
        across = a[:, c + 1 : c + 2] * inverse
        b = b - (b[:, c : c + 1] * inverse) * a
        b = b * (1.0 / b[:, c + 1 : c + 2])
        a = a * inverse - across * b
        rest = work - work[:, c : c + 1] * a - work[:, c + 1 : c + 2] * b
        work = jnp.where(rows == j, a, jnp.where(rows == j + 1, b, rest))
    step_t = work[:, 0:TR]
    step = step_t.T
    image_part = work[:, TR : 2 * TR]
    new_gram = dot(gram, dot(image_part, step_t)) - gram

    def times(small):
        first, second = pieces(small)
        both = jnp.concatenate([first, second], axis=0)

        def apply(value):
            top, rest = pieces(value)
            found = jnp.dot(both, top, preferred_element_type=F32)
            return (
                found[0:TR] + found[TR : 2 * TR] + jnp.dot(first, rest, preferred_element_type=F32)
            )

        return apply

    parts = [slice(at, at + NODE_DEV // 3) for at in range(0, NODE_DEV, NODE_DEV // 3)]
    apply_step = times(step)
    for part in parts:
        right = right_ref[:, part]
        solution_ref[:, part] = apply_step(right)
        residual_ref[:, part] = right - apply_step(image_ref[:, part])
    copies = [
        pltpu.make_async_copy(solution_ref, solution_out, sems.at[0]),
        pltpu.make_async_copy(residual_ref, residual_out, sems.at[1]),
        pltpu.make_async_copy(basis_ref, basis_out, sems.at[2]),
    ]
    copies[0].start()
    copies[1].start()

    work = jnp.concatenate([new_gram, jnp.zeros((TR, 128 - TR), F32)], axis=1)
    work = jnp.where(lanes == rows + TR, 1.0, work)
    scale = jnp.zeros((TR, 128), F32)
    for j in range(0, TR, 2):
        a, b = work[j : j + 1, :], work[j + 1 : j + 2, :]
        pivot, across = a[:, j : j + 1], a[:, j + 1 : j + 2]
        inverse = 1.0 / pivot
        b = b - (b[:, j : j + 1] * inverse) * a
        second_pivot = b[:, j + 1 : j + 2]
        factor = work[:, j : j + 1] * inverse
        second = (work[:, j + 1 : j + 2] - factor * across) * (1.0 / second_pivot)
        rest = work - factor * a - second * b
        work = jnp.where(rows > j + 1, rest, jnp.where(rows == j + 1, b, work))
        scale = jnp.where(rows == j, lax.rsqrt(pivot), scale)
        scale = jnp.where(rows == j + 1, lax.rsqrt(second_pivot), scale)
    apply_lower = times((work * scale)[:, TR : 2 * TR])
    for part in parts:
        basis_ref[:, part] = apply_lower(residual_ref[:, part])
    copies[2].start()
    for copy in copies:
        copy.wait()


def per_device(
    n, connectivity, send_down, send_up, jacobian, pair_blocks, pair_target, pair_source, source_values
):
    elements = connectivity.shape[0]
    pairs = pair_target.shape[0]
    chunks = elements * NP // CHUNK
    vmem = pl.BlockSpec(memory_space=pltpu.VMEM)
    smem = pl.BlockSpec(memory_space=pltpu.SMEM)

    ids = jax.ShapeDtypeStruct((chunks, CHUNK), jnp.int32)
    face_ids = jax.ShapeDtypeStruct((2, F), jnp.int32)
    prepared = pl.pallas_call(
        pair_kernel,
        out_shape=(
            jax.ShapeDtypeStruct((chunks, 2 * TR, CHUNK), BF16),
            ids,
            ids,
            jax.ShapeDtypeStruct((chunks, CHUNK), F32),
            face_ids,
            face_ids,
        ),
        in_specs=[smem, smem, pl.BlockSpec(memory_space=pl.ANY)] + [vmem] * 5,
        out_specs=(vmem,) * 6,
        scratch_shapes=[
            pltpu.VMEM(pair_blocks.shape, BF16),
            pltpu.VMEM((16 * 32, 128), F32),
            pltpu.VMEM((16 * 32, 128), F32),
            pltpu.VMEM((elements, TR, 128), BF16),
            pltpu.VMEM((elements, TR, 128), F32),
            pltpu.VMEM((elements, 128), F32),
            pltpu.SemaphoreType.DMA,
        ],
        compiler_params=pltpu.CompilerParams(vmem_limit_bytes=61 * 2**20),
        name="pair_stage",
    )(
        pair_target,
        pair_source,
        pair_blocks,
        source_values,
        connectivity.T,
        jacobian.reshape(1, elements),
        send_up,
        send_down,
    )

    group = min(GROUP, n)
    layers = n // group
    field = jax.ShapeDtypeStruct((TR, NODE_DEV), F32)
    right, image, gram = pl.pallas_call(
        functools.partial(exchange_kernel, n),
        out_shape=(field, field, jax.ShapeDtypeStruct((TR, 128), F32)),
        in_specs=[vmem] * 6,
        out_specs=(vmem, vmem, vmem),
        scratch_shapes=[
            pltpu.VMEM((Q_ALL * (LO // 128) * TR, 128), F32),
            pltpu.VMEM((Q_PRODUCT * 2 * TR, LO), BF16),
            pltpu.VMEM((2, 4 * NP, 4 * NP), BF16),
            pltpu.VMEM((chunks, LO, CHUNK), BF16),
            pltpu.VMEM((LO, 2 * F), BF16),
            pltpu.VMEM((chunks, TR, CHUNK), F32),
            pltpu.VMEM((chunks, 2 * TR, CHUNK), BF16),
            pltpu.VMEM((2, Q_ALL * TR, LO), F32),
            pltpu.VMEM((2, FACE, LO), F32),
            pltpu.VMEM((3, 2, FACE, LO), F32),
            pltpu.VMEM((group, TR, 128), F32),
            pltpu.VMEM((layers, TR, 128), F32),
            pltpu.SemaphoreType.DMA((3, 2)),
            pltpu.SemaphoreType.DMA((3, 2)),
            pltpu.SemaphoreType.DMA((group,)),
            pltpu.SemaphoreType.DMA((group,)),
            pltpu.SemaphoreType.DMA((layers,)),
            pltpu.SemaphoreType.DMA((layers,)),
        ],
        compiler_params=pltpu.CompilerParams(
            collective_id=0, has_side_effects=True, vmem_limit_bytes=61 * 2**20
        ),
        name="exchange_stage",
    )(*prepared)

    out = jax.ShapeDtypeStruct((TR, NODE_DEV), F32)
    return pl.pallas_call(
        output_kernel,
        out_shape=(out, out, out),
        in_specs=[vmem] * 3,
        out_specs=(pl.BlockSpec(memory_space=pl.ANY),) * 3,
        scratch_shapes=[pltpu.VMEM((TR, NODE_DEV), F32)] * 3 + [pltpu.SemaphoreType.DMA((3,))],
        compiler_params=pltpu.CompilerParams(vmem_limit_bytes=61 * 2**20),
        name="output_stage",
    )(gram, right, image)


def solution(mesh):
    return jax.shard_map(
        functools.partial(per_device, mesh.shape["dom"]),
        mesh=mesh,
        in_specs=(
            P("dom", None),
            P("dom", None),
            P("dom", None),
            P("dom"),
            P("dom", None),
            P("dom"),
            P("dom"),
            P(None, "dom"),
        ),
        out_specs=(P(None, "dom"), P(None, "dom"), P(None, "dom")),
        check_vma=False,
    )
```
